32 devices in a mesh: slab: 8 (over z, y), quad: 4 (over x, core).
Axes of the slice: x: 2, y: 2, z: 4, core: 2. Of those that a mesh axis runs over, the one named last changes fastest.
Arguments:
- grain_cell: int32 [4, 262144], P(None, ('slab', 'quad')), may hold values from 0 to 254, as said below
- grain_count: int32 [32], P(('slab', 'quad')), may hold values from 2048 to 8192, as said below
- grain_weight: float32 [262144], P(('slab', 'quad')), may hold values from 0.05 to 0.95
- grain_volume: float32 [262144], P(('slab', 'quad')), may hold values from 0.02 to 0.4
- grain_velocity: float32 [3, 262144], P(None, ('slab', 'quad')), may hold values from -6 to 6
Outputs:
- pressure: float32 [32, 64, 256], P('slab', 'quad')
- drag: float32 [3, 262144], P(None, ('slab', 'quad'))
The draws below stay inside these ranges and needn't reach their ends.
Inputs may be any that keep to these rules, and one draw needn't show every extreme that they name: grain_cell[0] < 4, grain_cell[1] < 4, grain_cell[2] < 16, grain_cell[3] <= 254; among the slots of one device at most 4096 name the same quarter, and on every device exactly 4096 name one quarter. `grain_count`: some device has all 8192 slots occupied.
All inputs are finite; a program needn't handle non-finite values.
Results may differ from the reference program's by a relative error of at most 0.00002.
Values sent between devices are 32-bit elements; how exact they have to be, the bound alone decides.
No kernel may reach another device: no remote copies, remote signals or barrier semaphores. Data moves between devices by JAX's collectives and lax.ppermute only.
A program may use at most 128 MiB of HBM per device.

```python
import math
import jax
import jax.numpy as jnp
from jax import lax

CH = 4
CA = 16
CB = 256
GR_DEV = 8192
ITERS = 12
GRAINS = 262144
N_SLAB = 8
N_QUAD = 4


def quarter_block(key):
    keys = jax.random.split(key, 3)
    heavy = jax.random.randint(keys[0], (), 0, N_QUAD)
    others = jax.random.randint(keys[1], (GR_DEV,), 1, N_QUAD)
    spread = (heavy + others) % N_QUAD
    index = jnp.arange(GR_DEV, dtype=jnp.int32)
    chosen = jnp.where(index < GR_DEV // 2, heavy, spread)
    return jax.random.permutation(keys[2], chosen)


def draw_grain_cell(key, part):
    keys = jax.random.split(key, 4)
    device_keys = jax.random.split(keys[0], N_SLAB * N_QUAD)
    quarter = jax.vmap(quarter_block)(device_keys).reshape(GRAINS)
    layer = jax.random.randint(keys[1], (GRAINS,), 0, CH)
    across = jax.random.randint(keys[2], (GRAINS,), 0, CA)
    along = jax.random.randint(keys[3], (GRAINS,), 0, CB - 1)
    return jnp.stack([quarter, layer, across, along]).astype(jnp.int32)


def draw_grain_count(key, part):
    keys = jax.random.split(key, 2)
    counts = jax.random.randint(keys[0], (N_SLAB * N_QUAD,), GR_DEV // 4, GR_DEV + 1)
    fullest = jax.random.randint(keys[1], (), 0, N_SLAB * N_QUAD)
    return counts.at[fullest].set(GR_DEV).astype(jnp.int32)


def level_of(stream_key, dims, cuts, least, high):
    level, own = 1.0, jax.random.fold_in(stream_key, 6)
    for dim, parts in cuts:
        draws = jnp.exp(jax.random.uniform(jax.random.fold_in(own, dim), (parts,), jnp.float32, least / len(cuts), high / len(cuts)))
        level = level * jnp.repeat(draws, dims[dim] // parts).reshape([-1 if axis == dim else 1 for axis in range(len(dims))])
    return level


def noise(own_key, dims, width, most, pieces=(), kind=jnp.bfloat16):
    factor_of = level_of(own_key, dims, pieces, -0.22, 0.18) if pieces else 1.0
    result = jax.random.normal(own_key, dims, jnp.float32) * width * factor_of
    return jnp.minimum(jnp.maximum(result, -most), most).astype(kind)


def setup_inputs(seed: int = 0) -> dict:
    streams_of = jax.random.split(jax.random.key(seed), 6)
    grain_cell = draw_grain_cell(jax.random.fold_in(streams_of[5], 71), 0)
    grain_count = draw_grain_count(jax.random.fold_in(streams_of[5], 71), 0)
    grain_weight = jnp.clip(0.05 + 0.9 * jax.random.uniform(streams_of[2], (GRAINS,), jnp.float32) ** level_of(streams_of[2], (GRAINS,), ((0, 32),), -0.2, 0.2), 0.05, 0.95)
    grain_volume = jnp.clip(jnp.exp(math.log(0.4) - 2.9957323 * jax.random.uniform(streams_of[3], (GRAINS,), jnp.float32) ** level_of(streams_of[3], (GRAINS,), ((0, 32),), -0.2, 0.2)), 0.02, 0.4)
    grain_velocity = noise(streams_of[4], (3, GRAINS), 1.0, 6.0, ((1, 32),), jnp.float32)
    return {"grain_cell": grain_cell, "grain_count": grain_count, "grain_weight": grain_weight, "grain_volume": grain_volume, "grain_velocity": grain_velocity}


damping = 0.05
source_gain = 4.0


def neighbours(padded):
    centre = padded[1:-1, 1:-1]
    along = jnp.pad(centre, ((0, 0), (0, 0), (1, 1)))
    total = padded[2:, 1:-1] + padded[:-2, 1:-1] + padded[1:-1, 2:] + padded[1:-1, :-2]
    return total + along[:, :, 2:] + along[:, :, :-2]


def gradient(wide):
    vel_height = -0.5 * (wide[2:, 1:-1, 1:-1] - wide[:-2, 1:-1, 1:-1])
    vel_across = -0.5 * (wide[1:-1, 2:, 1:-1] - wide[1:-1, :-2, 1:-1])
    vel_along = -0.5 * (wide[1:-1, 1:-1, 2:] - wide[1:-1, 1:-1, :-2])
    return vel_height, vel_across, vel_along


def reference(grain_cell, grain_count, grain_weight, grain_volume, grain_velocity):
    heights = CH * N_SLAB
    across = CA * N_QUAD
    cells = heights * across * CB
    slots = jnp.arange(GRAINS, dtype=jnp.int32)
    owner = (slots // GR_DEV).astype(jnp.int32)
    valid = ((slots % GR_DEV) < grain_count[owner]).astype(jnp.float32)
    slab_of = owner // N_QUAD
    height = slab_of * CH + grain_cell[1]
    flat = ((height * across + grain_cell[0] * CA + grain_cell[2]) * CB + grain_cell[3]).astype(jnp.int32)
    mass = valid * grain_volume
    lower = grain_weight
    upper = 1.0 - grain_weight
    amounts = jnp.stack([mass, mass * grain_velocity[0]])
    field = jnp.zeros((2, cells), jnp.float32)
    field = field.at[:, flat].add(amounts * lower).at[:, flat + 1].add(amounts * upper)
    field = field.reshape(2, heights, across, CB)
    solid = field[0]
    voidage = 1.0 / (1.0 + solid)
    source = source_gain * field[1]

    def relax(repeat, pressure):
        padded = jnp.pad(pressure, ((1, 1), (1, 1), (0, 0)))
        return (source + voidage * neighbours(padded)) / (6.0 * voidage + damping)

    pressure = lax.fori_loop(0, ITERS, relax, jnp.zeros((heights, across, CB), jnp.float32))
    vel_height, vel_across, vel_along = gradient(jnp.pad(pressure, 1))
    table = jnp.stack([vel_height, vel_across, vel_along, solid]).reshape(4, cells)
    sampled = lower * table[:, flat] + upper * table[:, flat + 1]
    factor = mass * (1.0 + sampled[3]) ** 2
    drag = factor * (sampled[:3] - grain_velocity)
    return pressure, drag
```

```python
import functools

import jax
import jax.numpy as jnp
from jax import lax
from jax.experimental import pallas as pl
from jax.experimental.pallas import tpu as pltpu
from jax.sharding import PartitionSpec as P

CH = 4
CA = 16
CB = 256
ITERS = 12
LANES = 128
DEPTH = -(-ITERS // CH)

damping = 0.05
source_gain = 4.0

VMEM = pl.BlockSpec(memory_space=pltpu.VMEM)
SMEM = pl.BlockSpec(memory_space=pltpu.SMEM)
LIMIT = pltpu.CompilerParams(vmem_limit_bytes=48 * 1024 * 1024)


def halves(value):
    high = value.astype(jnp.bfloat16)
    low = (value - high.astype(jnp.float32)).astype(jnp.bfloat16)
    return high, low


def row_of(cell_ref, span, across):
    return cell_ref[1:2, span] * across + cell_ref[0:1, span] * CA + cell_ref[2:3, span]


def mass_of(count_ref, volume_ref, first, span):
    volume = volume_ref[0:1, span]
    slot = lax.broadcasted_iota(jnp.int32, volume.shape, 1) + first
    return jnp.where(slot < count_ref[0], volume, 0.0)


def deposit_kernel(quads, width, chunk, place_ref, count_ref, cell_ref, weight_ref, volume_ref, velocity_ref, *outs):
    across = quads * CA
    rows = CH * across
    grains = weight_ref.shape[1]
    own = CB // quads
    halo = (width - own) // 2
    row_iota = lax.broadcasted_iota(jnp.int32, (rows, chunk), 0)
    col_iota = lax.broadcasted_iota(jnp.int32, (CB, chunk), 0)
    total = jnp.zeros((4 * CB, rows), jnp.float32)
    for first in range(0, grains, chunk):
        span = pl.ds(first, chunk)
        mass = mass_of(count_ref, volume_ref, first, span)
        moment = mass * velocity_ref[0:1, span]
        lower = weight_ref[0:1, span]
        upper = 1.0 - lower
        row = row_of(cell_ref, span, across)
        hot = jnp.where(row_iota == row, 1.0, 0.0).astype(jnp.bfloat16)
        col = cell_ref[3:4, span]
        at_lower = col_iota == col
        at_upper = col_iota == col + 1
        parts = []
        for amount in (mass, moment):
            low_pieces = halves(amount * lower)
            high_pieces = halves(amount * upper)
            for low, high in zip(low_pieces, high_pieces):
                spread = jnp.where(
                    at_lower,
                    low.astype(jnp.float32),
                    jnp.where(at_upper, high.astype(jnp.float32), 0.0),
                )
                parts.append(spread.astype(jnp.bfloat16))
        spread = jnp.concatenate(parts, axis=0)
        total = total + lax.dot_general(
            spread, hot, (((1,), (1,)), ((), ())), preferred_element_type=jnp.float32
        )
    lane = lax.broadcasted_iota(jnp.int32, (rows, width), 1)
    for field in range(2):
        base = 2 * field * CB
        whole = (total[base : base + CB] + total[base + CB : base + 2 * CB]).T
        for step, out in enumerate(outs):
            target = lax.rem(place_ref[0] + step, quads)
            first = target * own - halo
            moved = pltpu.roll(whole, lax.rem(CB - first, CB), 1)[:, :width]
            column = lane + first
            moved = jnp.where((column >= 0) & (column < CB), moved, 0.0)
            out[field] = moved.reshape(CH, across, width)


def packed(value, own):
    width = value.shape[-1]
    halo = (width - own) // 2
    pieces = width // own
    tall = value.shape[1] // pieces
    lane = lax.broadcasted_iota(jnp.int32, (value.shape[0], tall, width), 2)
    result = None
    for piece in range(pieces):
        part = value[:, piece * tall : (piece + 1) * tall]
        part = pltpu.roll(part, (piece * own - halo) % width, 2)
        result = part if result is None else jnp.where(lane < piece * own, result, part)
    return result


def coefficient_kernel(quads, place_ref, *refs):
    *parts, coef_ref, solid_ref = refs
    own = CB // quads
    width = coef_ref.shape[-1]
    halo = (width - own) // 2
    solid = parts[0][0]
    moment = parts[0][1]
    for part in parts[1:]:
        solid = solid + part[0]
        moment = moment + part[1]
    column = lax.broadcasted_iota(jnp.int32, solid.shape, 2) + (place_ref[0] * own - halo)
    inside = (column >= 0) & (column < CB)
    voidage = 1.0 / (1.0 + solid)
    scale = 1.0 / (6.0 * voidage + damping)
    coef_ref[0] = jnp.where(inside, source_gain * moment * scale, 0.0)
    coef_ref[1] = jnp.where(inside, voidage * scale, 0.0)
    solid_ref[...] = packed(solid, own)


def relax_kernel(quads, solid_ref, *refs):
    *parts, out_ref, offset_ref, gain_ref, even_ref, odd_ref = refs
    own = CB // quads
    layers = CH * len(parts)
    across, width = out_ref.shape[1] * (offset_ref.shape[-1] // own), offset_ref.shape[-1]
    for index, part in enumerate(parts):
        for layer in range(CH):
            offset_ref[index * CH + layer] = part[0, layer]
            gain_ref[index * CH + layer] = part[1, layer]
            even_ref[index * CH + layer] = part[0, layer]
    row = lax.broadcasted_iota(jnp.int32, (across, width), 0)
    old, new = even_ref, odd_ref
    for sweep in range(1, ITERS):

        def one(layer, carry, old=old, new=new):
            centre = old[layer]
            total = old[layer - 1] + old[layer + 1]
            total = total + pltpu.roll(centre, 1, 1) + pltpu.roll(centre, width - 1, 1)
            total = total + jnp.where(row == 0, 0.0, pltpu.roll(centre, 1, 0))
            total = total + jnp.where(row == across - 1, 0.0, pltpu.roll(centre, across - 1, 0))
            new[layer] = offset_ref[layer] + gain_ref[layer] * total
            return carry

        lax.fori_loop(sweep, layers - sweep, one, 0, unroll=2)
        old, new = new, old
    first = DEPTH * CH - 1
    pressure = jnp.stack([old[first + layer] for layer in range(CH + 2)])
    out_ref[: CH + 2] = packed(pressure, own)
    out_ref[CH + 2 :] = solid_ref[...]


def drag_kernel(
    quads, chunk, place_ref, count_ref, cell_ref, weight_ref, volume_ref, velocity_ref, *refs
):
    *parts, pressure_ref, drag_ref, gathered = refs
    across = quads * CA
    rows = CH * across
    own = CB // quads
    grains = weight_ref.shape[1]
    for step, part in enumerate(parts):
        gathered[lax.rem(place_ref[0] + quads - step, quads)] = part[...]
    tall, width = gathered.shape[2:]
    pieces = width // own
    lane = lax.broadcasted_iota(jnp.int32, (2 * CH + 2, tall, width), 2)
    bands = []
    for piece in range(pieces):
        columns = []
        for left in range(0, quads, pieces):
            block = None
            for near in range(pieces):
                part = gathered[left + near]
                if near != piece:
                    part = pltpu.roll(part, ((near - piece) * own) % width, 2)
                block = part if block is None else jnp.where(lane < near * own, block, part)
            columns.append(block)
        bands.append(jnp.concatenate(columns, axis=2))
    table = jnp.concatenate(bands, axis=1)
    pressure = table[: CH + 2]
    solid = table[CH + 2 :]
    centre = pressure[1 : CH + 1]
    gathered_rows = lax.rem(place_ref[0], quads) * CA
    shape = centre.shape
    row = lax.broadcasted_iota(jnp.int32, shape, 1)
    col = lax.broadcasted_iota(jnp.int32, shape, 2)
    after = jnp.where(row == across - 1, 0.0, pltpu.roll(centre, across - 1, 1))
    before = jnp.where(row == 0, 0.0, pltpu.roll(centre, 1, 1))
    right = jnp.where(col == CB - 1, 0.0, pltpu.roll(centre, CB - 1, 2))
    left = jnp.where(col == 0, 0.0, pltpu.roll(centre, 1, 2))
    fields = (
        -0.5 * (pressure[2:] - pressure[:-2]),
        -0.5 * (after - before),
        -0.5 * (right - left),
        solid,
    )
    fields = [field.reshape(rows, CB).T for field in fields]
    high, low = halves(jnp.concatenate(fields, axis=0))
    whole = pltpu.roll(centre, lax.rem(across - gathered_rows, across), 1)
    pressure_ref[...] = whole[:, :CA]

    row_iota = lax.broadcasted_iota(jnp.int32, (rows, chunk), 0)
    col_iota = lax.broadcasted_iota(jnp.int32, (CB, chunk), 0)
    for first in range(0, grains, chunk):
        span = pl.ds(first, chunk)
        mass = mass_of(count_ref, volume_ref, first, span)
        lower = weight_ref[0:1, span]
        upper = 1.0 - lower
        hot = jnp.where(row_iota == row_of(cell_ref, span, across), 1.0, 0.0).astype(jnp.bfloat16)
        at = cell_ref[3:4, span]
        blend = jnp.where(col_iota == at, lower, jnp.where(col_iota == at + 1, upper, 0.0))
        picked = jnp.dot(high, hot, preferred_element_type=jnp.float32) + jnp.dot(
            low, hot, preferred_element_type=jnp.float32
        )
        sampled = [
            jnp.sum(picked[field * CB : (field + 1) * CB] * blend, axis=0, keepdims=True)
            for field in range(4)
        ]
        factor = mass * (1.0 + sampled[3]) ** 2
        for component in range(3):
            drag_ref[component : component + 1, span] = factor * (
                sampled[component] - velocity_ref[component : component + 1, span]
            )


def body(grain_cell, grain_count, grain_weight, grain_volume, grain_velocity):
    quads = lax.axis_size("quad")
    slabs = lax.axis_size("slab")
    grains = grain_weight.shape[0]
    across = quads * CA
    own = CB // quads
    width = -(-(own + 2 * ITERS) // LANES) * LANES
    pieces = width // own
    place = lax.axis_index("quad").astype(jnp.int32).reshape(1)
    weight = grain_weight.reshape(1, grains)
    volume = grain_volume.reshape(1, grains)
    inputs = (place, grain_count, grain_cell, weight, volume, grain_velocity)
    input_specs = [SMEM, SMEM, VMEM, VMEM, VMEM, VMEM]

    windows = pl.pallas_call(
        functools.partial(deposit_kernel, quads, width, min(grains, 1024)),
        out_shape=[jax.ShapeDtypeStruct((2, CH, across, width), jnp.float32)] * quads,
        in_specs=input_specs,
        out_specs=[VMEM] * quads,
        compiler_params=LIMIT,
        name="deposit",
    )(*inputs)

    def turned(step):
        return [(index, (index + step) % quads) for index in range(quads)]

    parts = [windows[0]] + [
        lax.ppermute(windows[step], "quad", turned(step)) for step in range(1, quads)
    ]
    coef, solid = pl.pallas_call(
        functools.partial(coefficient_kernel, quads),
        out_shape=[
            jax.ShapeDtypeStruct((2, CH, across, width), jnp.float32),
            jax.ShapeDtypeStruct((CH, across // pieces, width), jnp.float32),
        ],
        in_specs=[SMEM] + [VMEM] * quads,
        out_specs=[VMEM] * 2,
        compiler_params=LIMIT,
        name="coefficients",
    )(place, *parts)

    def shifted(step):
        return [
            (index, index + step) for index in range(slabs) if 0 <= index + step < slabs
        ]

    stack = [
        coef if step == 0 else lax.ppermute(coef, "slab", shifted(-step))
        for step in range(-DEPTH, DEPTH + 1)
    ]
    layers = CH * len(stack)
    mine = pl.pallas_call(
        functools.partial(relax_kernel, quads),
        out_shape=jax.ShapeDtypeStruct((2 * CH + 2, across // pieces, width), jnp.float32),
        in_specs=[VMEM] * (1 + len(stack)),
        out_specs=VMEM,
        scratch_shapes=[pltpu.VMEM((layers, across, width), jnp.float32)] * 4,
        compiler_params=LIMIT,
        name="relax",
    )(solid, *stack)

    gathered = [mine] + [lax.ppermute(mine, "quad", turned(step)) for step in range(1, quads)]
    pressure, drag = pl.pallas_call(
        functools.partial(drag_kernel, quads, min(grains, 512)),
        out_shape=[
            jax.ShapeDtypeStruct((CH, CA, CB), jnp.float32),
            jax.ShapeDtypeStruct((3, grains), jnp.float32),
        ],
        in_specs=input_specs + [VMEM] * quads,
        out_specs=[VMEM] * 2,
        scratch_shapes=[pltpu.VMEM((quads,) + mine.shape, jnp.float32)],
        compiler_params=LIMIT,
        name="drag",
    )(*inputs, *gathered)
    return pressure, drag


def solution(mesh):
    placed = (
        P(None, ("slab", "quad")),
        P(("slab", "quad")),
        P(("slab", "quad")),
        P(("slab", "quad")),
        P(None, ("slab", "quad")),
    )
    return jax.shard_map(
        body,
        mesh=mesh,
        in_specs=placed,
        out_specs=(P("slab", "quad", None), P(None, ("slab", "quad"))),
        check_vma=False,
    )
```

```python
import functools

import jax
import jax.numpy as jnp
from jax import lax
from jax.experimental import pallas as pl
from jax.experimental.pallas import tpu as pltpu
from jax.sharding import PartitionSpec as P

CH = 4
CA = 16
CB = 256
ITERS = 12
LANES = 128
SUBLANES = 8
DEPTH = -(-ITERS // CH)

damping = 0.05
source_gain = 4.0

VMEM = pl.BlockSpec(memory_space=pltpu.VMEM)
SMEM = pl.BlockSpec(memory_space=pltpu.SMEM)
HBM = pl.BlockSpec(memory_space=pltpu.HBM)
LIMIT = pltpu.CompilerParams(vmem_limit_bytes=48 * 1024 * 1024)


def reach(distance):
    needed = ITERS - 1 - CH * (max(distance, 1) - 1)
    return 1 << (needed - 1).bit_length()


def lanes_of(shape):
    return lax.broadcasted_iota(jnp.int32, shape, len(shape) - 1)


def turned(value, shift):
    shift %= LANES
    return pltpu.roll(value, shift, value.ndim - 1) if shift else value


def pack_own(window, own):
    pieces = LANES // own
    tall = window.shape[1] // pieces
    lane = lanes_of((window.shape[0], tall, LANES))
    result = window[:, :tall]
    for piece in range(1, pieces):
        part = turned(window[:, piece * tall : (piece + 1) * tall], piece * own)
        result = jnp.where(lane < piece * own, result, part)
    return result


def unpack_own(packed, own):
    pieces = LANES // own
    return jnp.concatenate([turned(packed, -piece * own) for piece in range(pieces)], axis=1)


def strip_plan(across, fields, halo):
    rows = across * 2 * halo // LANES
    return (1, rows) if rows >= SUBLANES else (fields, rows * fields)


def packed_rows(across, fields, halo, own):
    shared, rows = strip_plan(across, fields, halo)
    return fields * CH * across * own // LANES + (fields // shared) * CH * rows


def pack(windows, halo, own):
    across = windows[0].shape[1]
    shared, rows = strip_plan(across, len(windows), halo)
    pieces = [pack_own(window, own) for window in windows]
    lane = lanes_of(windows[0].shape)
    joined = [
        jnp.where(lane >= LANES - halo, window, turned(window, LANES - 2 * halo - own))
        for window in windows
    ]
    lane = lanes_of((CH, rows, LANES))
    for first in range(0, len(windows), shared):
        strip, at = None, 0
        for value in joined[first : first + shared]:
            for row in range(0, across, rows):
                part = turned(value[:, row : row + rows], at + 2 * halo)
                strip = part if strip is None else jnp.where(lane < at, strip, part)
                at += 2 * halo
        pieces.append(strip)
    return jnp.concatenate([piece.reshape(-1, LANES) for piece in pieces], axis=0)


def unpack(value, fields, across, halo, own):
    shared, rows = strip_plan(across, fields, halo)
    tall = across * own // LANES
    count = fields * CH * tall
    owned = value[:count].reshape(fields, CH, tall, LANES)
    strips = value[count:].reshape(fields // shared, CH, rows, LANES)
    lane = lanes_of((CH, rows, LANES))
    windows = []
    for field in range(fields):
        window = unpack_own(owned[field], own)
        strip = strips[field // shared]
        at = (field % shared) * across // rows * 2 * halo
        blocks = []
        for row in range(0, across, rows):
            right = turned(strip, own - at)
            left = turned(strip, -2 * halo - at)
            block = jnp.where(lane < own + halo, right, 0.0)
            block = jnp.where(lane >= LANES - halo, left, block)
            blocks.append(jnp.where(lane < own, window[:, row : row + rows], block))
            at += 2 * halo
        windows.append(jnp.concatenate(blocks, axis=1))
    return windows


def halves(value):
    high = value.astype(jnp.bfloat16)
    low = (value - high.astype(jnp.float32)).astype(jnp.bfloat16)
    return high, low


def short_iota(shape):
    return lax.broadcasted_iota(jnp.int32, shape, 0).astype(jnp.int16)


def row_of(cell_ref, span, across):
    return cell_ref[1:2, span] * across + cell_ref[0:1, span] * CA + cell_ref[2:3, span]


def one_hot(rows, index):
    one, zero = jnp.bfloat16(1), jnp.bfloat16(0)
    return jnp.where(rows == index.astype(jnp.int16), one, zero)


def mass_of(count_ref, volume_ref, first, span):
    volume = volume_ref[0:1, span]
    slot = lax.broadcasted_iota(jnp.int32, volume.shape, 1) + first
    return jnp.where(slot < count_ref[0], volume, 0.0)


def deposit_kernel(quads, chunk, place_ref, count_ref, *refs):
    sources, outs = refs[:4], refs[4 : 4 + quads]
    cell_ref, weight_ref, volume_ref, velocity_ref, sems = refs[4 + quads :]
    copies = [
        pltpu.make_async_copy(source, target, sems.at[index])
        for index, (source, target) in enumerate(
            zip(sources, (cell_ref, weight_ref, volume_ref, velocity_ref))
        )
    ]
    for copy in copies:
        copy.start()
    across = quads * CA
    rows = CH * across
    grains = weight_ref.shape[1]
    own = CB // quads
    row_iota = short_iota((rows, chunk))
    col_iota = short_iota((CB, chunk))
    total = jnp.zeros((4 * CB, rows), jnp.float32)
    for copy in copies:
        copy.wait()
    for first in range(0, grains, chunk):
        span = pl.ds(first, chunk)
        mass = mass_of(count_ref, volume_ref, first, span)
        moment = mass * velocity_ref[0:1, span]
        lower = weight_ref[0:1, span]
        upper = 1.0 - lower
        hot = one_hot(row_iota, row_of(cell_ref, span, across))
        col = cell_ref[3:4, span]
        at_lower = col_iota == col.astype(jnp.int16)
        at_upper = col_iota == (col + 1).astype(jnp.int16)
        parts = []
        for amount in (mass, moment):
            for low, high in zip(halves(amount * lower), halves(amount * upper)):
                parts.append(jnp.where(at_lower, low, jnp.where(at_upper, high, jnp.bfloat16(0))))
        spread = jnp.concatenate(parts, axis=0)
        total = total + lax.dot_general(
            spread, hot, (((1,), (1,)), ((), ())), preferred_element_type=jnp.float32
        )
    lane = lanes_of((CH, across, LANES))
    fields = [
        (total[base : base + CB] + total[base + CB : base + 2 * CB]).T
        for base in range(0, 4 * CB, 2 * CB)
    ]
    for step, out in enumerate(outs):
        target = place_ref[0] ^ step
        windows = []
        for field in fields:
            moved = pltpu.roll(field, lax.rem(CB - target * own, CB), 1)
            moved = moved.reshape(CH, across, CB)
            near, past = moved[:, :, :LANES], moved[:, :, CB - LANES :]
            windows.append(jnp.where(lane < (LANES + own) // 2, near, past))
        out[...] = pack(windows, reach(0), own)


def coefficient_kernel(quads, place_ref, *refs):
    parts, outs, solid_ref = refs[:quads], refs[quads:-1], refs[-1]
    across, own = quads * CA, CB // quads
    total = parts[0][...]
    for part in parts[1:]:
        total = total + part[...]
    solid_ref[...] = total[: solid_ref.shape[0] * solid_ref.shape[1]].reshape(solid_ref.shape)
    solid, moment = unpack(total, 2, across, reach(0), own)
    lane = lanes_of(solid.shape)
    column = jnp.where(lane < (LANES + own) // 2, lane, lane - LANES) + place_ref[0] * own
    inside = (column >= 0) & (column < CB)
    voidage = 1.0 / (1.0 + solid)
    scale = 1.0 / (6.0 * voidage + damping)
    offset = jnp.where(inside, source_gain * moment * scale, 0.0)
    gain = jnp.where(inside, voidage * scale, 0.0)
    for distance, out in enumerate(outs):
        out[...] = pack((offset, gain), reach(distance + 1), own)


def relax_kernel(quads, *refs):
    *parts, out_ref, offset_ref, gain_ref, even_ref, odd_ref = refs
    across, own = quads * CA, CB // quads
    layers = CH * len(parts)
    for index, part in enumerate(parts):
        halo = reach(abs(index - DEPTH))
        span = pl.ds(index * CH, CH)
        offset, gain = unpack(part[...], 2, across, halo, own)
        offset_ref[span] = offset
        even_ref[span] = offset
        gain_ref[span] = gain
    row = lax.broadcasted_iota(jnp.int32, (across, LANES), 0)
    old, new = even_ref, odd_ref
    for sweep in range(1, ITERS):
        for layer in range(sweep, layers - sweep):
            centre = old[layer]
            total = old[layer - 1] + old[layer + 1]
            total = total + turned(centre, 1) + turned(centre, -1)
            total = total + jnp.where(row == 0, 0.0, pltpu.roll(centre, 1, 0))
            total = total + jnp.where(row == across - 1, 0.0, pltpu.roll(centre, across - 1, 0))
            new[layer] = offset_ref[layer] + gain_ref[layer] * total
        old, new = new, old
    first = DEPTH * CH - 1
    out_ref[...] = pack_own(old[first : first + CH + 2], own)


def whole_table(quads, place_ref, parts, gathered):
    own = CB // quads
    pieces = LANES // own
    for step, part in enumerate(parts):
        gathered[place_ref[0] ^ step] = part[...]
    lane = lanes_of(gathered.shape[1:])
    bands = []
    for piece in range(pieces):
        columns = []
        for first in range(0, quads, pieces):
            block = None
            for near in range(pieces):
                part = turned(gathered[first + near], (near - piece) * own)
                block = part if block is None else jnp.where(lane < near * own, block, part)
            columns.append(block)
        bands.append(jnp.concatenate(columns, axis=2))
    return jnp.concatenate(bands, axis=1)


def blend_of(col_iota, cell_ref, weight_ref, span):
    lower = weight_ref[0:1, span]
    at = cell_ref[3:4, span]
    return jnp.where(col_iota == at, lower, jnp.where(col_iota == at + 1, 1.0 - lower, 0.0))


def sample(pieces, hot, blend, fields):
    high, low = pieces
    picked = jnp.dot(high, hot, preferred_element_type=jnp.float32) + jnp.dot(
        low, hot, preferred_element_type=jnp.float32
    )
    return [
        jnp.sum(picked[field * CB : (field + 1) * CB] * blend, axis=0, keepdims=True)
        for field in range(fields)
    ]


def factor_kernel(quads, chunk, place_ref, count_ref, cell_ref, weight_ref, volume_ref, *refs):
    *parts, factor_ref, gathered = refs
    across = quads * CA
    rows = CH * across
    solid = whole_table(quads, place_ref, parts, gathered)
    pieces = halves(solid.reshape(rows, CB).T)
    row_iota = short_iota((rows, chunk))
    col_iota = lax.broadcasted_iota(jnp.int32, (CB, chunk), 0)
    for first in range(0, weight_ref.shape[1], chunk):
        span = pl.ds(first, chunk)
        mass = mass_of(count_ref, volume_ref, first, span)
        hot = one_hot(row_iota, row_of(cell_ref, span, across))
        blend = blend_of(col_iota, cell_ref, weight_ref, span)
        (sampled,) = sample(pieces, hot, blend, 1)
        factor_ref[0:1, span] = mass * (1.0 + sampled) ** 2


def drag_kernel(quads, chunk, place_ref, cell_ref, weight_ref, velocity_ref, factor_ref, *refs):
    *parts, pressure_ref, drag_ref, gathered = refs
    across = quads * CA
    rows = CH * across
    pressure = whole_table(quads, place_ref, parts, gathered)
    centre = pressure[1 : CH + 1]
    shape = centre.shape
    row = lax.broadcasted_iota(jnp.int32, shape, 1)
    col = lax.broadcasted_iota(jnp.int32, shape, 2)
    after = jnp.where(row == across - 1, 0.0, pltpu.roll(centre, across - 1, 1))
    before = jnp.where(row == 0, 0.0, pltpu.roll(centre, 1, 1))
    right = jnp.where(col == CB - 1, 0.0, pltpu.roll(centre, CB - 1, 2))
    left = jnp.where(col == 0, 0.0, pltpu.roll(centre, 1, 2))
    fields = (
        -0.5 * (pressure[2:] - pressure[:-2]),
        -0.5 * (after - before),
        -0.5 * (right - left),
    )
    pieces = halves(jnp.concatenate([field.reshape(rows, CB).T for field in fields], axis=0))
    whole = pltpu.roll(centre, lax.rem(across - place_ref[0] * CA, across), 1)
    pressure_ref[...] = whole[:, :CA]

    row_iota = short_iota((rows, chunk))
    col_iota = lax.broadcasted_iota(jnp.int32, (CB, chunk), 0)
    for first in range(0, weight_ref.shape[1], chunk):
        span = pl.ds(first, chunk)
        hot = one_hot(row_iota, row_of(cell_ref, span, across))
        blend = blend_of(col_iota, cell_ref, weight_ref, span)
        sampled = sample(pieces, hot, blend, 3)
        for component in range(3):
            one = pl.ds(component, 1)
            drag_ref[one, span] = factor_ref[0:1, span] * (
                sampled[component] - velocity_ref[one, span]
            )


def body(grain_cell, grain_count, grain_weight, grain_volume, grain_velocity):
    quads = lax.axis_size("quad")
    slabs = lax.axis_size("slab")
    grains = grain_weight.shape[0]
    across = quads * CA
    own = CB // quads
    tall = across * own // LANES
    place = lax.axis_index("quad").astype(jnp.int32).reshape(1)
    weight = grain_weight.reshape(1, grains)
    volume = grain_volume.reshape(1, grains)

    def cells(*shape):
        return jax.ShapeDtypeStruct(shape, jnp.float32)

    def over_quad(step, value):
        pairs = [(index, index ^ step) for index in range(quads)]
        return lax.ppermute(value, "quad", pairs)

    def over_slab(step, value):
        pairs = [(index, index + step) for index in range(slabs) if 0 <= index + step < slabs]
        return lax.ppermute(value, "slab", pairs)

    windows = pl.pallas_call(
        functools.partial(deposit_kernel, quads, min(grains, 1024)),
        out_shape=[cells(packed_rows(across, 2, reach(0), own), LANES)] * quads,
        in_specs=[SMEM, SMEM] + [HBM] * 4,
        out_specs=[VMEM] * quads,
        scratch_shapes=[
            pltpu.VMEM((4, grains), jnp.int32),
            pltpu.VMEM((1, grains), jnp.float32),
            pltpu.VMEM((1, grains), jnp.float32),
            pltpu.VMEM((3, grains), jnp.float32),
            pltpu.SemaphoreType.DMA((4,)),
        ],
        compiler_params=LIMIT,
        name="deposit",
    )(place, grain_count, grain_cell, weight, volume, grain_velocity)

    parts = [windows[0]] + [over_quad(step, windows[step]) for step in range(1, quads)]
    *coefs, solid = pl.pallas_call(
        functools.partial(coefficient_kernel, quads),
        out_shape=[
            cells(packed_rows(across, 2, reach(distance), own), LANES)
            for distance in range(1, DEPTH + 1)
        ]
        + [cells(CH, tall, LANES)],
        in_specs=[SMEM] + [VMEM] * quads,
        out_specs=[VMEM] * (DEPTH + 1),
        compiler_params=LIMIT,
        name="coefficients",
    )(place, *parts)

    stack = [
        coefs[0] if step == 0 else over_slab(-step, coefs[abs(step) - 1])
        for step in range(-DEPTH, DEPTH + 1)
    ]

    solids = [solid] + [over_quad(step, solid) for step in range(1, quads)]
    factor = pl.pallas_call(
        functools.partial(factor_kernel, quads, min(grains, 1024)),
        out_shape=cells(1, grains),
        in_specs=[SMEM, SMEM] + [VMEM] * (3 + quads),
        out_specs=VMEM,
        scratch_shapes=[pltpu.VMEM((quads,) + solid.shape, jnp.float32)],
        compiler_params=LIMIT,
        cost_estimate=pl.CostEstimate(
            flops=4 * CB * CH * across * grains, bytes_accessed=2**20, transcendentals=0
        ),
        name="factor",
    )(place, grain_count, grain_cell, weight, volume, *solids)

    layers = CH * len(stack)
    mine = pl.pallas_call(
        functools.partial(relax_kernel, quads),
        out_shape=cells(CH + 2, tall, LANES),
        in_specs=[VMEM] * len(stack),
        out_specs=VMEM,
        scratch_shapes=[pltpu.VMEM((layers, across, LANES), jnp.float32)] * 4,
        compiler_params=LIMIT,
        name="relax",
    )(*stack)

    gathered = [mine] + [over_quad(step, mine) for step in range(1, quads)]
    pressure, drag = pl.pallas_call(
        functools.partial(drag_kernel, quads, min(grains, 512)),
        out_shape=[cells(CH, CA, CB), cells(3, grains)],
        in_specs=[SMEM] + [VMEM] * (4 + quads),
        out_specs=[VMEM] * 2,
        scratch_shapes=[pltpu.VMEM((quads,) + mine.shape, jnp.float32)],
        compiler_params=LIMIT,
        name="drag",
    )(place, grain_cell, weight, grain_velocity, factor, *gathered)
    return pressure, drag


def solution(mesh):
    placed = (
        P(None, ("slab", "quad")),
        P(("slab", "quad")),
        P(("slab", "quad")),
        P(("slab", "quad")),
        P(None, ("slab", "quad")),
    )
    return jax.shard_map(
        body,
        mesh=mesh,
        in_specs=placed,
        out_specs=(P("slab", "quad", None), P(None, ("slab", "quad"))),
        check_vma=False,
    )
```

```python
import functools

import jax
import jax.numpy as jnp
from jax import lax
from jax.experimental import pallas as pl
from jax.experimental.pallas import tpu as pltpu
from jax.sharding import PartitionSpec as P

CH = 4
CA = 16
CB = 256
ITERS = 12
LANES = 128
SUBLANES = 8
DEPTH = 2
FIRST = CH * DEPTH + 1

damping = 0.05
source_gain = 4.0

VMEM = pl.BlockSpec(memory_space=pltpu.VMEM)
SMEM = pl.BlockSpec(memory_space=pltpu.SMEM)
HBM = pl.BlockSpec(memory_space=pltpu.HBM)
LIMIT = pltpu.CompilerParams(vmem_limit_bytes=48 * 1024 * 1024)


def reach(distance):
    needed = ITERS - 1 - CH * (max(distance, 1) - 1)
    return 1 << (needed - 1).bit_length()


def lanes_of(shape):
    return lax.broadcasted_iota(jnp.int32, shape, len(shape) - 1)


def turned(value, shift):
    shift %= LANES
    return pltpu.roll(value, shift, value.ndim - 1) if shift else value


def pack_own(window, own):
    pieces = LANES // own
    tall = window.shape[1] // pieces
    lane = lanes_of((window.shape[0], tall, LANES))
    result = window[:, :tall]
    for piece in range(1, pieces):
        part = turned(window[:, piece * tall : (piece + 1) * tall], piece * own)
        result = jnp.where(lane < piece * own, result, part)
    return result


def unpack_own(packed, own):
    pieces = LANES // own
    return jnp.concatenate([turned(packed, -piece * own) for piece in range(pieces)], axis=1)


def strip_plan(across, fields, halo):
    rows = across * 2 * halo // LANES
    return (1, rows) if rows >= SUBLANES else (fields, rows * fields)


def packed_rows(across, fields, halo, own):
    shared, rows = strip_plan(across, fields, halo)
    return fields * CH * across * own // LANES + (fields // shared) * CH * rows


def pack(windows, halo, own):
    across = windows[0].shape[1]
    shared, rows = strip_plan(across, len(windows), halo)
    pieces = [pack_own(window, own) for window in windows]
    lane = lanes_of(windows[0].shape)
    joined = [
        jnp.where(lane >= LANES - halo, window, turned(window, LANES - 2 * halo - own))
        for window in windows
    ]
    lane = lanes_of((CH, rows, LANES))
    for first in range(0, len(windows), shared):
        strip, at = None, 0
        for value in joined[first : first + shared]:
            for row in range(0, across, rows):
                part = turned(value[:, row : row + rows], at + 2 * halo)
                strip = part if strip is None else jnp.where(lane < at, strip, part)
                at += 2 * halo
        pieces.append(strip)
    return jnp.concatenate([piece.reshape(-1, LANES) for piece in pieces], axis=0)


def unpack(value, fields, across, halo, own):
    shared, rows = strip_plan(across, fields, halo)
    tall = across * own // LANES
    count = fields * CH * tall
    owned = value[:count].reshape(fields, CH, tall, LANES)
    strips = value[count:].reshape(fields // shared, CH, rows, LANES)
    lane = lanes_of((CH, rows, LANES))
    windows = []
    for field in range(fields):
        window = unpack_own(owned[field], own)
        strip = strips[field // shared]
        at = (field % shared) * across // rows * 2 * halo
        blocks = []
        for row in range(0, across, rows):
            right = turned(strip, own - at)
            left = turned(strip, -2 * halo - at)
            block = jnp.where(lane < own + halo, right, 0.0)
            block = jnp.where(lane >= LANES - halo, left, block)
            blocks.append(jnp.where(lane < own, window[:, row : row + rows], block))
            at += 2 * halo
        windows.append(jnp.concatenate(blocks, axis=1))
    return windows


def halves(value):
    high = value.astype(jnp.bfloat16)
    low = (value - high.astype(jnp.float32)).astype(jnp.bfloat16)
    return high, low


def short_iota(shape):
    return lax.broadcasted_iota(jnp.int32, shape, 0).astype(jnp.int16)


def row_of(cell_ref, span, across):
    return cell_ref[1:2, span] * across + cell_ref[0:1, span] * CA + cell_ref[2:3, span]


def one_hot(rows, index):
    one, zero = jnp.bfloat16(1), jnp.bfloat16(0)
    return jnp.where(rows == index.astype(jnp.int16), one, zero)


def mass_of(count_ref, volume_ref, first, span):
    volume = volume_ref[0:1, span]
    slot = lax.broadcasted_iota(jnp.int32, volume.shape, 1) + first
    return jnp.where(slot < count_ref[0], volume, 0.0)


def deposit_kernel(quads, chunk, place_ref, count_ref, *refs):
    sources, outs = refs[:4], refs[4:6]
    cell_ref, weight_ref, volume_ref, velocity_ref, sems = refs[6:]
    copies = [
        pltpu.make_async_copy(source, target, sems.at[index])
        for index, (source, target) in enumerate(
            zip(sources, (cell_ref, weight_ref, volume_ref, velocity_ref))
        )
    ]
    for copy in copies:
        copy.start()
    across = quads * CA
    rows = CH * across
    grains = weight_ref.shape[1]
    own = CB // quads
    row_iota = short_iota((rows, chunk))
    col_iota = short_iota((CB, chunk))
    total = jnp.zeros((4 * CB, rows), jnp.float32)
    for copy in copies:
        copy.wait()
    for first in range(0, grains, chunk):
        span = pl.ds(first, chunk)
        mass = mass_of(count_ref, volume_ref, first, span)
        moment = mass * velocity_ref[0:1, span]
        lower = weight_ref[0:1, span]
        upper = 1.0 - lower
        hot = one_hot(row_iota, row_of(cell_ref, span, across))
        col = cell_ref[3:4, span]
        at_lower = col_iota == col.astype(jnp.int16)
        at_upper = col_iota == (col + 1).astype(jnp.int16)
        parts = []
        for amount in (mass, moment):
            for low, high in zip(halves(amount * lower), halves(amount * upper)):
                parts.append(jnp.where(at_lower, low, jnp.where(at_upper, high, jnp.bfloat16(0))))
        spread = jnp.concatenate(parts, axis=0)
        total = total + lax.dot_general(
            spread, hot, (((1,), (1,)), ((), ())), preferred_element_type=jnp.float32
        )
    lane = lanes_of((CH, across, LANES))
    fields = [
        (total[base : base + CB] + total[base + CB : base + 2 * CB]).T
        for base in range(0, 4 * CB, 2 * CB)
    ]
    for step in range(quads):
        target = place_ref[0] ^ step
        windows = []
        for field in fields:
            moved = pltpu.roll(field, lax.rem(CB - target * own, CB), 1)
            moved = moved.reshape(CH, across, CB)
            near, past = moved[:, :, :LANES], moved[:, :, CB - LANES :]
            windows.append(jnp.where(lane < (LANES + own) // 2, near, past))
        outs[step % 2][step // 2] = pack(windows, reach(0), own)


def coefficient_kernel(quads, place_ref, kept_ref, got_ref, *refs):
    outs, solid_ref = refs[:-1], refs[-1]
    across, own = quads * CA, CB // quads
    total = kept_ref[0] + got_ref[0]
    solid_ref[...] = total[: solid_ref.shape[0] * solid_ref.shape[1]].reshape(solid_ref.shape)
    solid, moment = unpack(total, 2, across, reach(0), own)
    lane = lanes_of(solid.shape)
    column = jnp.where(lane < (LANES + own) // 2, lane, lane - LANES) + place_ref[0] * own
    inside = (column >= 0) & (column < CB)
    voidage = 1.0 / (1.0 + solid)
    scale = 1.0 / (6.0 * voidage + damping)
    offset = jnp.where(inside, source_gain * moment * scale, 0.0)
    gain = jnp.where(inside, voidage * scale, 0.0)
    for distance, out in enumerate(outs):
        out[...] = pack((offset, gain), reach(distance + 1), own)


def sweep_over(sweeps, layers, across, old, new, offset_ref, gain_ref):
    row = lax.broadcasted_iota(jnp.int32, (across, LANES), 0)
    for sweep in range(1, sweeps + 1):
        for layer in range(sweep, layers - sweep):
            centre = old[layer]
            total = old[layer - 1] + old[layer + 1]
            total = total + turned(centre, 1) + turned(centre, -1)
            total = total + jnp.where(row == 0, 0.0, pltpu.roll(centre, 1, 0))
            total = total + jnp.where(row == across - 1, 0.0, pltpu.roll(centre, across - 1, 0))
            new[layer] = offset_ref[layer] + gain_ref[layer] * total
        old, new = new, old
    return old


def relax_kernel(quads, *refs):
    *parts, out_ref, offset_ref, gain_ref, even_ref, odd_ref = refs
    across, own = quads * CA, CB // quads
    layers = CH * len(parts)
    for index, part in enumerate(parts):
        span = pl.ds(index * CH, CH)
        offset, gain = unpack(part[...], 2, across, reach(abs(index - DEPTH)), own)
        offset_ref[span] = offset
        even_ref[span] = offset
        gain_ref[span] = gain
    last = sweep_over(FIRST - 1, layers, across, even_ref, odd_ref, offset_ref, gain_ref)
    out_ref[...] = pack([last[DEPTH * CH : (DEPTH + 1) * CH]], SUBLANES, own)


def finish_kernel(quads, *refs):
    *parts, out_ref, offset_ref, gain_ref, even_ref, odd_ref = refs
    across, own = quads * CA, CB // quads
    half = len(parts) // 2
    for index in range(half):
        span = pl.ds(index * CH, CH)
        offset_ref[span], gain_ref[span] = unpack(parts[index][...], 2, across, reach(1), own)
        (even_ref[span],) = unpack(parts[half + index][...], 1, across, SUBLANES, own)
    last = sweep_over(ITERS - FIRST, half * CH, across, even_ref, odd_ref, offset_ref, gain_ref)
    out_ref[...] = pack_own(last[CH - 1 : 2 * CH + 1], own)


def whole_table(quads, place_ref, parts, gathered):
    own = CB // quads
    pieces = LANES // own
    for step, part in enumerate(parts):
        gathered[place_ref[0] ^ step] = part[...]
    lane = lanes_of(gathered.shape[1:])
    bands = []
    for piece in range(pieces):
        columns = []
        for first in range(0, quads, pieces):
            block = None
            for near in range(pieces):
                part = turned(gathered[first + near], (near - piece) * own)
                block = part if block is None else jnp.where(lane < near * own, block, part)
            columns.append(block)
        bands.append(jnp.concatenate(columns, axis=2))
    return jnp.concatenate(bands, axis=1)


def blend_of(col_iota, cell_ref, weight_ref, span):
    lower = weight_ref[0:1, span]
    at = cell_ref[3:4, span]
    return jnp.where(col_iota == at, lower, jnp.where(col_iota == at + 1, 1.0 - lower, 0.0))


def sample(pieces, hot, blend, fields):
    high, low = pieces
    picked = jnp.dot(high, hot, preferred_element_type=jnp.float32) + jnp.dot(
        low, hot, preferred_element_type=jnp.float32
    )
    return [
        jnp.sum(picked[field * CB : (field + 1) * CB] * blend, axis=0, keepdims=True)
        for field in range(fields)
    ]


def factor_kernel(quads, chunk, place_ref, count_ref, cell_ref, weight_ref, volume_ref, *refs):
    *parts, factor_ref, gathered = refs
    across = quads * CA
    rows = CH * across
    solid = whole_table(quads, place_ref, parts, gathered)
    pieces = halves(solid.reshape(rows, CB).T)
    row_iota = short_iota((rows, chunk))
    col_iota = lax.broadcasted_iota(jnp.int32, (CB, chunk), 0)
    for first in range(0, weight_ref.shape[1], chunk):
        span = pl.ds(first, chunk)
        mass = mass_of(count_ref, volume_ref, first, span)
        hot = one_hot(row_iota, row_of(cell_ref, span, across))
        blend = blend_of(col_iota, cell_ref, weight_ref, span)
        (sampled,) = sample(pieces, hot, blend, 1)
        factor_ref[0:1, span] = mass * (1.0 + sampled) ** 2


def drag_kernel(quads, chunk, place_ref, cell_ref, weight_ref, velocity_ref, factor_ref, *refs):
    *parts, pressure_ref, drag_ref, gathered = refs
    across = quads * CA
    rows = CH * across
    pressure = whole_table(quads, place_ref, parts, gathered)
    centre = pressure[1 : CH + 1]
    shape = centre.shape
    row = lax.broadcasted_iota(jnp.int32, shape, 1)
    col = lax.broadcasted_iota(jnp.int32, shape, 2)
    after = jnp.where(row == across - 1, 0.0, pltpu.roll(centre, across - 1, 1))
    before = jnp.where(row == 0, 0.0, pltpu.roll(centre, 1, 1))
    right = jnp.where(col == CB - 1, 0.0, pltpu.roll(centre, CB - 1, 2))
    left = jnp.where(col == 0, 0.0, pltpu.roll(centre, 1, 2))
    fields = (
        -0.5 * (pressure[2:] - pressure[:-2]),
        -0.5 * (after - before),
        -0.5 * (right - left),
    )
    pieces = halves(jnp.concatenate([field.reshape(rows, CB).T for field in fields], axis=0))
    whole = pltpu.roll(centre, lax.rem(across - place_ref[0] * CA, across), 1)
    pressure_ref[...] = whole[:, :CA]

    row_iota = short_iota((rows, chunk))
    col_iota = lax.broadcasted_iota(jnp.int32, (CB, chunk), 0)
    for first in range(0, weight_ref.shape[1], chunk):
        span = pl.ds(first, chunk)
        hot = one_hot(row_iota, row_of(cell_ref, span, across))
        blend = blend_of(col_iota, cell_ref, weight_ref, span)
        sampled = sample(pieces, hot, blend, 3)
        for component in range(3):
            one = pl.ds(component, 1)
            drag_ref[one, span] = factor_ref[0:1, span] * (
                sampled[component] - velocity_ref[one, span]
            )


def body(grain_cell, grain_count, grain_weight, grain_volume, grain_velocity):
    quads = lax.axis_size("quad")
    slabs = lax.axis_size("slab")
    grains = grain_weight.shape[0]
    across = quads * CA
    own = CB // quads
    tall = across * own // LANES
    place = lax.axis_index("quad").astype(jnp.int32).reshape(1)
    weight = grain_weight.reshape(1, grains)
    volume = grain_volume.reshape(1, grains)

    def cells(*shape):
        return jax.ShapeDtypeStruct(shape, jnp.float32)

    def over_quad(step, value):
        pairs = [(index, index ^ step) for index in range(quads)]
        return lax.ppermute(value, "quad", pairs)

    def over_slab(step, value):
        pairs = [(index, index + step) for index in range(slabs) if 0 <= index + step < slabs]
        return lax.ppermute(value, "slab", pairs)

    def pinned(value):
        return pltpu.with_memory_space_constraint(value, pltpu.HBM)

    kept, sent = pl.pallas_call(
        functools.partial(deposit_kernel, quads, min(grains, 2048)),
        out_shape=[cells(quads // 2, packed_rows(across, 2, reach(0), own), LANES)] * 2,
        in_specs=[SMEM, SMEM] + [HBM] * 4,
        out_specs=[VMEM] * 2,
        scratch_shapes=[
            pltpu.VMEM((4, grains), jnp.int32),
            pltpu.VMEM((1, grains), jnp.float32),
            pltpu.VMEM((1, grains), jnp.float32),
            pltpu.VMEM((3, grains), jnp.float32),
            pltpu.SemaphoreType.DMA((4,)),
        ],
        compiler_params=LIMIT,
        name="deposit",
    )(
        place,
        grain_count,
        pinned(grain_cell),
        pinned(weight),
        pinned(volume),
        pinned(grain_velocity),
    )

    bit = 1
    got = over_quad(bit, sent)
    while kept.shape[0] > 1:
        bit *= 2
        total = kept + got
        kept, sent = total[0::2], total[1::2]
        got = over_quad(bit, sent)
    *coefs, solid = pl.pallas_call(
        functools.partial(coefficient_kernel, quads),
        out_shape=[
            cells(packed_rows(across, 2, reach(distance), own), LANES)
            for distance in range(1, DEPTH + 1)
        ]
        + [cells(CH, tall, LANES)],
        in_specs=[SMEM] + [VMEM] * 2,
        out_specs=[VMEM] * (DEPTH + 1),
        compiler_params=LIMIT,
        name="coefficients",
    )(place, kept, got)

    stack = [
        coefs[0] if step == 0 else over_slab(-step, coefs[abs(step) - 1])
        for step in range(-DEPTH, DEPTH + 1)
    ]

    solids = [solid] + [over_quad(step, solid) for step in range(1, quads)]
    stack, solids = lax.optimization_barrier((stack, solids))
    factor = pl.pallas_call(
        functools.partial(factor_kernel, quads, min(grains, 512)),
        out_shape=cells(1, grains),
        in_specs=[SMEM, SMEM] + [VMEM] * (3 + quads),
        out_specs=VMEM,
        scratch_shapes=[pltpu.VMEM((quads,) + solid.shape, jnp.float32)],
        compiler_params=LIMIT,
        cost_estimate=pl.CostEstimate(
            flops=4 * CB * CH * across * grains, bytes_accessed=2**20, transcendentals=0
        ),
        name="factor",
    )(place, grain_count, grain_cell, weight, volume, *solids)

    layers = CH * len(stack)
    centre = pl.pallas_call(
        functools.partial(relax_kernel, quads),
        out_shape=cells(packed_rows(across, 1, SUBLANES, own), LANES),
        in_specs=[VMEM] * len(stack),
        out_specs=VMEM,
        scratch_shapes=[pltpu.VMEM((layers, across, LANES), jnp.float32)] * 4,
        compiler_params=LIMIT,
        name="relax",
    )(*stack)
    near = stack[DEPTH - 1 : DEPTH + 2]
    pressures = [over_slab(1, centre), centre, over_slab(-1, centre)]
    mine = pl.pallas_call(
        functools.partial(finish_kernel, quads),
        out_shape=cells(CH + 2, tall, LANES),
        in_specs=[VMEM] * 6,
        out_specs=VMEM,
        scratch_shapes=[pltpu.VMEM((3 * CH, across, LANES), jnp.float32)] * 4,
        compiler_params=LIMIT,
        name="finish",
    )(*near, *pressures)

    gathered = [mine] + [over_quad(step, mine) for step in range(1, quads)]
    pressure, drag = pl.pallas_call(
        functools.partial(drag_kernel, quads, min(grains, 256)),
        out_shape=[cells(CH, CA, CB), cells(3, grains)],
        in_specs=[SMEM] + [VMEM] * (4 + quads),
        out_specs=[VMEM] * 2,
        scratch_shapes=[pltpu.VMEM((quads,) + mine.shape, jnp.float32)],
        compiler_params=LIMIT,
        name="drag",
    )(place, grain_cell, weight, grain_velocity, factor, *gathered)
    return pressure, drag


def solution(mesh):
    placed = (
        P(None, ("slab", "quad")),
        P(("slab", "quad")),
        P(("slab", "quad")),
        P(("slab", "quad")),
        P(None, ("slab", "quad")),
    )
    return jax.shard_map(
        body,
        mesh=mesh,
        in_specs=placed,
        out_specs=(P("slab", "quad", None), P(None, ("slab", "quad"))),
        check_vma=False,
    )
```

```python
import functools

import jax
import jax.numpy as jnp
from jax import lax
from jax.experimental import pallas as pl
from jax.experimental.pallas import tpu as pltpu
from jax.sharding import PartitionSpec as P

CH = 4
CA = 16
CB = 256
ITERS = 12
LANES = 128
SUBLANES = 8
DEPTH = 2
FIRST = CH * DEPTH + 1

damping = 0.05
source_gain = 4.0

VMEM = pl.BlockSpec(memory_space=pltpu.VMEM)
SMEM = pl.BlockSpec(memory_space=pltpu.SMEM)
HBM = pl.BlockSpec(memory_space=pltpu.HBM)
LIMIT = pltpu.CompilerParams(vmem_limit_bytes=48 * 1024 * 1024)


def reach(distance):
    needed = ITERS - 1 - CH * (max(distance, 1) - 1)
    return 1 << (needed - 1).bit_length()


def lanes_of(shape):
    return lax.broadcasted_iota(jnp.int32, shape, len(shape) - 1)


def turned(value, shift):
    shift %= LANES
    return pltpu.roll(value, shift, value.ndim - 1) if shift else value


def pack_own(window, own):
    pieces = LANES // own
    tall = window.shape[1] // pieces
    lane = lanes_of((window.shape[0], tall, LANES))
    result = window[:, :tall]
    for piece in range(1, pieces):
        part = turned(window[:, piece * tall : (piece + 1) * tall], piece * own)
        result = jnp.where(lane < piece * own, result, part)
    return result


def unpack_own(packed, own):
    pieces = LANES // own
    return jnp.concatenate([turned(packed, -piece * own) for piece in range(pieces)], axis=1)


def strip_plan(across, fields, halo):
    rows = across * 2 * halo // LANES
    return (1, rows) if rows >= SUBLANES else (fields, rows * fields)


def packed_rows(across, fields, halo, own):
    shared, rows = strip_plan(across, fields, halo)
    return fields * CH * across * own // LANES + (fields // shared) * CH * rows


def pack(windows, halo, own):
    across = windows[0].shape[1]
    shared, rows = strip_plan(across, len(windows), halo)
    pieces = [pack_own(window, own) for window in windows]
    lane = lanes_of(windows[0].shape)
    joined = [
        jnp.where(lane >= LANES - halo, window, turned(window, LANES - 2 * halo - own))
        for window in windows
    ]
    lane = lanes_of((CH, rows, LANES))
    for first in range(0, len(windows), shared):
        strip, at = None, 0
        for value in joined[first : first + shared]:
            for row in range(0, across, rows):
                part = turned(value[:, row : row + rows], at + 2 * halo)
                strip = part if strip is None else jnp.where(lane < at, strip, part)
                at += 2 * halo
        pieces.append(strip)
    return jnp.concatenate([piece.reshape(-1, LANES) for piece in pieces], axis=0)


def unpack(value, fields, across, halo, own):
    shared, rows = strip_plan(across, fields, halo)
    tall = across * own // LANES
    count = fields * CH * tall
    owned = value[:count].reshape(fields, CH, tall, LANES)
    strips = value[count:].reshape(fields // shared, CH, rows, LANES)
    lane = lanes_of((CH, rows, LANES))
    windows = []
    for field in range(fields):
        window = unpack_own(owned[field], own)
        strip = strips[field // shared]
        at = (field % shared) * across // rows * 2 * halo
        blocks = []
        for row in range(0, across, rows):
            right = turned(strip, own - at)
            left = turned(strip, -2 * halo - at)
            block = jnp.where(lane < own + halo, right, 0.0)
            block = jnp.where(lane >= LANES - halo, left, block)
            blocks.append(jnp.where(lane < own, window[:, row : row + rows], block))
            at += 2 * halo
        windows.append(jnp.concatenate(blocks, axis=1))
    return windows


def halves(value):
    high = value.astype(jnp.bfloat16)
    low = (value - high.astype(jnp.float32)).astype(jnp.bfloat16)
    return high, low


def short_iota(shape):
    return lax.broadcasted_iota(jnp.int32, shape, 0).astype(jnp.int16)


def row_of(cell_ref, span, across):
    return cell_ref[1:2, span] * across + cell_ref[0:1, span] * CA + cell_ref[2:3, span]


def one_hot(rows, index):
    one, zero = jnp.bfloat16(1), jnp.bfloat16(0)
    return jnp.where(rows == index.astype(jnp.int16), one, zero)


def mass_of(count_ref, volume_ref, first, span):
    volume = volume_ref[0:1, span]
    slot = lax.broadcasted_iota(jnp.int32, volume.shape, 1) + first
    return jnp.where(slot < count_ref[0], volume, 0.0)


def deposit_kernel(quads, chunk, place_ref, count_ref, *refs):
    sources, outs = refs[:4], refs[4:6]
    cell_ref, weight_ref, volume_ref, velocity_ref, sems = refs[6:]
    copies = [
        pltpu.make_async_copy(source, target, sems.at[index])
        for index, (source, target) in enumerate(
            zip(sources, (cell_ref, weight_ref, volume_ref, velocity_ref))
        )
    ]
    for copy in copies:
        copy.start()
    across = quads * CA
    rows = CH * across
    grains = weight_ref.shape[1]
    own = CB // quads
    row_iota = short_iota((rows, chunk))
    col_iota = short_iota((CB, chunk))
    total = jnp.zeros((4 * CB, rows), jnp.float32)
    for copy in copies:
        copy.wait()
    for first in range(0, grains, chunk):
        span = pl.ds(first, chunk)
        mass = mass_of(count_ref, volume_ref, first, span)
        moment = mass * velocity_ref[0:1, span]
        lower = weight_ref[0:1, span]
        upper = 1.0 - lower
        hot = one_hot(row_iota, row_of(cell_ref, span, across))
        col = cell_ref[3:4, span]
        at_lower = col_iota == col.astype(jnp.int16)
        at_upper = col_iota == (col + 1).astype(jnp.int16)
        parts = []
        for amount in (mass, moment):
            for low, high in zip(halves(amount * lower), halves(amount * upper)):
                parts.append(jnp.where(at_lower, low, jnp.where(at_upper, high, jnp.bfloat16(0))))
        spread = jnp.concatenate(parts, axis=0)
        total = total + lax.dot_general(
            spread, hot, (((1,), (1,)), ((), ())), preferred_element_type=jnp.float32
        )
    lane = lanes_of((CH, across, LANES))
    fields = [
        (total[base : base + CB] + total[base + CB : base + 2 * CB]).T
        for base in range(0, 4 * CB, 2 * CB)
    ]
    for step in range(quads):
        target = place_ref[0] ^ step
        windows = []
        for field in fields:
            moved = pltpu.roll(field, lax.rem(CB - target * own, CB), 1)
            moved = moved.reshape(CH, across, CB)
            near, past = moved[:, :, :LANES], moved[:, :, CB - LANES :]
            windows.append(jnp.where(lane < (LANES + own) // 2, near, past))
        outs[step % 2][step // 2] = pack(windows, reach(0), own)


def coefficient_kernel(quads, place_ref, kept_ref, got_ref, *refs):
    outs, solid_ref = refs[:-1], refs[-1]
    across, own = quads * CA, CB // quads
    total = kept_ref[0] + got_ref[0]
    solid_ref[...] = total[: solid_ref.shape[0] * solid_ref.shape[1]].reshape(solid_ref.shape)
    solid, moment = unpack(total, 2, across, reach(0), own)
    lane = lanes_of(solid.shape)
    column = jnp.where(lane < (LANES + own) // 2, lane, lane - LANES) + place_ref[0] * own
    inside = (column >= 0) & (column < CB)
    voidage = 1.0 / (1.0 + solid)
    scale = 1.0 / (6.0 * voidage + damping)
    offset = jnp.where(inside, source_gain * moment * scale, 0.0)
    gain = jnp.where(inside, voidage * scale, 0.0)
    for distance, out in enumerate(outs):
        out[...] = pack((offset, gain), reach(distance + 1), own)


def sweep_over(sweeps, layers, across, old, new, offset_ref, gain_ref):
    row = lax.broadcasted_iota(jnp.int32, (across, LANES), 0)
    for sweep in range(1, sweeps + 1):
        for layer in range(sweep, layers - sweep):
            centre = old[layer]
            total = old[layer - 1] + old[layer + 1]
            total = total + turned(centre, 1) + turned(centre, -1)
            total = total + jnp.where(row == 0, 0.0, pltpu.roll(centre, 1, 0))
            total = total + jnp.where(row == across - 1, 0.0, pltpu.roll(centre, across - 1, 0))
            new[layer] = offset_ref[layer] + gain_ref[layer] * total
        old, new = new, old
    return old


def slot_of(slab, distance, matching):
    upward = lax.rem(lax.div(slab, distance), 2) ^ matching
    return distance * (1 - 2 * upward)


def swap_plan(depth):
    return [(distance, matching) for distance in range(1, depth + 1) for matching in range(2)]


def relax_kernel(quads, slab_ref, own_ref, *refs):
    *parts, out_ref, offset_ref, gain_ref, even_ref, odd_ref = refs
    across, own = quads * CA, CB // quads
    layers = CH * (1 + len(parts))
    plan = [(DEPTH, own_ref, 1)] + [
        (DEPTH + slot_of(slab_ref[0], distance, matching), part, distance)
        for part, (distance, matching) in zip(parts, swap_plan(DEPTH))
    ]
    for slot, part, distance in plan:
        span = pl.ds(slot * CH, CH)
        offset, gain = unpack(part[...], 2, across, reach(distance), own)
        offset_ref[span] = offset
        even_ref[span] = offset
        gain_ref[span] = gain
    sweeps = min(FIRST, ITERS) - 1
    last = sweep_over(sweeps, layers, across, even_ref, odd_ref, offset_ref, gain_ref)
    if FIRST < ITERS:
        out_ref[...] = pack([last[DEPTH * CH : (DEPTH + 1) * CH]], SUBLANES, own)
    else:
        out_ref[...] = pack_own(last[DEPTH * CH - 1 : (DEPTH + 1) * CH + 1], own)


def finish_kernel(quads, slab_ref, *refs):
    *parts, out_ref, offset_ref, gain_ref, even_ref, odd_ref = refs
    across, own = quads * CA, CB // quads
    slots = [1] + [1 + slot_of(slab_ref[0], *swap) for swap in swap_plan(1)]
    for slot, coef, pressure in zip(slots, parts[:3], parts[3:]):
        span = pl.ds(slot * CH, CH)
        offset_ref[span], gain_ref[span] = unpack(coef[...], 2, across, reach(1), own)
        (even_ref[span],) = unpack(pressure[...], 1, across, SUBLANES, own)
    last = sweep_over(ITERS - FIRST, 3 * CH, across, even_ref, odd_ref, offset_ref, gain_ref)
    out_ref[...] = pack_own(last[CH - 1 : 2 * CH + 1], own)


def halving(quads):
    return [1 << bit for bit in reversed(range(quads.bit_length() - 1))]


def whole_table(quads, place_ref, parts, gathered):
    own = CB // quads
    pieces = LANES // own
    offsets = [0]
    for bit in halving(quads):
        offsets += [offset ^ bit for offset in offsets]
    for half, part in enumerate(parts):
        for index in range(quads // 2):
            gathered[place_ref[0] ^ offsets[half * (quads // 2) + index]] = part[index]
    lane = lanes_of(gathered.shape[1:])
    bands = []
    for piece in range(pieces):
        columns = []
        for first in range(0, quads, pieces):
            block = None
            for near in range(pieces):
                part = turned(gathered[first + near], (near - piece) * own)
                block = part if block is None else jnp.where(lane < near * own, block, part)
            columns.append(block)
        bands.append(jnp.concatenate(columns, axis=2))
    return jnp.concatenate(bands, axis=1)


def blend_of(col_iota, cell_ref, weight_ref, span):
    lower = weight_ref[0:1, span]
    at = cell_ref[3:4, span]
    return jnp.where(col_iota == at, lower, jnp.where(col_iota == at + 1, 1.0 - lower, 0.0))


def sample(pieces, hot, blend, fields):
    picked = jnp.dot(pieces, hot, preferred_element_type=jnp.float32)
    picked = picked[: fields * CB] + picked[fields * CB :]
    return [
        jnp.sum(picked[field * CB : (field + 1) * CB] * blend, axis=0, keepdims=True)
        for field in range(fields)
    ]


def factor_kernel(quads, chunk, place_ref, count_ref, cell_ref, weight_ref, volume_ref, *refs):
    *parts, factor_ref, gathered = refs
    across = quads * CA
    rows = CH * across
    solid = whole_table(quads, place_ref, parts, gathered)
    pieces = jnp.concatenate(halves(solid.reshape(rows, CB).T), axis=0)
    row_iota = short_iota((rows, chunk))
    col_iota = lax.broadcasted_iota(jnp.int32, (CB, chunk), 0)
    for first in range(0, weight_ref.shape[1], chunk):
        span = pl.ds(first, chunk)
        mass = mass_of(count_ref, volume_ref, first, span)
        hot = one_hot(row_iota, row_of(cell_ref, span, across))
        blend = blend_of(col_iota, cell_ref, weight_ref, span)
        (sampled,) = sample(pieces, hot, blend, 1)
        factor_ref[0:1, span] = mass * (1.0 + sampled) ** 2


def drag_kernel(quads, chunk, place_ref, cell_ref, weight_ref, velocity_ref, factor_ref, *refs):
    *parts, pressure_ref, drag_ref, gathered = refs
    across = quads * CA
    rows = CH * across
    pressure = whole_table(quads, place_ref, parts, gathered)
    centre = pressure[1 : CH + 1]
    shape = centre.shape
    row = lax.broadcasted_iota(jnp.int32, shape, 1)
    col = lax.broadcasted_iota(jnp.int32, shape, 2)
    after = jnp.where(row == across - 1, 0.0, pltpu.roll(centre, across - 1, 1))
    before = jnp.where(row == 0, 0.0, pltpu.roll(centre, 1, 1))
    right = jnp.where(col == CB - 1, 0.0, pltpu.roll(centre, CB - 1, 2))
    left = jnp.where(col == 0, 0.0, pltpu.roll(centre, 1, 2))
    fields = (
        -0.5 * (pressure[2:] - pressure[:-2]),
        -0.5 * (after - before),
        -0.5 * (right - left),
    )
    pieces = halves(jnp.concatenate([field.reshape(rows, CB).T for field in fields], axis=0))
    pieces = jnp.concatenate(pieces, axis=0)
    whole = pltpu.roll(centre, lax.rem(across - place_ref[0] * CA, across), 1)
    pressure_ref[...] = whole[:, :CA]

    row_iota = short_iota((rows, chunk))
    col_iota = lax.broadcasted_iota(jnp.int32, (CB, chunk), 0)
    for first in range(0, weight_ref.shape[1], chunk):
        span = pl.ds(first, chunk)
        hot = one_hot(row_iota, row_of(cell_ref, span, across))
        blend = blend_of(col_iota, cell_ref, weight_ref, span)
        sampled = sample(pieces, hot, blend, 3)
        for component in range(3):
            one = pl.ds(component, 1)
            drag_ref[one, span] = factor_ref[0:1, span] * (
                sampled[component] - velocity_ref[one, span]
            )


def body(grain_cell, grain_count, grain_weight, grain_volume, grain_velocity):
    quads = lax.axis_size("quad")
    slabs = lax.axis_size("slab")
    grains = grain_weight.shape[0]
    across = quads * CA
    own = CB // quads
    tall = across * own // LANES
    place = lax.axis_index("quad").astype(jnp.int32).reshape(1)
    level = lax.axis_index("slab").astype(jnp.int32).reshape(1)
    weight = grain_weight.reshape(1, grains)
    volume = grain_volume.reshape(1, grains)

    def cells(*shape):
        return jax.ShapeDtypeStruct(shape, jnp.float32)

    def over_quad(step, value):
        pairs = [(index, index ^ step) for index in range(quads)]
        return lax.ppermute(value, "quad", pairs)

    def swapped(distance, matching, value):
        lower = [
            index
            for index in range(slabs - distance)
            if (index // distance) % 2 == matching
        ]
        pairs = [(index, index + distance) for index in lower]
        return lax.ppermute(value, "slab", pairs + [(high, low) for low, high in pairs])

    *early, last = halving(quads)

    def nearly_all(value):
        held = value[None]
        for bit in early:
            held = jnp.concatenate([held, over_quad(bit, held)], axis=0)
        return held

    def pinned(value):
        return pltpu.with_memory_space_constraint(value, pltpu.HBM)

    kept, sent = pl.pallas_call(
        functools.partial(deposit_kernel, quads, min(grains, 2048)),
        out_shape=[cells(quads // 2, packed_rows(across, 2, reach(0), own), LANES)] * 2,
        in_specs=[SMEM, SMEM] + [HBM] * 4,
        out_specs=[VMEM] * 2,
        scratch_shapes=[
            pltpu.VMEM((4, grains), jnp.int32),
            pltpu.VMEM((1, grains), jnp.float32),
            pltpu.VMEM((1, grains), jnp.float32),
            pltpu.VMEM((3, grains), jnp.float32),
            pltpu.SemaphoreType.DMA((4,)),
        ],
        compiler_params=LIMIT,
        name="deposit",
    )(
        place,
        grain_count,
        pinned(grain_cell),
        pinned(weight),
        pinned(volume),
        pinned(grain_velocity),
    )

    bit = 1
    got = over_quad(bit, sent)
    while kept.shape[0] > 1:
        bit *= 2
        total = kept + got
        kept, sent = total[0::2], total[1::2]
        got = over_quad(bit, sent)
    *coefs, solid = pl.pallas_call(
        functools.partial(coefficient_kernel, quads),
        out_shape=[
            cells(packed_rows(across, 2, reach(distance), own), LANES)
            for distance in range(1, DEPTH + 1)
        ]
        + [cells(CH, tall, LANES)],
        in_specs=[SMEM] + [VMEM] * 2,
        out_specs=[VMEM] * (DEPTH + 1),
        compiler_params=LIMIT,
        name="coefficients",
    )(place, kept, got)

    stack = [coefs[0]] + [
        swapped(distance, matching, coefs[distance - 1])
        for distance, matching in swap_plan(DEPTH)
    ]
    solids = nearly_all(solid)
    stack, solids = lax.optimization_barrier((stack, solids))
    solids = [solids, over_quad(last, solids)]
    layers = CH * len(stack)
    two_rounds = FIRST < ITERS
    centre = pl.pallas_call(
        functools.partial(relax_kernel, quads),
        out_shape=cells(packed_rows(across, 1, SUBLANES, own), LANES)
        if two_rounds
        else cells(CH + 2, tall, LANES),
        in_specs=[SMEM] + [VMEM] * len(stack),
        out_specs=VMEM,
        scratch_shapes=[pltpu.VMEM((layers, across, LANES), jnp.float32)] * 4,
        compiler_params=LIMIT,
        name="relax",
    )(level, *stack)
    mine = centre
    if two_rounds:
        pressures = [centre] + [swapped(*swap, centre) for swap in swap_plan(1)]
        pressures, solids = lax.optimization_barrier((pressures, solids))
        mine = pl.pallas_call(
            functools.partial(finish_kernel, quads),
            out_shape=cells(CH + 2, tall, LANES),
            in_specs=[SMEM] + [VMEM] * 6,
            out_specs=VMEM,
            scratch_shapes=[pltpu.VMEM((3 * CH, across, LANES), jnp.float32)] * 4,
            compiler_params=LIMIT,
            name="finish",
        )(level, *stack[:3], *pressures)

    factor = pl.pallas_call(
        functools.partial(factor_kernel, quads, min(grains, 512)),
        out_shape=cells(1, grains),
        in_specs=[SMEM, SMEM] + [VMEM] * 5,
        out_specs=VMEM,
        scratch_shapes=[pltpu.VMEM((quads,) + solid.shape, jnp.float32)],
        compiler_params=LIMIT,
        cost_estimate=pl.CostEstimate(
            flops=4 * CB * CH * across * grains, bytes_accessed=2**20, transcendentals=0
        ),
        name="factor",
    )(place, grain_count, grain_cell, weight, volume, *solids)

    held, factor = lax.optimization_barrier((nearly_all(mine), factor))
    gathered = [held, over_quad(last, held)]
    pressure, drag = pl.pallas_call(
        functools.partial(drag_kernel, quads, min(grains, 256)),
        out_shape=[cells(CH, CA, CB), cells(3, grains)],
        in_specs=[SMEM] + [VMEM] * 6,
        out_specs=[VMEM] * 2,
        scratch_shapes=[pltpu.VMEM((quads,) + mine.shape, jnp.float32)],
        compiler_params=LIMIT,
        name="drag",
    )(place, grain_cell, weight, grain_velocity, factor, *gathered)
    return pressure, drag


def solution(mesh):
    placed = (
        P(None, ("slab", "quad")),
        P(("slab", "quad")),
        P(("slab", "quad")),
        P(("slab", "quad")),
        P(None, ("slab", "quad")),
    )
    return jax.shard_map(
        body,
        mesh=mesh,
        in_specs=placed,
        out_specs=(P("slab", "quad", None), P(None, ("slab", "quad"))),
        check_vma=False,
    )
```

```python
import functools

import jax
import jax.numpy as jnp
from jax import lax
from jax.experimental import pallas as pl
from jax.experimental.pallas import tpu as pltpu
from jax.sharding import PartitionSpec as P

CH = 4
CA = 16
CB = 256
ITERS = 12
LANES = 128
SUBLANES = 8
DEPTH = 3
FIRST = CH * DEPTH + 1

damping = 0.05
source_gain = 4.0

VMEM = pl.BlockSpec(memory_space=pltpu.VMEM)
SMEM = pl.BlockSpec(memory_space=pltpu.SMEM)
HBM = pl.BlockSpec(memory_space=pltpu.HBM)
LIMIT = pltpu.CompilerParams(vmem_limit_bytes=48 * 1024 * 1024)


def reach(distance):
    needed = ITERS - 1 - CH * (max(distance, 1) - 1)
    return 1 << (needed - 1).bit_length()


def lanes_of(shape):
    return lax.broadcasted_iota(jnp.int32, shape, len(shape) - 1)


def turned(value, shift):
    shift %= LANES
    return pltpu.roll(value, shift, value.ndim - 1) if shift else value


def pack_own(window, own):
    pieces = LANES // own
    tall = window.shape[1] // pieces
    lane = lanes_of((window.shape[0], tall, LANES))
    result = window[:, :tall]
    for piece in range(1, pieces):
        part = turned(window[:, piece * tall : (piece + 1) * tall], piece * own)
        result = jnp.where(lane < piece * own, result, part)
    return result


def unpack_own(packed, own):
    pieces = LANES // own
    return jnp.concatenate([turned(packed, -piece * own) for piece in range(pieces)], axis=1)


def strip_plan(across, fields, halo):
    rows = across * 2 * halo // LANES
    return (1, rows) if rows >= SUBLANES else (fields, rows * fields)


def packed_rows(across, fields, halo, own):
    shared, rows = strip_plan(across, fields, halo)
    return fields * CH * across * own // LANES + (fields // shared) * CH * rows


def pack(windows, halo, own):
    across = windows[0].shape[1]
    shared, rows = strip_plan(across, len(windows), halo)
    pieces = [pack_own(window, own) for window in windows]
    lane = lanes_of(windows[0].shape)
    joined = [
        jnp.where(lane >= LANES - halo, window, turned(window, LANES - 2 * halo - own))
        for window in windows
    ]
    lane = lanes_of((CH, rows, LANES))
    for first in range(0, len(windows), shared):
        strip, at = None, 0
        for value in joined[first : first + shared]:
            for row in range(0, across, rows):
                part = turned(value[:, row : row + rows], at + 2 * halo)
                strip = part if strip is None else jnp.where(lane < at, strip, part)
                at += 2 * halo
        pieces.append(strip)
    return jnp.concatenate([piece.reshape(-1, LANES) for piece in pieces], axis=0)


def unpack(value, fields, across, halo, own):
    shared, rows = strip_plan(across, fields, halo)
    tall = across * own // LANES
    count = fields * CH * tall
    owned = value[:count].reshape(fields, CH, tall, LANES)
    strips = value[count:].reshape(fields // shared, CH, rows, LANES)
    lane = lanes_of((CH, rows, LANES))
    windows = []
    for field in range(fields):
        window = unpack_own(owned[field], own)
        strip = strips[field // shared]
        at = (field % shared) * across // rows * 2 * halo
        blocks = []
        for row in range(0, across, rows):
            right = turned(strip, own - at)
            left = turned(strip, -2 * halo - at)
            block = jnp.where(lane < own + halo, right, 0.0)
            block = jnp.where(lane >= LANES - halo, left, block)
            blocks.append(jnp.where(lane < own, window[:, row : row + rows], block))
            at += 2 * halo
        windows.append(jnp.concatenate(blocks, axis=1))
    return windows


def halves(value):
    high = value.astype(jnp.bfloat16)
    low = (value - high.astype(jnp.float32)).astype(jnp.bfloat16)
    return high, low


def short_iota(shape):
    return lax.broadcasted_iota(jnp.int32, shape, 0).astype(jnp.int16)


def row_of(cell_ref, span, across):
    return cell_ref[1:2, span] * across + cell_ref[0:1, span] * CA + cell_ref[2:3, span]


def one_hot(rows, index):
    one, zero = jnp.bfloat16(1), jnp.bfloat16(0)
    return jnp.where(rows == index.astype(jnp.int16), one, zero)


def mass_of(count_ref, volume_ref, first, span):
    volume = volume_ref[0:1, span]
    slot = lax.broadcasted_iota(jnp.int32, volume.shape, 1) + first
    return jnp.where(slot < count_ref[0], volume, 0.0)


def deposit_kernel(quads, chunk, place_ref, count_ref, *refs):
    sources, outs = refs[:4], refs[4:6]
    cell_ref, weight_ref, volume_ref, velocity_ref, sems = refs[6:]
    copies = [
        pltpu.make_async_copy(source, target, sems.at[index])
        for index, (source, target) in enumerate(
            zip(sources, (cell_ref, weight_ref, volume_ref, velocity_ref))
        )
    ]
    for copy in copies:
        copy.start()
    across = quads * CA
    rows = CH * across
    grains = weight_ref.shape[1]
    own = CB // quads
    row_iota = short_iota((rows, chunk))
    col_iota = short_iota((CB, chunk))
    total = jnp.zeros((4 * CB, rows), jnp.float32)
    for copy in copies:
        copy.wait()
    for first in range(0, grains, chunk):
        span = pl.ds(first, chunk)
        mass = mass_of(count_ref, volume_ref, first, span)
        moment = mass * velocity_ref[0:1, span]
        lower = weight_ref[0:1, span]
        upper = 1.0 - lower
        hot = one_hot(row_iota, row_of(cell_ref, span, across))
        col = cell_ref[3:4, span]
        at_lower = col_iota == col.astype(jnp.int16)
        at_upper = col_iota == (col + 1).astype(jnp.int16)
        parts = []
        for amount in (mass, moment):
            for low, high in zip(halves(amount * lower), halves(amount * upper)):
                parts.append(jnp.where(at_lower, low, jnp.where(at_upper, high, jnp.bfloat16(0))))
        spread = jnp.concatenate(parts, axis=0)
        total = total + lax.dot_general(
            spread, hot, (((1,), (1,)), ((), ())), preferred_element_type=jnp.float32
        )
    lane = lanes_of((CH, across, LANES))
    fields = [
        (total[base : base + CB] + total[base + CB : base + 2 * CB]).T
        for base in range(0, 4 * CB, 2 * CB)
    ]
    for step in range(quads):
        target = place_ref[0] ^ step
        windows = []
        for field in fields:
            moved = pltpu.roll(field, lax.rem(CB - target * own, CB), 1)
            moved = moved.reshape(CH, across, CB)
            near, past = moved[:, :, :LANES], moved[:, :, CB - LANES :]
            windows.append(jnp.where(lane < (LANES + own) // 2, near, past))
        outs[step % 2][step // 2] = pack(windows, reach(0), own)


def coefficient_kernel(quads, place_ref, kept_ref, got_ref, *refs):
    outs, solid_ref = refs[:-1], refs[-1]
    across, own = quads * CA, CB // quads
    total = kept_ref[0] + got_ref[0]
    solid_ref[...] = total[: solid_ref.shape[0] * solid_ref.shape[1]].reshape(solid_ref.shape)
    solid, moment = unpack(total, 2, across, reach(0), own)
    lane = lanes_of(solid.shape)
    column = jnp.where(lane < (LANES + own) // 2, lane, lane - LANES) + place_ref[0] * own
    inside = (column >= 0) & (column < CB)
    voidage = 1.0 / (1.0 + solid)
    scale = 1.0 / (6.0 * voidage + damping)
    offset = jnp.where(inside, source_gain * moment * scale, 0.0)
    gain = jnp.where(inside, voidage * scale, 0.0)
    for distance, out in enumerate(outs):
        out[...] = pack((offset, gain), reach(distance + 1), own)


def sweep_over(sweeps, layers, across, old, new, offset_ref, gain_ref):
    row = lax.broadcasted_iota(jnp.int32, (across, LANES), 0)
    for sweep in range(1, sweeps + 1):
        for layer in range(sweep, layers - sweep):
            centre = old[layer]
            total = old[layer - 1] + old[layer + 1]
            total = total + turned(centre, 1) + turned(centre, -1)
            total = total + jnp.where(row == 0, 0.0, pltpu.roll(centre, 1, 0))
            total = total + jnp.where(row == across - 1, 0.0, pltpu.roll(centre, across - 1, 0))
            new[layer] = offset_ref[layer] + gain_ref[layer] * total
        old, new = new, old
    return old


def slot_of(slab, distance, matching):
    upward = lax.rem(lax.div(slab, distance), 2) ^ matching
    return distance * (1 - 2 * upward)


def swap_plan(depth):
    return [(distance, matching) for distance in range(1, depth + 1) for matching in range(2)]


def relax_kernel(quads, slab_ref, own_ref, *refs):
    *parts, out_ref, offset_ref, gain_ref, even_ref, odd_ref = refs
    across, own = quads * CA, CB // quads
    layers = CH * (1 + len(parts))
    plan = [(DEPTH, own_ref, 1)] + [
        (DEPTH + slot_of(slab_ref[0], distance, matching), part, distance)
        for part, (distance, matching) in zip(parts, swap_plan(DEPTH))
    ]
    for slot, part, distance in plan:
        span = pl.ds(slot * CH, CH)
        offset, gain = unpack(part[...], 2, across, reach(distance), own)
        offset_ref[span] = offset
        even_ref[span] = offset
        gain_ref[span] = gain
    sweeps = min(FIRST, ITERS) - 1
    last = sweep_over(sweeps, layers, across, even_ref, odd_ref, offset_ref, gain_ref)
    if FIRST < ITERS:
        out_ref[...] = pack([last[DEPTH * CH : (DEPTH + 1) * CH]], SUBLANES, own)
    else:
        out_ref[...] = pack_own(last[DEPTH * CH - 1 : (DEPTH + 1) * CH + 1], own)


def finish_kernel(quads, slab_ref, *refs):
    *parts, out_ref, offset_ref, gain_ref, even_ref, odd_ref = refs
    across, own = quads * CA, CB // quads
    slots = [1] + [1 + slot_of(slab_ref[0], *swap) for swap in swap_plan(1)]
    for slot, coef, pressure in zip(slots, parts[:3], parts[3:]):
        span = pl.ds(slot * CH, CH)
        offset_ref[span], gain_ref[span] = unpack(coef[...], 2, across, reach(1), own)
        (even_ref[span],) = unpack(pressure[...], 1, across, SUBLANES, own)
    last = sweep_over(ITERS - FIRST, 3 * CH, across, even_ref, odd_ref, offset_ref, gain_ref)
    out_ref[...] = pack_own(last[CH - 1 : 2 * CH + 1], own)


def halving(quads):
    return [1 << bit for bit in reversed(range(quads.bit_length() - 1))]


def whole_table(quads, place_ref, parts, gathered):
    own = CB // quads
    pieces = LANES // own
    offsets = [0]
    for bit in halving(quads):
        offsets += [offset ^ bit for offset in offsets]
    for half, part in enumerate(parts):
        for index in range(quads // 2):
            gathered[place_ref[0] ^ offsets[half * (quads // 2) + index]] = part[index]
    lane = lanes_of(gathered.shape[1:])
    bands = []
    for piece in range(pieces):
        columns = []
        for first in range(0, quads, pieces):
            block = None
            for near in range(pieces):
                part = turned(gathered[first + near], (near - piece) * own)
                block = part if block is None else jnp.where(lane < near * own, block, part)
            columns.append(block)
        bands.append(jnp.concatenate(columns, axis=2))
    return jnp.concatenate(bands, axis=1)


def blend_of(col_iota, cell_ref, weight_ref, span):
    lower = weight_ref[0:1, span]
    at = cell_ref[3:4, span]
    return jnp.where(col_iota == at, lower, jnp.where(col_iota == at + 1, 1.0 - lower, 0.0))


def sample(pieces, hot, blend, fields):
    twice = jnp.concatenate([hot, hot], axis=0)
    picked = jnp.dot(pieces, twice, preferred_element_type=jnp.float32)
    return [
        jnp.sum(picked[field * CB : (field + 1) * CB] * blend, axis=0, keepdims=True)
        for field in range(fields)
    ]


def factor_kernel(quads, chunk, place_ref, count_ref, cell_ref, weight_ref, volume_ref, *refs):
    *parts, factor_ref, gathered = refs
    across = quads * CA
    rows = CH * across
    solid = whole_table(quads, place_ref, parts, gathered)
    pieces = jnp.concatenate(halves(solid.reshape(rows, CB).T), axis=1)
    row_iota = short_iota((rows, chunk))
    col_iota = lax.broadcasted_iota(jnp.int32, (CB, chunk), 0)
    for first in range(0, weight_ref.shape[1], chunk):
        span = pl.ds(first, chunk)
        mass = mass_of(count_ref, volume_ref, first, span)
        hot = one_hot(row_iota, row_of(cell_ref, span, across))
        blend = blend_of(col_iota, cell_ref, weight_ref, span)
        (sampled,) = sample(pieces, hot, blend, 1)
        factor_ref[0:1, span] = mass * (1.0 + sampled) ** 2


def drag_kernel(quads, chunk, place_ref, cell_ref, weight_ref, velocity_ref, factor_ref, *refs):
    *parts, pressure_ref, drag_ref, gathered = refs
    across = quads * CA
    rows = CH * across
    pressure = whole_table(quads, place_ref, parts, gathered)
    centre = pressure[1 : CH + 1]
    shape = centre.shape
    row = lax.broadcasted_iota(jnp.int32, shape, 1)
    col = lax.broadcasted_iota(jnp.int32, shape, 2)
    after = jnp.where(row == across - 1, 0.0, pltpu.roll(centre, across - 1, 1))
    before = jnp.where(row == 0, 0.0, pltpu.roll(centre, 1, 1))
    right = jnp.where(col == CB - 1, 0.0, pltpu.roll(centre, CB - 1, 2))
    left = jnp.where(col == 0, 0.0, pltpu.roll(centre, 1, 2))
    fields = (
        -0.5 * (pressure[2:] - pressure[:-2]),
        -0.5 * (after - before),
        -0.5 * (right - left),
    )
    pieces = halves(jnp.concatenate([field.reshape(rows, CB).T for field in fields], axis=0))
    pieces = jnp.concatenate(pieces, axis=1)
    whole = pltpu.roll(centre, lax.rem(across - place_ref[0] * CA, across), 1)
    pressure_ref[...] = whole[:, :CA]

    row_iota = short_iota((rows, chunk))
    col_iota = lax.broadcasted_iota(jnp.int32, (CB, chunk), 0)
    for first in range(0, weight_ref.shape[1], chunk):
        span = pl.ds(first, chunk)
        hot = one_hot(row_iota, row_of(cell_ref, span, across))
        blend = blend_of(col_iota, cell_ref, weight_ref, span)
        sampled = sample(pieces, hot, blend, 3)
        for component in range(3):
            one = pl.ds(component, 1)
            drag_ref[one, span] = factor_ref[0:1, span] * (
                sampled[component] - velocity_ref[one, span]
            )


def body(grain_cell, grain_count, grain_weight, grain_volume, grain_velocity):
    quads = lax.axis_size("quad")
    slabs = lax.axis_size("slab")
    grains = grain_weight.shape[0]
    across = quads * CA
    own = CB // quads
    tall = across * own // LANES
    place = lax.axis_index("quad").astype(jnp.int32).reshape(1)
    level = lax.axis_index("slab").astype(jnp.int32).reshape(1)
    weight = grain_weight.reshape(1, grains)
    volume = grain_volume.reshape(1, grains)

    def cells(*shape):
        return jax.ShapeDtypeStruct(shape, jnp.float32)

    def over_quad(step, value):
        pairs = [(index, index ^ step) for index in range(quads)]
        return lax.ppermute(value, "quad", pairs)

    def swapped(distance, matching, value):
        lower = [
            index
            for index in range(slabs - distance)
            if (index // distance) % 2 == matching
        ]
        pairs = [(index, index + distance) for index in lower]
        return lax.ppermute(value, "slab", pairs + [(high, low) for low, high in pairs])

    *early, last = halving(quads)

    def nearly_all(value):
        held = value[None]
        for bit in early:
            held = jnp.concatenate([held, over_quad(bit, held)], axis=0)
        return held

    def pinned(value):
        return pltpu.with_memory_space_constraint(value, pltpu.HBM)

    kept, sent = pl.pallas_call(
        functools.partial(deposit_kernel, quads, min(grains, 2048)),
        out_shape=[cells(quads // 2, packed_rows(across, 2, reach(0), own), LANES)] * 2,
        in_specs=[SMEM, SMEM] + [HBM] * 4,
        out_specs=[VMEM] * 2,
        scratch_shapes=[
            pltpu.VMEM((4, grains), jnp.int32),
            pltpu.VMEM((1, grains), jnp.float32),
            pltpu.VMEM((1, grains), jnp.float32),
            pltpu.VMEM((3, grains), jnp.float32),
            pltpu.SemaphoreType.DMA((4,)),
        ],
        compiler_params=LIMIT,
        name="deposit",
    )(
        place,
        grain_count,
        pinned(grain_cell),
        pinned(weight),
        pinned(volume),
        pinned(grain_velocity),
    )

    bit = 1
    got = over_quad(bit, sent)
    while kept.shape[0] > 1:
        bit *= 2
        total = kept + got
        kept, sent = total[0::2], total[1::2]
        got = over_quad(bit, sent)
    *coefs, solid = pl.pallas_call(
        functools.partial(coefficient_kernel, quads),
        out_shape=[
            cells(packed_rows(across, 2, reach(distance), own), LANES)
            for distance in range(1, DEPTH + 1)
        ]
        + [cells(CH, tall, LANES)],
        in_specs=[SMEM] + [VMEM] * 2,
        out_specs=[VMEM] * (DEPTH + 1),
        compiler_params=LIMIT,
        name="coefficients",
    )(place, kept, got)

    stack = [coefs[0]] + [
        swapped(distance, matching, coefs[distance - 1])
        for distance, matching in swap_plan(DEPTH)
    ]
    solids = nearly_all(solid)
    solids = [solids, over_quad(last, solids)]
    stack, solids = lax.optimization_barrier((stack, solids))
    layers = CH * len(stack)
    two_rounds = FIRST < ITERS
    centre = pl.pallas_call(
        functools.partial(relax_kernel, quads),
        out_shape=cells(packed_rows(across, 1, SUBLANES, own), LANES)
        if two_rounds
        else cells(CH + 2, tall, LANES),
        in_specs=[SMEM] + [VMEM] * len(stack),
        out_specs=VMEM,
        scratch_shapes=[pltpu.VMEM((layers, across, LANES), jnp.float32)] * 4,
        compiler_params=LIMIT,
        name="relax",
    )(level, *stack)
    mine = centre
    if two_rounds:
        pressures = [centre] + [swapped(*swap, centre) for swap in swap_plan(1)]
        mine = pl.pallas_call(
            functools.partial(finish_kernel, quads),
            out_shape=cells(CH + 2, tall, LANES),
            in_specs=[SMEM] + [VMEM] * 6,
            out_specs=VMEM,
            scratch_shapes=[pltpu.VMEM((3 * CH, across, LANES), jnp.float32)] * 4,
            compiler_params=LIMIT,
            name="finish",
        )(level, *stack[:3], *pressures)

    factor = pl.pallas_call(
        functools.partial(factor_kernel, quads, min(grains, 512)),
        out_shape=cells(1, grains),
        in_specs=[SMEM, SMEM] + [VMEM] * 5,
        out_specs=VMEM,
        scratch_shapes=[pltpu.VMEM((quads,) + solid.shape, jnp.float32)],
        compiler_params=LIMIT,
        cost_estimate=pl.CostEstimate(
            flops=4 * CB * CH * across * grains, bytes_accessed=2**20, transcendentals=0
        ),
        name="factor",
    )(place, grain_count, grain_cell, weight, volume, *solids)

    held, factor = lax.optimization_barrier((nearly_all(mine), factor))
    gathered = [held, over_quad(last, held)]
    pressure, drag = pl.pallas_call(
        functools.partial(drag_kernel, quads, min(grains, 256)),
        out_shape=[cells(CH, CA, CB), cells(3, grains)],
        in_specs=[SMEM] + [VMEM] * 6,
        out_specs=[VMEM] * 2,
        scratch_shapes=[pltpu.VMEM((quads,) + mine.shape, jnp.float32)],
        compiler_params=LIMIT,
        name="drag",
    )(place, grain_cell, weight, grain_velocity, factor, *gathered)
    return pressure, drag


def solution(mesh):
    placed = (
        P(None, ("slab", "quad")),
        P(("slab", "quad")),
        P(("slab", "quad")),
        P(("slab", "quad")),
        P(None, ("slab", "quad")),
    )
    return jax.shard_map(
        body,
        mesh=mesh,
        in_specs=placed,
        out_specs=(P("slab", "quad", None), P(None, ("slab", "quad"))),
        check_vma=False,
    )
```

```python
import functools

import jax
import jax.numpy as jnp
from jax import lax
from jax.experimental import pallas as pl
from jax.experimental.pallas import tpu as pltpu
from jax.sharding import PartitionSpec as P

CH = 4
CA = 16
CB = 256
ITERS = 12
LANES = 128
SUBLANES = 8
DEPTH = 2
FIRST = CH * DEPTH + 1

damping = 0.05
source_gain = 4.0

VMEM = pl.BlockSpec(memory_space=pltpu.VMEM)
SMEM = pl.BlockSpec(memory_space=pltpu.SMEM)
HBM = pl.BlockSpec(memory_space=pltpu.HBM)
LIMIT = pltpu.CompilerParams(vmem_limit_bytes=48 * 1024 * 1024)


def reach(distance):
    needed = ITERS - 1 - CH * (max(distance, 1) - 1)
    return 1 << (needed - 1).bit_length()


def lanes_of(shape):
    return lax.broadcasted_iota(jnp.int32, shape, len(shape) - 1)


def turned(value, shift):
    shift %= LANES
    return pltpu.roll(value, shift, value.ndim - 1) if shift else value


def pack_own(window, own):
    pieces = LANES // own
    tall = window.shape[1] // pieces
    lane = lanes_of((window.shape[0], tall, LANES))
    result = window[:, :tall]
    for piece in range(1, pieces):
        part = turned(window[:, piece * tall : (piece + 1) * tall], piece * own)
        result = jnp.where(lane < piece * own, result, part)
    return result


def unpack_own(packed, own):
    pieces = LANES // own
    return jnp.concatenate([turned(packed, -piece * own) for piece in range(pieces)], axis=1)


def strip_plan(across, fields, halo):
    rows = across * 2 * halo // LANES
    return (1, rows) if rows >= SUBLANES else (fields, rows * fields)


def packed_rows(across, fields, halo, own):
    shared, rows = strip_plan(across, fields, halo)
    return fields * CH * across * own // LANES + (fields // shared) * CH * rows


def pack(windows, halo, own):
    across = windows[0].shape[1]
    shared, rows = strip_plan(across, len(windows), halo)
    pieces = [pack_own(window, own) for window in windows]
    lane = lanes_of(windows[0].shape)
    joined = [
        jnp.where(lane >= LANES - halo, window, turned(window, LANES - 2 * halo - own))
        for window in windows
    ]
    lane = lanes_of((CH, rows, LANES))
    for first in range(0, len(windows), shared):
        strip, at = None, 0
        for value in joined[first : first + shared]:
            for row in range(0, across, rows):
                part = turned(value[:, row : row + rows], at + 2 * halo)
                strip = part if strip is None else jnp.where(lane < at, strip, part)
                at += 2 * halo
        pieces.append(strip)
    return jnp.concatenate([piece.reshape(-1, LANES) for piece in pieces], axis=0)


def unpack(value, fields, across, halo, own):
    shared, rows = strip_plan(across, fields, halo)
    tall = across * own // LANES
    count = fields * CH * tall
    owned = value[:count].reshape(fields, CH, tall, LANES)
    strips = value[count:].reshape(fields // shared, CH, rows, LANES)
    lane = lanes_of((CH, rows, LANES))
    windows = []
    for field in range(fields):
        window = unpack_own(owned[field], own)
        strip = strips[field // shared]
        at = (field % shared) * across // rows * 2 * halo
        blocks = []
        for row in range(0, across, rows):
            right = turned(strip, own - at)
            left = turned(strip, -2 * halo - at)
            block = jnp.where(lane < own + halo, right, 0.0)
            block = jnp.where(lane >= LANES - halo, left, block)
            blocks.append(jnp.where(lane < own, window[:, row : row + rows], block))
            at += 2 * halo
        windows.append(jnp.concatenate(blocks, axis=1))
    return windows


def halves(value):
    high = value.astype(jnp.bfloat16)
    low = (value - high.astype(jnp.float32)).astype(jnp.bfloat16)
    return high, low


def short_iota(shape):
    return lax.broadcasted_iota(jnp.int32, shape, 0).astype(jnp.int16)


def row_of(cell_ref, span, across):
    return cell_ref[1:2, span] * across + cell_ref[0:1, span] * CA + cell_ref[2:3, span]


def one_hot(rows, index):
    one, zero = jnp.bfloat16(1), jnp.bfloat16(0)
    return jnp.where(rows == index.astype(jnp.int16), one, zero)


def mass_of(count_ref, volume_ref, first, span):
    volume = volume_ref[0:1, span]
    slot = lax.broadcasted_iota(jnp.int32, volume.shape, 1) + first
    return jnp.where(slot < count_ref[0], volume, 0.0)


def deposit_kernel(quads, chunk, place_ref, count_ref, *refs):
    sources, outs = refs[:4], refs[4:6]
    cell_ref, weight_ref, volume_ref, velocity_ref, sems = refs[6:]
    copies = [
        pltpu.make_async_copy(source, target, sems.at[index])
        for index, (source, target) in enumerate(
            zip(sources, (cell_ref, weight_ref, volume_ref, velocity_ref))
        )
    ]
    for copy in copies:
        copy.start()
    across = quads * CA
    rows = CH * across
    grains = weight_ref.shape[1]
    own = CB // quads
    row_iota = short_iota((rows, chunk))
    col_iota = short_iota((CB, chunk))
    total = jnp.zeros((4 * CB, rows), jnp.float32)
    for copy in copies:
        copy.wait()
    for first in range(0, grains, chunk):
        span = pl.ds(first, chunk)
        mass = mass_of(count_ref, volume_ref, first, span)
        moment = mass * velocity_ref[0:1, span]
        lower = weight_ref[0:1, span]
        upper = 1.0 - lower
        hot = one_hot(row_iota, row_of(cell_ref, span, across))
        col = cell_ref[3:4, span]
        at_lower = col_iota == col.astype(jnp.int16)
        at_upper = col_iota == (col + 1).astype(jnp.int16)
        parts = []
        for amount in (mass, moment):
            for low, high in zip(halves(amount * lower), halves(amount * upper)):
                parts.append(jnp.where(at_lower, low, jnp.where(at_upper, high, jnp.bfloat16(0))))
        spread = jnp.concatenate(parts, axis=0)
        total = total + lax.dot_general(
            spread, hot, (((1,), (1,)), ((), ())), preferred_element_type=jnp.float32
        )
    lane = lanes_of((CH, across, LANES))
    fields = [
        (total[base : base + CB] + total[base + CB : base + 2 * CB]).T
        for base in range(0, 4 * CB, 2 * CB)
    ]
    for step in range(quads):
        target = place_ref[0] ^ step
        windows = []
        for field in fields:
            moved = pltpu.roll(field, lax.rem(CB - target * own, CB), 1)
            moved = moved.reshape(CH, across, CB)
            near, past = moved[:, :, :LANES], moved[:, :, CB - LANES :]
            windows.append(jnp.where(lane < (LANES + own) // 2, near, past))
        outs[step % 2][step // 2] = pack(windows, reach(0), own)


def coefficient_kernel(quads, place_ref, kept_ref, got_ref, *refs):
    outs, solid_ref = refs[:-1], refs[-1]
    across, own = quads * CA, CB // quads
    total = kept_ref[0] + got_ref[0]
    solid_ref[...] = total[: solid_ref.shape[0] * solid_ref.shape[1]].reshape(solid_ref.shape)
    solid, moment = unpack(total, 2, across, reach(0), own)
    lane = lanes_of(solid.shape)
    column = jnp.where(lane < (LANES + own) // 2, lane, lane - LANES) + place_ref[0] * own
    inside = (column >= 0) & (column < CB)
    voidage = 1.0 / (1.0 + solid)
    scale = 1.0 / (6.0 * voidage + damping)
    offset = jnp.where(inside, source_gain * moment * scale, 0.0)
    gain = jnp.where(inside, voidage * scale, 0.0)
    for distance, out in enumerate(outs):
        out[...] = pack((offset, gain), reach(distance + 1), own)


def sweep_over(sweeps, layers, across, old, new, offset_ref, gain_ref):
    row = lax.broadcasted_iota(jnp.int32, (across, LANES), 0)
    for sweep in range(1, sweeps + 1):
        for layer in range(sweep, layers - sweep):
            centre = old[layer]
            total = old[layer - 1] + old[layer + 1]
            total = total + turned(centre, 1) + turned(centre, -1)
            total = total + jnp.where(row == 0, 0.0, pltpu.roll(centre, 1, 0))
            total = total + jnp.where(row == across - 1, 0.0, pltpu.roll(centre, across - 1, 0))
            new[layer] = offset_ref[layer] + gain_ref[layer] * total
        old, new = new, old
    return old


def slot_of(slab, distance, matching):
    upward = lax.rem(lax.div(slab, distance), 2) ^ matching
    return distance * (1 - 2 * upward)


def swap_plan(depth):
    return [(distance, matching) for distance in range(1, depth + 1) for matching in range(2)]


def framed(last, first, own):
    inner = pack([last[first : first + CH]], SUBLANES, own)
    outer = [pack_own(last[layer : layer + 1], own)[0] for layer in (first - 1, first + CH)]
    return jnp.concatenate([inner] + outer, axis=0)


def relax_kernel(quads, slab_ref, own_ref, *refs):
    *parts, out_ref, offset_ref, gain_ref, even_ref, odd_ref = refs
    across, own = quads * CA, CB // quads
    layers = CH * (1 + len(parts))
    plan = [(DEPTH, own_ref, 1)] + [
        (DEPTH + slot_of(slab_ref[0], distance, matching), part, distance)
        for part, (distance, matching) in zip(parts, swap_plan(DEPTH))
    ]
    for slot, part, distance in plan:
        span = pl.ds(slot * CH, CH)
        offset, gain = unpack(part[...], 2, across, reach(distance), own)
        offset_ref[span] = offset
        even_ref[span] = offset
        gain_ref[span] = gain
    sweeps = min(FIRST, ITERS) - 1
    last = sweep_over(sweeps, layers, across, even_ref, odd_ref, offset_ref, gain_ref)
    if FIRST < ITERS:
        out_ref[...] = pack([last[DEPTH * CH : (DEPTH + 1) * CH]], SUBLANES, own)
    else:
        out_ref[...] = framed(last, DEPTH * CH, own)


def finish_kernel(quads, slab_ref, *refs):
    *parts, out_ref, offset_ref, gain_ref, even_ref, odd_ref = refs
    across, own = quads * CA, CB // quads
    slots = [1] + [1 + slot_of(slab_ref[0], *swap) for swap in swap_plan(1)]
    for slot, coef, pressure in zip(slots, parts[:3], parts[3:]):
        span = pl.ds(slot * CH, CH)
        offset_ref[span], gain_ref[span] = unpack(coef[...], 2, across, reach(1), own)
        (even_ref[span],) = unpack(pressure[...], 1, across, SUBLANES, own)
    last = sweep_over(ITERS - FIRST, 3 * CH, across, even_ref, odd_ref, offset_ref, gain_ref)
    out_ref[...] = framed(last, CH, own)


def halving(quads):
    return [1 << bit for bit in reversed(range(quads.bit_length() - 1))]


def place_offsets(quads):
    offsets = [0]
    for bit in halving(quads):
        offsets += [offset ^ bit for offset in offsets]
    return offsets


def whole_table(quads, place_ref, parts, gathered):
    own = CB // quads
    pieces = LANES // own
    for offset, part in zip(place_offsets(quads), parts):
        gathered[place_ref[0] ^ offset] = part
    lane = lanes_of(gathered.shape[1:])
    bands = []
    for piece in range(pieces):
        columns = []
        for first in range(0, quads, pieces):
            block = None
            for near in range(pieces):
                part = turned(gathered[first + near], (near - piece) * own)
                block = part if block is None else jnp.where(lane < near * own, block, part)
            columns.append(block)
        bands.append(jnp.concatenate(columns, axis=2))
    return jnp.concatenate(bands, axis=1)


def blend_of(col_iota, at, lower):
    return jnp.where(col_iota == at, lower, jnp.where(col_iota == at + 1, 1.0 - lower, 0.0))


def picked_by(pieces, hot):
    twice = jnp.concatenate([hot, hot], axis=0)
    return jnp.dot(pieces, twice, preferred_element_type=jnp.float32)


def blended(picked, blend, field):
    size = blend.shape[0]
    return jnp.sum(picked[field * size : (field + 1) * size] * blend, axis=0, keepdims=True)


def factor_kernel(quads, chunk, place_ref, count_ref, cell_ref, weight_ref, volume_ref, *refs):
    *halfs, factor_ref, gathered = refs
    across = quads * CA
    rows = CH * across
    parts = [half[index] for half in halfs for index in range(quads // 2)]
    solid = whole_table(quads, place_ref, parts, gathered)
    pieces = jnp.concatenate(halves(solid.reshape(rows, CB).T), axis=1)
    row_iota = short_iota((rows, chunk))
    col_iota = lax.broadcasted_iota(jnp.int32, (CB, chunk), 0)
    for first in range(0, weight_ref.shape[1], chunk):
        span = pl.ds(first, chunk)
        mass = mass_of(count_ref, volume_ref, first, span)
        hot = one_hot(row_iota, row_of(cell_ref, span, across))
        blend = blend_of(col_iota, cell_ref[3:4, span], weight_ref[0:1, span])
        sampled = blended(picked_by(pieces, hot), blend, 0)
        factor_ref[0:1, span] = mass * (1.0 + sampled) ** 2


def velocity_table(value, across, own):
    tall = across * own // LANES
    count = packed_rows(across, 1, SUBLANES, own)
    (inner,) = unpack(value[:count], 1, across, SUBLANES, own)
    outer = unpack_own(value[count:].reshape(2, tall, LANES), own)
    row = lax.broadcasted_iota(jnp.int32, inner.shape, 1)
    above = jnp.concatenate([inner[1:], outer[1:]], axis=0)
    below = jnp.concatenate([outer[:1], inner[:-1]], axis=0)
    after = jnp.where(row == across - 1, 0.0, pltpu.roll(inner, across - 1, 1))
    before = jnp.where(row == 0, 0.0, pltpu.roll(inner, 1, 1))
    fields = (
        -0.5 * (above - below),
        -0.5 * (after - before),
        -0.5 * (turned(inner, -1) - turned(inner, 1)),
    )
    columns = [field.reshape(CH * across, LANES).T[:own] for field in fields]
    return jnp.concatenate(halves(jnp.concatenate(columns, axis=0)), axis=1)


def velocity_chunk(quads, place_ref, tables, offsets, cell_ref, weight_ref, row_iota, span):
    across, own = quads * CA, CB // quads
    hot = one_hot(row_iota, row_of(cell_ref, span, across))
    lower = weight_ref[0:1, span]
    picked = picked_by(tables, hot)
    col_iota = lax.broadcasted_iota(jnp.int32, (own, picked.shape[1]), 0)
    sums = [0.0] * 3
    for index, offset in enumerate(offsets):
        at = cell_ref[3:4, span] - (place_ref[0] ^ offset) * own
        blend = blend_of(col_iota, at, lower)
        for component in range(3):
            sums[component] += blended(picked, blend, 3 * index + component)
    return sums


def sampled_kernel(quads, chunk, offset, index, place_ref, cell_ref, weight_ref, held_ref, *refs):
    *earlier, out_ref = refs
    across, own = quads * CA, CB // quads
    table = velocity_table(held_ref[index], across, own)
    row_iota = short_iota((CH * across, chunk))
    for first in range(0, weight_ref.shape[1], chunk):
        span = pl.ds(first, chunk)
        sums = velocity_chunk(
            quads, place_ref, table, [offset], cell_ref, weight_ref, row_iota, span
        )
        for component, value in enumerate(sums):
            one = pl.ds(component, 1)
            for partial in earlier:
                value = value + partial[one, span]
            out_ref[one, span] = value


def drag_kernel(quads, chunk, place_ref, cell_ref, weight_ref, velocity_ref, factor_ref, *refs):
    sampled_ref, held_ref, got_ref, pressure_ref, drag_ref, gathered = refs
    across, own = quads * CA, CB // quads
    half = quads // 2
    offsets = place_offsets(quads)[half:]
    tables = [velocity_table(got_ref[index], across, own) for index in range(half)]
    tables = jnp.concatenate(tables, axis=0)
    row_iota = short_iota((CH * across, chunk))
    for first in range(0, weight_ref.shape[1], chunk):
        span = pl.ds(first, chunk)
        sums = velocity_chunk(
            quads, place_ref, tables, offsets, cell_ref, weight_ref, row_iota, span
        )
        for component, value in enumerate(sums):
            one = pl.ds(component, 1)
            drag_ref[one, span] = factor_ref[0:1, span] * (
                value + sampled_ref[one, span] - velocity_ref[one, span]
            )
    shape = gathered.shape[1:]
    count = CH * shape[1]
    parts = [
        ref[index][:count].reshape(shape) for ref in (held_ref, got_ref) for index in range(half)
    ]
    pressure = whole_table(quads, place_ref, parts, gathered)
    mine = pltpu.roll(pressure, lax.rem(across - place_ref[0] * CA, across), 1)
    pressure_ref[...] = mine[:, :CA]


def body(grain_cell, grain_count, grain_weight, grain_volume, grain_velocity):
    quads = lax.axis_size("quad")
    slabs = lax.axis_size("slab")
    grains = grain_weight.shape[0]
    across = quads * CA
    own = CB // quads
    tall = across * own // LANES
    place = lax.axis_index("quad").astype(jnp.int32).reshape(1)
    level = lax.axis_index("slab").astype(jnp.int32).reshape(1)
    weight = grain_weight.reshape(1, grains)
    volume = grain_volume.reshape(1, grains)

    def cells(*shape):
        return jax.ShapeDtypeStruct(shape, jnp.float32)

    def over_quad(step, value):
        pairs = [(index, index ^ step) for index in range(quads)]
        return lax.ppermute(value, "quad", pairs)

    def swapped(distance, matching, value):
        lower = [
            index
            for index in range(slabs - distance)
            if (index // distance) % 2 == matching
        ]
        pairs = [(index, index + distance) for index in lower]
        return lax.ppermute(value, "slab", pairs + [(high, low) for low, high in pairs])

    *early, last = halving(quads)

    def nearly_all(value):
        held = value[None]
        for bit in early:
            held = jnp.concatenate([held, over_quad(bit, held)], axis=0)
        return held

    def pinned(value):
        return pltpu.with_memory_space_constraint(value, pltpu.HBM)

    kept, sent = pl.pallas_call(
        functools.partial(deposit_kernel, quads, min(grains, 2048)),
        out_shape=[cells(quads // 2, packed_rows(across, 2, reach(0), own), LANES)] * 2,
        in_specs=[SMEM, SMEM] + [HBM] * 4,
        out_specs=[VMEM] * 2,
        scratch_shapes=[
            pltpu.VMEM((4, grains), jnp.int32),
            pltpu.VMEM((1, grains), jnp.float32),
            pltpu.VMEM((1, grains), jnp.float32),
            pltpu.VMEM((3, grains), jnp.float32),
            pltpu.SemaphoreType.DMA((4,)),
        ],
        compiler_params=LIMIT,
        name="deposit",
    )(
        place,
        grain_count,
        pinned(grain_cell),
        pinned(weight),
        pinned(volume),
        pinned(grain_velocity),
    )

    bit = 1
    got = over_quad(bit, sent)
    while kept.shape[0] > 1:
        bit *= 2
        total = kept + got
        kept, sent = total[0::2], total[1::2]
        got = over_quad(bit, sent)
    *coefs, solid = pl.pallas_call(
        functools.partial(coefficient_kernel, quads),
        out_shape=[
            cells(packed_rows(across, 2, reach(distance), own), LANES)
            for distance in range(1, DEPTH + 1)
        ]
        + [cells(CH, tall, LANES)],
        in_specs=[SMEM] + [VMEM] * 2,
        out_specs=[VMEM] * (DEPTH + 1),
        compiler_params=LIMIT,
        name="coefficients",
    )(place, kept, got)

    stack = [coefs[0]] + [
        swapped(distance, matching, coefs[distance - 1])
        for distance, matching in swap_plan(DEPTH)
    ]
    solids = nearly_all(solid)
    solids = [solids, over_quad(last, solids)]
    stack, solids = lax.optimization_barrier((stack, solids))
    factor = pl.pallas_call(
        functools.partial(factor_kernel, quads, min(grains, 512)),
        out_shape=cells(1, grains),
        in_specs=[SMEM, SMEM] + [VMEM] * 5,
        out_specs=VMEM,
        scratch_shapes=[pltpu.VMEM((quads,) + solid.shape, jnp.float32)],
        compiler_params=LIMIT,
        cost_estimate=pl.CostEstimate(
            flops=4 * CB * CH * across * grains, bytes_accessed=2**20, transcendentals=0
        ),
        name="factor",
    )(place, grain_count, grain_cell, weight, volume, *solids)

    frame = cells(packed_rows(across, 1, SUBLANES, own) + 2 * tall, LANES)
    layers = CH * len(stack)
    two_rounds = FIRST < ITERS
    centre = pl.pallas_call(
        functools.partial(relax_kernel, quads),
        out_shape=cells(packed_rows(across, 1, SUBLANES, own), LANES)
        if two_rounds
        else frame,
        in_specs=[SMEM] + [VMEM] * len(stack),
        out_specs=VMEM,
        scratch_shapes=[pltpu.VMEM((layers, across, LANES), jnp.float32)] * 4,
        compiler_params=LIMIT,
        name="relax",
    )(level, *stack)
    mine = centre
    if two_rounds:
        pressures = [centre] + [swapped(*swap, centre) for swap in swap_plan(1)]
        pressures, factor = lax.optimization_barrier((pressures, factor))
        mine = pl.pallas_call(
            functools.partial(finish_kernel, quads),
            out_shape=frame,
            in_specs=[SMEM] + [VMEM] * 6,
            out_specs=VMEM,
            scratch_shapes=[pltpu.VMEM((3 * CH, across, LANES), jnp.float32)] * 4,
            compiler_params=LIMIT,
            name="finish",
        )(level, *stack[:3], *pressures)

    grain_chunk = min(grains, 512)

    def sampled_from(held, index, *earlier):
        return pl.pallas_call(
            functools.partial(
                sampled_kernel, quads, grain_chunk, place_offsets(quads)[index], index
            ),
            out_shape=cells(3, grains),
            in_specs=[SMEM] + [VMEM] * (3 + len(earlier)),
            out_specs=VMEM,
            compiler_params=LIMIT,
            cost_estimate=pl.CostEstimate(
                flops=12 * own * CH * across * grains, bytes_accessed=2**20, transcendentals=0
            ),
            name="sampled",
        )(place, grain_cell, weight, held, *earlier)

    held = mine[None]
    partial = sampled_from(held, 0)
    for bit in early:
        known = held.shape[0]
        held = jnp.concatenate([held, over_quad(bit, held)], axis=0)
        held, partial = lax.optimization_barrier((held, partial))
        for index in range(known, held.shape[0]):
            partial = sampled_from(held, index, partial)
    got = over_quad(last, held)
    pressure, drag = pl.pallas_call(
        functools.partial(drag_kernel, quads, grain_chunk),
        out_shape=[cells(CH, CA, CB), cells(3, grains)],
        in_specs=[SMEM] + [VMEM] * 7,
        out_specs=[VMEM] * 2,
        scratch_shapes=[pltpu.VMEM((quads, CH, tall, LANES), jnp.float32)],
        compiler_params=LIMIT,
        name="drag",
    )(place, grain_cell, weight, grain_velocity, factor, partial, held, got)
    return pressure, drag


def solution(mesh):
    placed = (
        P(None, ("slab", "quad")),
        P(("slab", "quad")),
        P(("slab", "quad")),
        P(("slab", "quad")),
        P(None, ("slab", "quad")),
    )
    return jax.shard_map(
        body,
        mesh=mesh,
        in_specs=placed,
        out_specs=(P("slab", "quad", None), P(None, ("slab", "quad"))),
        check_vma=False,
    )
```

```python
import functools

import jax
import jax.numpy as jnp
from jax import lax
from jax.experimental import pallas as pl
from jax.experimental.pallas import tpu as pltpu
from jax.sharding import PartitionSpec as P

CH = 4
CA = 16
CB = 256
ITERS = 12
LANES = 128
SUBLANES = 8
DEPTH = 2
FIRST = CH * DEPTH + 1

damping = 0.05
source_gain = 4.0

VMEM = pl.BlockSpec(memory_space=pltpu.VMEM)
SMEM = pl.BlockSpec(memory_space=pltpu.SMEM)
HBM = pl.BlockSpec(memory_space=pltpu.HBM)
LIMIT = pltpu.CompilerParams(vmem_limit_bytes=48 * 1024 * 1024)


def reach(distance):
    needed = ITERS - 1 - CH * (max(distance, 1) - 1)
    return 1 << (needed - 1).bit_length()


def lanes_of(shape):
    return lax.broadcasted_iota(jnp.int32, shape, len(shape) - 1)


def turned(value, shift):
    shift %= LANES
    return pltpu.roll(value, shift, value.ndim - 1) if shift else value


def pack_own(window, own):
    pieces = LANES // own
    tall = window.shape[1] // pieces
    lane = lanes_of((window.shape[0], tall, LANES))
    result = window[:, :tall]
    for piece in range(1, pieces):
        part = turned(window[:, piece * tall : (piece + 1) * tall], piece * own)
        result = jnp.where(lane < piece * own, result, part)
    return result


def unpack_own(packed, own):
    pieces = LANES // own
    return jnp.concatenate([turned(packed, -piece * own) for piece in range(pieces)], axis=1)


def strip_plan(across, fields, halo):
    rows = across * 2 * halo // LANES
    return (1, rows) if rows >= SUBLANES else (fields, rows * fields)


def packed_rows(across, fields, halo, own):
    shared, rows = strip_plan(across, fields, halo)
    return fields * CH * across * own // LANES + (fields // shared) * CH * rows


def pack(windows, halo, own):
    across = windows[0].shape[1]
    shared, rows = strip_plan(across, len(windows), halo)
    pieces = [pack_own(window, own) for window in windows]
    lane = lanes_of(windows[0].shape)
    joined = [
        jnp.where(lane >= LANES - halo, window, turned(window, LANES - 2 * halo - own))
        for window in windows
    ]
    lane = lanes_of((CH, rows, LANES))
    for first in range(0, len(windows), shared):
        strip, at = None, 0
        for value in joined[first : first + shared]:
            for row in range(0, across, rows):
                part = turned(value[:, row : row + rows], at + 2 * halo)
                strip = part if strip is None else jnp.where(lane < at, strip, part)
                at += 2 * halo
        pieces.append(strip)
    return jnp.concatenate([piece.reshape(-1, LANES) for piece in pieces], axis=0)


def unpack(value, fields, across, halo, own):
    shared, rows = strip_plan(across, fields, halo)
    tall = across * own // LANES
    count = fields * CH * tall
    owned = value[:count].reshape(fields, CH, tall, LANES)
    strips = value[count:].reshape(fields // shared, CH, rows, LANES)
    lane = lanes_of((CH, rows, LANES))
    windows = []
    for field in range(fields):
        window = unpack_own(owned[field], own)
        strip = strips[field // shared]
        at = (field % shared) * across // rows * 2 * halo
        blocks = []
        for row in range(0, across, rows):
            right = turned(strip, own - at)
            left = turned(strip, -2 * halo - at)
            block = jnp.where(lane < own + halo, right, 0.0)
            block = jnp.where(lane >= LANES - halo, left, block)
            blocks.append(jnp.where(lane < own, window[:, row : row + rows], block))
            at += 2 * halo
        windows.append(jnp.concatenate(blocks, axis=1))
    return windows


def halves(value):
    high = value.astype(jnp.bfloat16)
    low = (value - high.astype(jnp.float32)).astype(jnp.bfloat16)
    return high, low


def short_iota(shape):
    return lax.broadcasted_iota(jnp.int32, shape, 0).astype(jnp.int16)


def row_of(cell_ref, span, across):
    return cell_ref[1:2, span] * across + cell_ref[0:1, span] * CA + cell_ref[2:3, span]


def one_hot(rows, index):
    one, zero = jnp.bfloat16(1), jnp.bfloat16(0)
    return jnp.where(rows == index.astype(jnp.int16), one, zero)


def mass_of(count_ref, volume_ref, first, span):
    volume = volume_ref[0:1, span]
    slot = lax.broadcasted_iota(jnp.int32, volume.shape, 1) + first
    return jnp.where(slot < count_ref[0], volume, 0.0)


def deposit_kernel(quads, chunk, place_ref, count_ref, *refs):
    sources, outs = refs[:4], refs[4:6]
    cell_ref, weight_ref, volume_ref, velocity_ref, sems = refs[6:]
    copies = [
        pltpu.make_async_copy(source, target, sems.at[index])
        for index, (source, target) in enumerate(
            zip(sources, (cell_ref, weight_ref, volume_ref, velocity_ref))
        )
    ]
    for copy in copies:
        copy.start()
    across = quads * CA
    rows = CH * across
    grains = weight_ref.shape[1]
    own = CB // quads
    row_iota = short_iota((rows, chunk))
    col_iota = short_iota((CB, chunk))
    total = jnp.zeros((4 * CB, rows), jnp.float32)
    for copy in copies:
        copy.wait()
    for first in range(0, grains, chunk):
        span = pl.ds(first, chunk)
        mass = mass_of(count_ref, volume_ref, first, span)
        moment = mass * velocity_ref[0:1, span]
        lower = weight_ref[0:1, span]
        upper = 1.0 - lower
        hot = one_hot(row_iota, row_of(cell_ref, span, across))
        col = cell_ref[3:4, span]
        at_lower = col_iota == col.astype(jnp.int16)
        at_upper = col_iota == (col + 1).astype(jnp.int16)
        parts = []
        for amount in (mass, moment):
            for low, high in zip(halves(amount * lower), halves(amount * upper)):
                parts.append(jnp.where(at_lower, low, jnp.where(at_upper, high, jnp.bfloat16(0))))
        spread = jnp.concatenate(parts, axis=0)
        total = total + lax.dot_general(
            spread, hot, (((1,), (1,)), ((), ())), preferred_element_type=jnp.float32
        )
    lane = lanes_of((CH, across, LANES))
    fields = [
        (total[base : base + CB] + total[base + CB : base + 2 * CB]).T
        for base in range(0, 4 * CB, 2 * CB)
    ]
    for step in range(quads):
        target = place_ref[0] ^ step
        windows = []
        for field in fields:
            moved = pltpu.roll(field, lax.rem(CB - target * own, CB), 1)
            moved = moved.reshape(CH, across, CB)
            near, past = moved[:, :, :LANES], moved[:, :, CB - LANES :]
            windows.append(jnp.where(lane < (LANES + own) // 2, near, past))
        outs[step % 2][step // 2] = pack(windows, reach(0), own)


def coefficient_kernel(quads, place_ref, kept_ref, got_ref, *refs):
    outs, solid_ref = refs[:-1], refs[-1]
    across, own = quads * CA, CB // quads
    total = kept_ref[0] + got_ref[0]
    solid_ref[...] = total[: solid_ref.shape[0] * solid_ref.shape[1]].reshape(solid_ref.shape)
    solid, moment = unpack(total, 2, across, reach(0), own)
    lane = lanes_of(solid.shape)
    column = jnp.where(lane < (LANES + own) // 2, lane, lane - LANES) + place_ref[0] * own
    inside = (column >= 0) & (column < CB)
    voidage = 1.0 / (1.0 + solid)
    scale = 1.0 / (6.0 * voidage + damping)
    offset = jnp.where(inside, source_gain * moment * scale, 0.0)
    gain = jnp.where(inside, voidage * scale, 0.0)
    for distance, out in enumerate(outs):
        out[...] = pack((offset, gain), reach(distance + 1), own)


def sweep_over(sweeps, layers, across, old, new, offset_ref, gain_ref):
    row = lax.broadcasted_iota(jnp.int32, (across, LANES), 0)
    for sweep in range(1, sweeps + 1):
        for layer in range(sweep, layers - sweep):
            centre = old[layer]
            total = old[layer - 1] + old[layer + 1]
            total = total + turned(centre, 1) + turned(centre, -1)
            total = total + jnp.where(row == 0, 0.0, pltpu.roll(centre, 1, 0))
            total = total + jnp.where(row == across - 1, 0.0, pltpu.roll(centre, across - 1, 0))
            new[layer] = offset_ref[layer] + gain_ref[layer] * total
        old, new = new, old
    return old


def slot_of(slab, distance, matching):
    upward = lax.rem(lax.div(slab, distance), 2) ^ matching
    return distance * (1 - 2 * upward)


def swap_plan(depth):
    return [(distance, matching) for distance in range(1, depth + 1) for matching in range(2)]


def framed(last, first, own):
    inner = pack([last[first : first + CH]], SUBLANES, own)
    outer = [pack_own(last[layer : layer + 1], own)[0] for layer in (first - 1, first + CH)]
    return jnp.concatenate([inner] + outer, axis=0)


def relax_kernel(quads, slab_ref, own_ref, *refs):
    *parts, out_ref, offset_ref, gain_ref, even_ref, odd_ref = refs
    across, own = quads * CA, CB // quads
    layers = CH * (1 + len(parts))
    plan = [(DEPTH, own_ref, 1)] + [
        (DEPTH + slot_of(slab_ref[0], distance, matching), part, distance)
        for part, (distance, matching) in zip(parts, swap_plan(DEPTH))
    ]
    for slot, part, distance in plan:
        span = pl.ds(slot * CH, CH)
        offset, gain = unpack(part[...], 2, across, reach(distance), own)
        offset_ref[span] = offset
        even_ref[span] = offset
        gain_ref[span] = gain
    sweeps = min(FIRST, ITERS) - 1
    last = sweep_over(sweeps, layers, across, even_ref, odd_ref, offset_ref, gain_ref)
    if FIRST < ITERS:
        out_ref[...] = pack([last[DEPTH * CH : (DEPTH + 1) * CH]], SUBLANES, own)
    else:
        out_ref[...] = framed(last, DEPTH * CH, own)


def finish_kernel(quads, slab_ref, *refs):
    *parts, out_ref, offset_ref, gain_ref, even_ref, odd_ref = refs
    across, own = quads * CA, CB // quads
    slots = [1] + [1 + slot_of(slab_ref[0], *swap) for swap in swap_plan(1)]
    for slot, coef, pressure in zip(slots, parts[:3], parts[3:]):
        span = pl.ds(slot * CH, CH)
        offset_ref[span], gain_ref[span] = unpack(coef[...], 2, across, reach(1), own)
        (even_ref[span],) = unpack(pressure[...], 1, across, SUBLANES, own)
    last = sweep_over(ITERS - FIRST, 3 * CH, across, even_ref, odd_ref, offset_ref, gain_ref)
    out_ref[...] = framed(last, CH, own)


def halving(quads):
    return [1 << bit for bit in reversed(range(quads.bit_length() - 1))]


def place_offsets(quads):
    offsets = [0]
    for bit in halving(quads):
        offsets += [offset ^ bit for offset in offsets]
    return offsets


def whole_table(quads, place_ref, parts, gathered):
    own = CB // quads
    pieces = LANES // own
    for offset, part in zip(place_offsets(quads), parts):
        gathered[place_ref[0] ^ offset] = part
    lane = lanes_of(gathered.shape[1:])
    bands = []
    for piece in range(pieces):
        columns = []
        for first in range(0, quads, pieces):
            block = None
            for near in range(pieces):
                part = turned(gathered[first + near], (near - piece) * own)
                block = part if block is None else jnp.where(lane < near * own, block, part)
            columns.append(block)
        bands.append(jnp.concatenate(columns, axis=2))
    return jnp.concatenate(bands, axis=1)


def blend_of(col_iota, at, lower):
    return jnp.where(col_iota == at, lower, jnp.where(col_iota == at + 1, 1.0 - lower, 0.0))


def picked_by(pieces, hot):
    twice = jnp.concatenate([hot, hot], axis=0)
    return jnp.dot(pieces, twice, preferred_element_type=jnp.float32)


def blended(picked, blend, field):
    size = blend.shape[0]
    return jnp.sum(picked[field * size : (field + 1) * size] * blend, axis=0, keepdims=True)


def factor_kernel(quads, chunk, place_ref, count_ref, cell_ref, weight_ref, volume_ref, *refs):
    *halfs, factor_ref, gathered = refs
    across = quads * CA
    rows = CH * across
    parts = [half[index] for half in halfs for index in range(quads // 2)]
    solid = whole_table(quads, place_ref, parts, gathered)
    pieces = jnp.concatenate(halves(solid.reshape(rows, CB).T), axis=1)
    row_iota = short_iota((rows, chunk))
    col_iota = lax.broadcasted_iota(jnp.int32, (CB, chunk), 0)
    for first in range(0, weight_ref.shape[1], chunk):
        span = pl.ds(first, chunk)
        mass = mass_of(count_ref, volume_ref, first, span)
        hot = one_hot(row_iota, row_of(cell_ref, span, across))
        blend = blend_of(col_iota, cell_ref[3:4, span], weight_ref[0:1, span])
        sampled = blended(picked_by(pieces, hot), blend, 0)
        factor_ref[0:1, span] = mass * (1.0 + sampled) ** 2


def velocity_table(value, across, own):
    tall = across * own // LANES
    count = packed_rows(across, 1, SUBLANES, own)
    (inner,) = unpack(value[:count], 1, across, SUBLANES, own)
    outer = unpack_own(value[count:].reshape(2, tall, LANES), own)
    row = lax.broadcasted_iota(jnp.int32, inner.shape, 1)
    above = jnp.concatenate([inner[1:], outer[1:]], axis=0)
    below = jnp.concatenate([outer[:1], inner[:-1]], axis=0)
    after = jnp.where(row == across - 1, 0.0, pltpu.roll(inner, across - 1, 1))
    before = jnp.where(row == 0, 0.0, pltpu.roll(inner, 1, 1))
    fields = (
        -0.5 * (above - below),
        -0.5 * (after - before),
        -0.5 * (turned(inner, -1) - turned(inner, 1)),
    )
    columns = [field.reshape(CH * across, LANES).T[:own] for field in fields]
    return jnp.concatenate(halves(jnp.concatenate(columns, axis=0)), axis=1)


def velocity_chunk(quads, place_ref, tables, offsets, cell_ref, weight_ref, row_iota, span):
    across, own = quads * CA, CB // quads
    hot = one_hot(row_iota, row_of(cell_ref, span, across))
    lower = weight_ref[0:1, span]
    picked = picked_by(tables, hot)
    col_iota = lax.broadcasted_iota(jnp.int32, (own, picked.shape[1]), 0)
    sums = [0.0] * 3
    for index, offset in enumerate(offsets):
        at = cell_ref[3:4, span] - (place_ref[0] ^ offset) * own
        blend = blend_of(col_iota, at, lower)
        for component in range(3):
            sums[component] += blended(picked, blend, 3 * index + component)
    return sums


def sampled_kernel(quads, chunk, offset, index, place_ref, cell_ref, weight_ref, held_ref, *refs):
    *earlier, out_ref = refs
    across, own = quads * CA, CB // quads
    table = velocity_table(held_ref[index], across, own)
    row_iota = short_iota((CH * across, chunk))
    for first in range(0, weight_ref.shape[1], chunk):
        span = pl.ds(first, chunk)
        sums = velocity_chunk(
            quads, place_ref, table, [offset], cell_ref, weight_ref, row_iota, span
        )
        for component, value in enumerate(sums):
            one = pl.ds(component, 1)
            for partial in earlier:
                value = value + partial[one, span]
            out_ref[one, span] = value


def drag_kernel(quads, chunk, place_ref, cell_ref, weight_ref, velocity_ref, factor_ref, *refs):
    sampled_ref, held_ref, got_ref, pressure_ref, drag_ref, gathered = refs
    across, own = quads * CA, CB // quads
    half = quads // 2
    offsets = place_offsets(quads)[half:]
    tables = [velocity_table(got_ref[index], across, own) for index in range(half)]
    tables = jnp.concatenate(tables, axis=0)
    row_iota = short_iota((CH * across, chunk))
    for first in range(0, weight_ref.shape[1], chunk):
        span = pl.ds(first, chunk)
        sums = velocity_chunk(
            quads, place_ref, tables, offsets, cell_ref, weight_ref, row_iota, span
        )
        for component, value in enumerate(sums):
            one = pl.ds(component, 1)
            drag_ref[one, span] = factor_ref[0:1, span] * (
                value + sampled_ref[one, span] - velocity_ref[one, span]
            )
    shape = gathered.shape[1:]
    count = CH * shape[1]
    parts = [
        ref[index][:count].reshape(shape) for ref in (held_ref, got_ref) for index in range(half)
    ]
    pressure = whole_table(quads, place_ref, parts, gathered)
    mine = pltpu.roll(pressure, lax.rem(across - place_ref[0] * CA, across), 1)
    pressure_ref[...] = mine[:, :CA]


def body(grain_cell, grain_count, grain_weight, grain_volume, grain_velocity):
    quads = lax.axis_size("quad")
    slabs = lax.axis_size("slab")
    grains = grain_weight.shape[0]
    across = quads * CA
    own = CB // quads
    tall = across * own // LANES
    place = lax.axis_index("quad").astype(jnp.int32).reshape(1)
    level = lax.axis_index("slab").astype(jnp.int32).reshape(1)
    weight = grain_weight.reshape(1, grains)
    volume = grain_volume.reshape(1, grains)

    def cells(*shape):
        return jax.ShapeDtypeStruct(shape, jnp.float32)

    def over_quad(step, value):
        pairs = [(index, index ^ step) for index in range(quads)]
        return lax.ppermute(value, "quad", pairs)

    def swapped(distance, matching, value):
        lower = [
            index
            for index in range(slabs - distance)
            if (index // distance) % 2 == matching
        ]
        pairs = [(index, index + distance) for index in lower]
        return lax.ppermute(value, "slab", pairs + [(high, low) for low, high in pairs])

    *early, last = halving(quads)

    def nearly_all(value):
        held = value[None]
        for bit in early:
            held = jnp.concatenate([held, over_quad(bit, held)], axis=0)
        return held

    def pinned(value):
        return pltpu.with_memory_space_constraint(value, pltpu.HBM)

    kept, sent = pl.pallas_call(
        functools.partial(deposit_kernel, quads, min(grains, 2048)),
        out_shape=[cells(quads // 2, packed_rows(across, 2, reach(0), own), LANES)] * 2,
        in_specs=[SMEM, SMEM] + [HBM] * 4,
        out_specs=[VMEM] * 2,
        scratch_shapes=[
            pltpu.VMEM((4, grains), jnp.int32),
            pltpu.VMEM((1, grains), jnp.float32),
            pltpu.VMEM((1, grains), jnp.float32),
            pltpu.VMEM((3, grains), jnp.float32),
            pltpu.SemaphoreType.DMA((4,)),
        ],
        compiler_params=LIMIT,
        name="deposit",
    )(
        place,
        grain_count,
        pinned(grain_cell),
        pinned(weight),
        pinned(volume),
        pinned(grain_velocity),
    )

    bit = 1
    got = over_quad(bit, sent)
    while kept.shape[0] > 1:
        bit *= 2
        total = kept + got
        kept, sent = total[0::2], total[1::2]
        got = over_quad(bit, sent)
    *coefs, solid = pl.pallas_call(
        functools.partial(coefficient_kernel, quads),
        out_shape=[
            cells(packed_rows(across, 2, reach(distance), own), LANES)
            for distance in range(1, DEPTH + 1)
        ]
        + [cells(CH, tall, LANES)],
        in_specs=[SMEM] + [VMEM] * 2,
        out_specs=[VMEM] * (DEPTH + 1),
        compiler_params=LIMIT,
        name="coefficients",
    )(place, kept, got)

    stack = [coefs[0]] + [
        swapped(distance, matching, coefs[distance - 1])
        for distance, matching in swap_plan(DEPTH)
    ]
    stack[-1], solid = lax.optimization_barrier((stack[-1], solid))
    solids = nearly_all(solid)
    frame = cells(packed_rows(across, 1, SUBLANES, own) + 2 * tall, LANES)
    layers = CH * len(stack)
    two_rounds = FIRST < ITERS
    centre = pl.pallas_call(
        functools.partial(relax_kernel, quads),
        out_shape=cells(packed_rows(across, 1, SUBLANES, own), LANES)
        if two_rounds
        else frame,
        in_specs=[SMEM] + [VMEM] * len(stack),
        out_specs=VMEM,
        scratch_shapes=[pltpu.VMEM((layers, across, LANES), jnp.float32)] * 4,
        compiler_params=LIMIT,
        name="relax",
    )(level, *stack)
    centre, solids = lax.optimization_barrier((centre, solids))
    solids = [solids, over_quad(last, solids)]
    factor = pl.pallas_call(
        functools.partial(factor_kernel, quads, min(grains, 512)),
        out_shape=cells(1, grains),
        in_specs=[SMEM, SMEM] + [VMEM] * 5,
        out_specs=VMEM,
        scratch_shapes=[pltpu.VMEM((quads,) + solid.shape, jnp.float32)],
        compiler_params=LIMIT,
        cost_estimate=pl.CostEstimate(
            flops=4 * CB * CH * across * grains, bytes_accessed=2**20, transcendentals=0
        ),
        name="factor",
    )(place, grain_count, grain_cell, weight, volume, *solids)

    mine = centre
    if two_rounds:
        pressures = [centre] + [swapped(*swap, centre) for swap in swap_plan(1)]
        pressures, factor = lax.optimization_barrier((pressures, factor))
        mine = pl.pallas_call(
            functools.partial(finish_kernel, quads),
            out_shape=frame,
            in_specs=[SMEM] + [VMEM] * 6,
            out_specs=VMEM,
            scratch_shapes=[pltpu.VMEM((3 * CH, across, LANES), jnp.float32)] * 4,
            compiler_params=LIMIT,
            name="finish",
        )(level, *stack[:3], *pressures)

    grain_chunk = min(grains, 512)

    def sampled_from(held, index, *earlier):
        return pl.pallas_call(
            functools.partial(
                sampled_kernel, quads, grain_chunk, place_offsets(quads)[index], index
            ),
            out_shape=cells(3, grains),
            in_specs=[SMEM] + [VMEM] * (3 + len(earlier)),
            out_specs=VMEM,
            compiler_params=LIMIT,
            cost_estimate=pl.CostEstimate(
                flops=12 * own * CH * across * grains, bytes_accessed=2**20, transcendentals=0
            ),
            name="sampled",
        )(place, grain_cell, weight, held, *earlier)

    held = mine[None]
    partial = sampled_from(held, 0)
    for bit in early:
        known = held.shape[0]
        held = jnp.concatenate([held, over_quad(bit, held)], axis=0)
        held, partial = lax.optimization_barrier((held, partial))
        for index in range(known, held.shape[0]):
            partial = sampled_from(held, index, partial)
    got = over_quad(last, held)
    pressure, drag = pl.pallas_call(
        functools.partial(drag_kernel, quads, grain_chunk),
        out_shape=[cells(CH, CA, CB), cells(3, grains)],
        in_specs=[SMEM] + [VMEM] * 7,
        out_specs=[VMEM] * 2,
        scratch_shapes=[pltpu.VMEM((quads, CH, tall, LANES), jnp.float32)],
        compiler_params=LIMIT,
        name="drag",
    )(place, grain_cell, weight, grain_velocity, factor, partial, held, got)
    return pressure, drag


def solution(mesh):
    placed = (
        P(None, ("slab", "quad")),
        P(("slab", "quad")),
        P(("slab", "quad")),
        P(("slab", "quad")),
        P(None, ("slab", "quad")),
    )
    return jax.shard_map(
        body,
        mesh=mesh,
        in_specs=placed,
        out_specs=(P("slab", "quad", None), P(None, ("slab", "quad"))),
        check_vma=False,
    )
```

```python
import functools

import jax
import jax.numpy as jnp
from jax import lax
from jax.experimental import pallas as pl
from jax.experimental.pallas import tpu as pltpu
from jax.sharding import PartitionSpec as P

CH = 4
CA = 16
CB = 256
ITERS = 12
LANES = 128
SUBLANES = 8
DEPTH = 2
FIRST = CH * DEPTH + 1

damping = 0.05
source_gain = 4.0

VMEM = pl.BlockSpec(memory_space=pltpu.VMEM)
SMEM = pl.BlockSpec(memory_space=pltpu.SMEM)
HBM = pl.BlockSpec(memory_space=pltpu.HBM)
LIMIT = pltpu.CompilerParams(vmem_limit_bytes=48 * 1024 * 1024)


def reach(distance):
    needed = ITERS - 1 - CH * (max(distance, 1) - 1)
    return 1 << (needed - 1).bit_length()


def lanes_of(shape):
    return lax.broadcasted_iota(jnp.int32, shape, len(shape) - 1)


def turned(value, shift):
    shift %= LANES
    return pltpu.roll(value, shift, value.ndim - 1) if shift else value


def pack_own(window, own):
    pieces = LANES // own
    tall = window.shape[1] // pieces
    lane = lanes_of((window.shape[0], tall, LANES))
    result = window[:, :tall]
    for piece in range(1, pieces):
        part = turned(window[:, piece * tall : (piece + 1) * tall], piece * own)
        result = jnp.where(lane < piece * own, result, part)
    return result


def unpack_own(packed, own):
    pieces = LANES // own
    return jnp.concatenate([turned(packed, -piece * own) for piece in range(pieces)], axis=1)


def strip_plan(across, fields, halo):
    rows = across * 2 * halo // LANES
    return (1, rows) if rows >= SUBLANES else (fields, rows * fields)


def packed_rows(across, fields, halo, own):
    shared, rows = strip_plan(across, fields, halo)
    return fields * CH * across * own // LANES + (fields // shared) * CH * rows


def pack(windows, halo, own):
    across = windows[0].shape[1]
    shared, rows = strip_plan(across, len(windows), halo)
    pieces = [pack_own(window, own) for window in windows]
    lane = lanes_of(windows[0].shape)
    joined = [
        jnp.where(lane >= LANES - halo, window, turned(window, LANES - 2 * halo - own))
        for window in windows
    ]
    lane = lanes_of((CH, rows, LANES))
    for first in range(0, len(windows), shared):
        strip, at = None, 0
        for value in joined[first : first + shared]:
            for row in range(0, across, rows):
                part = turned(value[:, row : row + rows], at + 2 * halo)
                strip = part if strip is None else jnp.where(lane < at, strip, part)
                at += 2 * halo
        pieces.append(strip)
    return jnp.concatenate([piece.reshape(-1, LANES) for piece in pieces], axis=0)


def unpack(value, fields, across, halo, own):
    shared, rows = strip_plan(across, fields, halo)
    tall = across * own // LANES
    count = fields * CH * tall
    owned = value[:count].reshape(fields, CH, tall, LANES)
    strips = value[count:].reshape(fields // shared, CH, rows, LANES)
    lane = lanes_of((CH, rows, LANES))
    windows = []
    for field in range(fields):
        window = unpack_own(owned[field], own)
        strip = strips[field // shared]
        at = (field % shared) * across // rows * 2 * halo
        blocks = []
        for row in range(0, across, rows):
            right = turned(strip, own - at)
            left = turned(strip, -2 * halo - at)
            block = jnp.where(lane < own + halo, right, 0.0)
            block = jnp.where(lane >= LANES - halo, left, block)
            blocks.append(jnp.where(lane < own, window[:, row : row + rows], block))
            at += 2 * halo
        windows.append(jnp.concatenate(blocks, axis=1))
    return windows


def halves(value):
    high = value.astype(jnp.bfloat16)
    low = (value - high.astype(jnp.float32)).astype(jnp.bfloat16)
    return high, low


def short_iota(shape):
    return lax.broadcasted_iota(jnp.int32, shape, 0).astype(jnp.int16)


def row_of(cell_ref, span, across):
    return cell_ref[1:2, span] * across + cell_ref[0:1, span] * CA + cell_ref[2:3, span]


def one_hot(rows, index):
    one, zero = jnp.bfloat16(1), jnp.bfloat16(0)
    return jnp.where(rows == index.astype(jnp.int16), one, zero)


def mass_of(count_ref, volume_ref, first, span):
    volume = volume_ref[0:1, span]
    slot = lax.broadcasted_iota(jnp.int32, volume.shape, 1) + first
    return jnp.where(slot < count_ref[0], volume, 0.0)


def deposit_kernel(quads, chunk, place_ref, count_ref, *refs):
    sources, outs = refs[:4], refs[4:6]
    cell_ref, weight_ref, volume_ref, velocity_ref, sems = refs[6:]
    copies = [
        pltpu.make_async_copy(source, target, sems.at[index])
        for index, (source, target) in enumerate(
            zip(sources, (cell_ref, weight_ref, volume_ref, velocity_ref))
        )
    ]
    for copy in copies:
        copy.start()
    across = quads * CA
    rows = CH * across
    grains = weight_ref.shape[1]
    own = CB // quads
    row_iota = short_iota((rows, chunk))
    col_iota = short_iota((CB, chunk))
    total = jnp.zeros((4 * CB, rows), jnp.float32)
    for copy in copies:
        copy.wait()
    for first in range(0, grains, chunk):
        span = pl.ds(first, chunk)
        mass = mass_of(count_ref, volume_ref, first, span)
        moment = mass * velocity_ref[0:1, span]
        lower = weight_ref[0:1, span]
        upper = 1.0 - lower
        hot = one_hot(row_iota, row_of(cell_ref, span, across))
        col = cell_ref[3:4, span]
        at_lower = col_iota == col.astype(jnp.int16)
        at_upper = col_iota == (col + 1).astype(jnp.int16)
        parts = []
        for amount in (mass, moment):
            for low, high in zip(halves(amount * lower), halves(amount * upper)):
                parts.append(jnp.where(at_lower, low, jnp.where(at_upper, high, jnp.bfloat16(0))))
        spread = jnp.concatenate(parts, axis=0)
        total = total + lax.dot_general(
            spread, hot, (((1,), (1,)), ((), ())), preferred_element_type=jnp.float32
        )
    lane = lanes_of((CH, across, LANES))
    fields = [
        (total[base : base + CB] + total[base + CB : base + 2 * CB]).T
        for base in range(0, 4 * CB, 2 * CB)
    ]
    for step in range(quads):
        target = place_ref[0] ^ step
        windows = []
        for field in fields:
            moved = pltpu.roll(field, lax.rem(CB - target * own, CB), 1)
            moved = moved.reshape(CH, across, CB)
            near, past = moved[:, :, :LANES], moved[:, :, CB - LANES :]
            windows.append(jnp.where(lane < (LANES + own) // 2, near, past))
        outs[step % 2][step // 2] = pack(windows, reach(0), own)


def coefficient_kernel(quads, place_ref, kept_ref, got_ref, *refs):
    outs, solid_ref = refs[:-1], refs[-1]
    across, own = quads * CA, CB // quads
    total = kept_ref[0] + got_ref[0]
    solid_ref[...] = total[: solid_ref.shape[0]]
    solid, moment = unpack(total, 2, across, reach(0), own)
    lane = lanes_of(solid.shape)
    column = jnp.where(lane < (LANES + own) // 2, lane, lane - LANES) + place_ref[0] * own
    inside = (column >= 0) & (column < CB)
    voidage = 1.0 / (1.0 + solid)
    scale = 1.0 / (6.0 * voidage + damping)
    offset = jnp.where(inside, source_gain * moment * scale, 0.0)
    gain = jnp.where(inside, voidage * scale, 0.0)
    for distance, out in enumerate(outs):
        out[...] = pack((offset, gain), reach(distance + 1), own)


def sweep_over(sweeps, layers, across, old, new, offset_ref, gain_ref):
    row = lax.broadcasted_iota(jnp.int32, (across, LANES), 0)
    for sweep in range(1, sweeps + 1):
        for layer in range(sweep, layers - sweep):
            centre = old[layer]
            total = old[layer - 1] + old[layer + 1]
            total = total + turned(centre, 1) + turned(centre, -1)
            total = total + jnp.where(row == 0, 0.0, pltpu.roll(centre, 1, 0))
            total = total + jnp.where(row == across - 1, 0.0, pltpu.roll(centre, across - 1, 0))
            new[layer] = offset_ref[layer] + gain_ref[layer] * total
        old, new = new, old
    return old


def slot_of(slab, distance, matching):
    upward = lax.rem(lax.div(slab, distance), 2) ^ matching
    return distance * (1 - 2 * upward)


def swap_plan(depth):
    return [(distance, matching) for distance in range(1, depth + 1) for matching in range(2)]


def framed(last, first, own):
    inner = pack([last[first : first + CH]], SUBLANES, own)
    outer = [pack_own(last[layer : layer + 1], own)[0] for layer in (first - 1, first + CH)]
    return jnp.concatenate([inner] + outer, axis=0)


def relax_kernel(quads, slab_ref, own_ref, *refs):
    *parts, out_ref, offset_ref, gain_ref, even_ref, odd_ref = refs
    across, own = quads * CA, CB // quads
    layers = CH * (1 + len(parts))
    plan = [(DEPTH, own_ref, 1)] + [
        (DEPTH + slot_of(slab_ref[0], distance, matching), part, distance)
        for part, (distance, matching) in zip(parts, swap_plan(DEPTH))
    ]
    for slot, part, distance in plan:
        span = pl.ds(slot * CH, CH)
        offset, gain = unpack(part[...], 2, across, reach(distance), own)
        offset_ref[span] = offset
        even_ref[span] = offset
        gain_ref[span] = gain
    sweeps = min(FIRST, ITERS) - 1
    last = sweep_over(sweeps, layers, across, even_ref, odd_ref, offset_ref, gain_ref)
    if FIRST < ITERS:
        out_ref[...] = pack([last[DEPTH * CH : (DEPTH + 1) * CH]], SUBLANES, own)
    else:
        out_ref[...] = framed(last, DEPTH * CH, own)


def finish_kernel(quads, slab_ref, offset_ref, gain_ref, *refs):
    *parts, out_ref, even_ref, odd_ref = refs
    across, own = quads * CA, CB // quads
    slots = [1] + [1 + slot_of(slab_ref[0], *swap) for swap in swap_plan(1)]
    for slot, pressure in zip(slots, parts):
        (even_ref[pl.ds(slot * CH, CH)],) = unpack(pressure[...], 1, across, SUBLANES, own)
    near = pl.ds((DEPTH - 1) * CH, 3 * CH)
    last = sweep_over(
        ITERS - FIRST,
        3 * CH,
        across,
        even_ref,
        odd_ref,
        offset_ref.at[near],
        gain_ref.at[near],
    )
    out_ref[...] = framed(last, CH, own)


def halving(quads):
    return [1 << bit for bit in reversed(range(quads.bit_length() - 1))]


def place_offsets(quads):
    offsets = [0]
    for bit in halving(quads):
        offsets += [offset ^ bit for offset in offsets]
    return offsets


def whole_table(quads, place_ref, parts, gathered):
    own = CB // quads
    pieces = LANES // own
    for offset, part in zip(place_offsets(quads), parts):
        gathered[place_ref[0] ^ offset] = part
    lane = lanes_of(gathered.shape[1:])
    bands = []
    for piece in range(pieces):
        columns = []
        for first in range(0, quads, pieces):
            block = None
            for near in range(pieces):
                part = turned(gathered[first + near], (near - piece) * own)
                block = part if block is None else jnp.where(lane < near * own, block, part)
            columns.append(block)
        bands.append(jnp.concatenate(columns, axis=2))
    return jnp.concatenate(bands, axis=1)


def blend_of(col_iota, at, lower):
    return jnp.where(col_iota == at, lower, jnp.where(col_iota == at + 1, 1.0 - lower, 0.0))


def picked_by(pieces, hot):
    twice = jnp.concatenate([hot, hot], axis=0)
    return jnp.dot(pieces, twice, preferred_element_type=jnp.float32)


def blended(picked, blend, field):
    size = blend.shape[0]
    return jnp.sum(picked[field * size : (field + 1) * size] * blend, axis=0, keepdims=True)


def solid_table(value, across, own):
    window = unpack_own(value.reshape(CH, across * own // LANES, LANES), own)
    return jnp.concatenate(halves(window.reshape(CH * across, LANES).T[:own]), axis=1)


def velocity_table(value, across, own):
    tall = across * own // LANES
    count = packed_rows(across, 1, SUBLANES, own)
    (inner,) = unpack(value[:count], 1, across, SUBLANES, own)
    outer = unpack_own(value[count:].reshape(2, tall, LANES), own)
    row = lax.broadcasted_iota(jnp.int32, inner.shape, 1)
    above = jnp.concatenate([inner[1:], outer[1:]], axis=0)
    below = jnp.concatenate([outer[:1], inner[:-1]], axis=0)
    after = jnp.where(row == across - 1, 0.0, pltpu.roll(inner, across - 1, 1))
    before = jnp.where(row == 0, 0.0, pltpu.roll(inner, 1, 1))
    fields = (
        -0.5 * (above - below),
        -0.5 * (after - before),
        -0.5 * (turned(inner, -1) - turned(inner, 1)),
    )
    columns = [field.reshape(CH * across, LANES).T[:own] for field in fields]
    return jnp.concatenate(halves(jnp.concatenate(columns, axis=0)), axis=1)


def chunk_sums(quads, place_ref, table, offsets, fields, cell_ref, weight_ref, row_iota, span):
    across, own = quads * CA, CB // quads
    hot = one_hot(row_iota, row_of(cell_ref, span, across))
    lower = weight_ref[0:1, span]
    picked = picked_by(table, hot)
    col_iota = lax.broadcasted_iota(jnp.int32, (own, picked.shape[1]), 0)
    sums = [0.0] * fields
    for index, offset in enumerate(offsets):
        at = cell_ref[3:4, span] - (place_ref[0] ^ offset) * own
        blend = blend_of(col_iota, at, lower)
        for field in range(fields):
            sums[field] += blended(picked, blend, fields * index + field)
    return sums


def store_sums(chunk, table, offsets, fields, quads, place_ref, cell_ref, weight_ref, earlier, out_ref):
    row_iota = short_iota((CH * quads * CA, chunk))
    for first in range(0, weight_ref.shape[1], chunk):
        span = pl.ds(first, chunk)
        sums = chunk_sums(
            quads, place_ref, table, offsets, fields, cell_ref, weight_ref, row_iota, span
        )
        for field, value in enumerate(sums):
            one = pl.ds(field, 1)
            for partial in earlier:
                value = value + partial[one, span]
            out_ref[one, span] = value


def solid_kernel(quads, chunk, place_ref, cell_ref, weight_ref, held_ref, out_ref):
    across, own = quads * CA, CB // quads
    half = quads // 2
    tables = [solid_table(held_ref[index], across, own) for index in range(half)]
    store_sums(
        chunk,
        jnp.concatenate(tables, axis=0),
        place_offsets(quads)[:half],
        1,
        quads,
        place_ref,
        cell_ref,
        weight_ref,
        [],
        out_ref,
    )


def sampled_kernel(quads, chunk, offset, index, place_ref, cell_ref, weight_ref, held_ref, *refs):
    *earlier, out_ref = refs
    table = velocity_table(held_ref[index], quads * CA, CB // quads)
    store_sums(
        chunk, table, [offset], 3, quads, place_ref, cell_ref, weight_ref, earlier, out_ref
    )


def drag_kernel(quads, chunk, place_ref, count_ref, cell_ref, weight_ref, volume_ref, *refs):
    velocity_ref, solid_ref, sampled_ref, held_ref, got_ref = refs[:5]
    pressure_ref, drag_ref, gathered = refs[5:]
    across, own = quads * CA, CB // quads
    half = quads // 2
    frame = held_ref.shape[1]
    tables = []
    for index in range(half):
        got = got_ref[index]
        tables += [velocity_table(got[:frame], across, own), solid_table(got[frame:], across, own)]
    table = jnp.concatenate(tables, axis=0)
    row_iota = short_iota((CH * across, chunk))
    for first in range(0, weight_ref.shape[1], chunk):
        span = pl.ds(first, chunk)
        *sums, solid = chunk_sums(
            quads,
            place_ref,
            table,
            place_offsets(quads)[half:],
            4,
            cell_ref,
            weight_ref,
            row_iota,
            span,
        )
        factor = mass_of(count_ref, volume_ref, first, span)
        factor = factor * (1.0 + (solid + solid_ref[0:1, span])) ** 2
        for component, value in enumerate(sums):
            one = pl.ds(component, 1)
            drag_ref[one, span] = factor * (
                value + sampled_ref[one, span] - velocity_ref[one, span]
            )
    shape = gathered.shape[1:]
    count = CH * shape[1]
    parts = [
        ref[index][:count].reshape(shape) for ref in (held_ref, got_ref) for index in range(half)
    ]
    pressure = whole_table(quads, place_ref, parts, gathered)
    mine = pltpu.roll(pressure, lax.rem(across - place_ref[0] * CA, across), 1)
    pressure_ref[...] = mine[:, :CA]


def body(grain_cell, grain_count, grain_weight, grain_volume, grain_velocity):
    quads = lax.axis_size("quad")
    slabs = lax.axis_size("slab")
    grains = grain_weight.shape[0]
    across = quads * CA
    own = CB // quads
    tall = across * own // LANES
    place = lax.axis_index("quad").astype(jnp.int32).reshape(1)
    level = lax.axis_index("slab").astype(jnp.int32).reshape(1)
    weight = grain_weight.reshape(1, grains)
    volume = grain_volume.reshape(1, grains)

    grain_chunk = min(grains, 512)

    def cells(*shape):
        return jax.ShapeDtypeStruct(shape, jnp.float32)

    def over_quad(step, value):
        pairs = [(index, index ^ step) for index in range(quads)]
        return lax.ppermute(value, "quad", pairs)

    def swapped(distance, matching, value):
        lower = [
            index
            for index in range(slabs - distance)
            if (index // distance) % 2 == matching
        ]
        pairs = [(index, index + distance) for index in lower]
        return lax.ppermute(value, "slab", pairs + [(high, low) for low, high in pairs])

    *early, last = halving(quads)

    def nearly_all(value):
        held = value[None]
        for bit in early:
            held = jnp.concatenate([held, over_quad(bit, held)], axis=0)
        return held

    def pinned(value):
        return pltpu.with_memory_space_constraint(value, pltpu.HBM)

    kept, sent = pl.pallas_call(
        functools.partial(deposit_kernel, quads, min(grains, 2048)),
        out_shape=[cells(quads // 2, packed_rows(across, 2, reach(0), own), LANES)] * 2,
        in_specs=[SMEM, SMEM] + [HBM] * 4,
        out_specs=[VMEM] * 2,
        scratch_shapes=[
            pltpu.VMEM((4, grains), jnp.int32),
            pltpu.VMEM((1, grains), jnp.float32),
            pltpu.VMEM((1, grains), jnp.float32),
            pltpu.VMEM((3, grains), jnp.float32),
            pltpu.SemaphoreType.DMA((4,)),
        ],
        compiler_params=LIMIT,
        name="deposit",
    )(
        place,
        grain_count,
        pinned(grain_cell),
        pinned(weight),
        pinned(volume),
        pinned(grain_velocity),
    )

    bit = 1
    got = over_quad(bit, sent)
    while kept.shape[0] > 1:
        bit *= 2
        total = kept + got
        kept, sent = total[0::2], total[1::2]
        got = over_quad(bit, sent)
    *coefs, solid = pl.pallas_call(
        functools.partial(coefficient_kernel, quads),
        out_shape=[
            cells(packed_rows(across, 2, reach(distance), own), LANES)
            for distance in range(1, DEPTH + 1)
        ]
        + [cells(CH * tall, LANES)],
        in_specs=[SMEM] + [VMEM] * 2,
        out_specs=[VMEM] * (DEPTH + 1),
        compiler_params=LIMIT,
        name="coefficients",
    )(place, kept, got)

    stack = [coefs[0]] + [
        swapped(distance, matching, coefs[distance - 1])
        for distance, matching in swap_plan(DEPTH)
    ]
    stack[-1], solid = lax.optimization_barrier((stack[-1], solid))
    solids = nearly_all(solid)
    frame = cells(packed_rows(across, 1, SUBLANES, own) + 2 * tall, LANES)
    layers = CH * len(stack)
    two_rounds = FIRST < ITERS
    window = cells(layers, across, LANES)
    centre, offset, gain = pl.pallas_call(
        functools.partial(relax_kernel, quads),
        out_shape=[
            cells(packed_rows(across, 1, SUBLANES, own), LANES) if two_rounds else frame,
            window,
            window,
        ],
        in_specs=[SMEM] + [VMEM] * len(stack),
        out_specs=[VMEM] * 3,
        scratch_shapes=[pltpu.VMEM(window.shape, window.dtype)] * 2,
        compiler_params=LIMIT,
        name="relax",
    )(level, *stack)
    centre, solids = lax.optimization_barrier((centre, solids))
    solid_sampled = pl.pallas_call(
        functools.partial(solid_kernel, quads, grain_chunk),
        out_shape=cells(1, grains),
        in_specs=[SMEM] + [VMEM] * 3,
        out_specs=VMEM,
        compiler_params=LIMIT,
        cost_estimate=pl.CostEstimate(
            flops=8 * own * CH * across * grains, bytes_accessed=2**20, transcendentals=0
        ),
        name="solid",
    )(place, grain_cell, weight, solids)

    mine = centre
    if two_rounds:
        pressures = [centre] + [swapped(*swap, centre) for swap in swap_plan(1)]
        pressures, solid_sampled = lax.optimization_barrier((pressures, solid_sampled))
        mine = pl.pallas_call(
            functools.partial(finish_kernel, quads),
            out_shape=frame,
            in_specs=[SMEM] + [VMEM] * 5,
            out_specs=VMEM,
            scratch_shapes=[pltpu.VMEM((3 * CH, across, LANES), jnp.float32)] * 2,
            compiler_params=LIMIT,
            name="finish",
        )(level, offset, gain, *pressures)

    def sampled_from(held, index, *earlier):
        return pl.pallas_call(
            functools.partial(
                sampled_kernel, quads, grain_chunk, place_offsets(quads)[index], index
            ),
            out_shape=cells(3, grains),
            in_specs=[SMEM] + [VMEM] * (3 + len(earlier)),
            out_specs=VMEM,
            compiler_params=LIMIT,
            cost_estimate=pl.CostEstimate(
                flops=12 * own * CH * across * grains, bytes_accessed=2**20, transcendentals=0
            ),
            name="sampled",
        )(place, grain_cell, weight, held, *earlier)

    held = mine[None]
    partial = sampled_from(held, 0)
    for bit in early:
        known = held.shape[0]
        held = jnp.concatenate([held, over_quad(bit, held)], axis=0)
        held, partial = lax.optimization_barrier((held, partial))
        for index in range(known, held.shape[0]):
            partial = sampled_from(held, index, partial)
    got = over_quad(last, jnp.concatenate([held, solids], axis=1))
    pressure, drag = pl.pallas_call(
        functools.partial(drag_kernel, quads, grain_chunk),
        out_shape=[cells(CH, CA, CB), cells(3, grains)],
        in_specs=[SMEM] * 2 + [VMEM] * 8,
        out_specs=[VMEM] * 2,
        scratch_shapes=[pltpu.VMEM((quads, CH, tall, LANES), jnp.float32)],
        compiler_params=LIMIT,
        name="drag",
    )(
        place,
        grain_count,
        grain_cell,
        weight,
        volume,
        grain_velocity,
        solid_sampled,
        partial,
        held,
        got,
    )
    return pressure, drag


def solution(mesh):
    placed = (
        P(None, ("slab", "quad")),
        P(("slab", "quad")),
        P(("slab", "quad")),
        P(("slab", "quad")),
        P(None, ("slab", "quad")),
    )
    return jax.shard_map(
        body,
        mesh=mesh,
        in_specs=placed,
        out_specs=(P("slab", "quad", None), P(None, ("slab", "quad"))),
        check_vma=False,
    )
```

```python
import functools

import jax
import jax.numpy as jnp
from jax import lax
from jax.experimental import pallas as pl
from jax.experimental.pallas import tpu as pltpu
from jax.sharding import PartitionSpec as P

CH = 4
CA = 16
CB = 256
ITERS = 12
LANES = 128
SUBLANES = 8
DEPTH = 3

damping = 0.05
source_gain = 4.0

VMEM = pl.BlockSpec(memory_space=pltpu.VMEM)
SMEM = pl.BlockSpec(memory_space=pltpu.SMEM)
HBM = pl.BlockSpec(memory_space=pltpu.HBM)
LIMIT = pltpu.CompilerParams(vmem_limit_bytes=48 * 1024 * 1024)


def reach(distance):
    needed = ITERS - 1 - CH * (max(distance, 1) - 1)
    return 1 << (needed - 1).bit_length()


def lanes_of(shape):
    return lax.broadcasted_iota(jnp.int32, shape, len(shape) - 1)


def turned(value, shift):
    shift %= LANES
    return pltpu.roll(value, shift, value.ndim - 1) if shift else value


def pack_own(window, own):
    pieces = LANES // own
    tall = window.shape[1] // pieces
    lane = lanes_of((window.shape[0], tall, LANES))
    result = window[:, :tall]
    for piece in range(1, pieces):
        part = turned(window[:, piece * tall : (piece + 1) * tall], piece * own)
        result = jnp.where(lane < piece * own, result, part)
    return result


def unpack_own(packed, own):
    pieces = LANES // own
    return jnp.concatenate([turned(packed, -piece * own) for piece in range(pieces)], axis=1)


def strip_plan(across, fields, halo):
    rows = across * 2 * halo // LANES
    return (1, rows) if rows >= SUBLANES else (fields, rows * fields)


def packed_rows(across, fields, halo, own):
    shared, rows = strip_plan(across, fields, halo)
    return fields * CH * across * own // LANES + (fields // shared) * CH * rows


def pack(windows, halo, own):
    across = windows[0].shape[1]
    shared, rows = strip_plan(across, len(windows), halo)
    pieces = [pack_own(window, own) for window in windows]
    lane = lanes_of(windows[0].shape)
    joined = [
        jnp.where(lane >= LANES - halo, window, turned(window, LANES - 2 * halo - own))
        for window in windows
    ]
    lane = lanes_of((CH, rows, LANES))
    for first in range(0, len(windows), shared):
        strip, at = None, 0
        for value in joined[first : first + shared]:
            for row in range(0, across, rows):
                part = turned(value[:, row : row + rows], at + 2 * halo)
                strip = part if strip is None else jnp.where(lane < at, strip, part)
                at += 2 * halo
        pieces.append(strip)
    return jnp.concatenate([piece.reshape(-1, LANES) for piece in pieces], axis=0)


def unpack(value, fields, across, halo, own):
    shared, rows = strip_plan(across, fields, halo)
    tall = across * own // LANES
    count = fields * CH * tall
    owned = value[:count].reshape(fields, CH, tall, LANES)
    strips = value[count:].reshape(fields // shared, CH, rows, LANES)
    lane = lanes_of((CH, rows, LANES))
    windows = []
    for field in range(fields):
        window = unpack_own(owned[field], own)
        strip = strips[field // shared]
        at = (field % shared) * across // rows * 2 * halo
        blocks = []
        for row in range(0, across, rows):
            right = turned(strip, own - at)
            left = turned(strip, -2 * halo - at)
            block = jnp.where(lane < own + halo, right, 0.0)
            block = jnp.where(lane >= LANES - halo, left, block)
            blocks.append(jnp.where(lane < own, window[:, row : row + rows], block))
            at += 2 * halo
        windows.append(jnp.concatenate(blocks, axis=1))
    return windows


def halves(value):
    high = value.astype(jnp.bfloat16)
    low = (value - high.astype(jnp.float32)).astype(jnp.bfloat16)
    return high, low


def short_iota(shape):
    return lax.broadcasted_iota(jnp.int32, shape, 0).astype(jnp.int16)


def row_of(cell_ref, span, across):
    return cell_ref[1:2, span] * across + cell_ref[0:1, span] * CA + cell_ref[2:3, span]


def one_hot(rows, index):
    one, zero = jnp.bfloat16(1), jnp.bfloat16(0)
    return jnp.where(rows == index.astype(jnp.int16), one, zero)


def mass_of(count_ref, volume_ref, first, span):
    volume = volume_ref[0:1, span]
    slot = lax.broadcasted_iota(jnp.int32, volume.shape, 1) + first
    return jnp.where(slot < count_ref[0], volume, 0.0)


def deposit_kernel(quads, chunk, place_ref, count_ref, *refs):
    sources, outs = refs[:4], refs[4:6]
    cell_ref, weight_ref, volume_ref, velocity_ref, sems = refs[6:]
    copies = [
        pltpu.make_async_copy(source, target, sems.at[index])
        for index, (source, target) in enumerate(
            zip(sources, (cell_ref, weight_ref, volume_ref, velocity_ref))
        )
    ]
    for copy in copies:
        copy.start()
    across = quads * CA
    rows = CH * across
    grains = weight_ref.shape[1]
    own = CB // quads
    row_iota = short_iota((rows, chunk))
    col_iota = short_iota((CB, chunk))
    total = jnp.zeros((4 * CB, rows), jnp.float32)
    for copy in copies:
        copy.wait()
    for first in range(0, grains, chunk):
        span = pl.ds(first, chunk)
        mass = mass_of(count_ref, volume_ref, first, span)
        moment = mass * velocity_ref[0:1, span]
        lower = weight_ref[0:1, span]
        upper = 1.0 - lower
        hot = one_hot(row_iota, row_of(cell_ref, span, across))
        col = cell_ref[3:4, span]
        at_lower = col_iota == col.astype(jnp.int16)
        at_upper = col_iota == (col + 1).astype(jnp.int16)
        parts = []
        for amount in (mass, moment):
            for low, high in zip(halves(amount * lower), halves(amount * upper)):
                parts.append(jnp.where(at_lower, low, jnp.where(at_upper, high, jnp.bfloat16(0))))
        spread = jnp.concatenate(parts, axis=0)
        total = total + lax.dot_general(
            spread, hot, (((1,), (1,)), ((), ())), preferred_element_type=jnp.float32
        )
    lane = lanes_of((CH, across, LANES))
    fields = [
        (total[base : base + CB] + total[base + CB : base + 2 * CB]).T
        for base in range(0, 4 * CB, 2 * CB)
    ]
    for step in range(quads):
        target = place_ref[0] ^ step
        windows = []
        for field in fields:
            moved = pltpu.roll(field, lax.rem(CB - target * own, CB), 1)
            moved = moved.reshape(CH, across, CB)
            near, past = moved[:, :, :LANES], moved[:, :, CB - LANES :]
            windows.append(jnp.where(lane < (LANES + own) // 2, near, past))
        outs[step % 2][step // 2] = pack(windows, reach(0), own)


def coefficient_kernel(quads, place_ref, kept_ref, got_ref, *refs):
    outs, solid_ref = refs[:-1], refs[-1]
    across, own = quads * CA, CB // quads
    total = kept_ref[0] + got_ref[0]
    solid_ref[...] = total[: solid_ref.shape[0]]
    solid, moment = unpack(total, 2, across, reach(0), own)
    lane = lanes_of(solid.shape)
    column = jnp.where(lane < (LANES + own) // 2, lane, lane - LANES) + place_ref[0] * own
    inside = (column >= 0) & (column < CB)
    voidage = 1.0 / (1.0 + solid)
    scale = 1.0 / (6.0 * voidage + damping)
    offset = jnp.where(inside, source_gain * moment * scale, 0.0)
    gain = jnp.where(inside, voidage * scale, 0.0)
    for distance, out in enumerate(outs):
        out[...] = pack((offset, gain), reach(distance + 1), own)


def sweep_over(sweeps, layers, across, old, new, offset_ref, gain_ref):
    row = lax.broadcasted_iota(jnp.int32, (across, LANES), 0)
    for sweep in range(1, sweeps + 1):
        for layer in range(sweep, layers - sweep):
            centre = old[layer]
            total = old[layer - 1] + old[layer + 1]
            total = total + turned(centre, 1) + turned(centre, -1)
            total = total + jnp.where(row == 0, 0.0, pltpu.roll(centre, 1, 0))
            total = total + jnp.where(row == across - 1, 0.0, pltpu.roll(centre, across - 1, 0))
            new[layer] = offset_ref[layer] + gain_ref[layer] * total
        old, new = new, old
    return old


def slot_of(slab, distance, matching):
    upward = lax.rem(lax.div(slab, distance), 2) ^ matching
    return distance * (1 - 2 * upward)


def swap_plan(depth):
    return [(distance, matching) for distance in range(1, depth + 1) for matching in range(2)]


def framed(last, first, own):
    inner = pack([last[first : first + CH]], SUBLANES, own)
    outer = [pack_own(last[layer : layer + 1], own)[0] for layer in (first - 1, first + CH)]
    return jnp.concatenate([inner] + outer, axis=0)


def relax_kernel(quads, slab_ref, own_ref, *refs):
    *parts, out_ref, offset_ref, gain_ref, even_ref, odd_ref = refs
    across, own = quads * CA, CB // quads
    layers = CH * (1 + len(parts))
    plan = [(DEPTH, own_ref, 1)] + [
        (DEPTH + slot_of(slab_ref[0], distance, matching), part, distance)
        for part, (distance, matching) in zip(parts, swap_plan(DEPTH))
    ]
    for slot, part, distance in plan:
        span = pl.ds(slot * CH, CH)
        offset, gain = unpack(part[...], 2, across, reach(distance), own)
        offset_ref[span] = offset
        even_ref[span] = offset
        gain_ref[span] = gain
    last = sweep_over(ITERS - 1, layers, across, even_ref, odd_ref, offset_ref, gain_ref)
    out_ref[...] = framed(last, DEPTH * CH, own)


def halving(quads):
    return [1 << bit for bit in reversed(range(quads.bit_length() - 1))]


def place_offsets(quads):
    offsets = [0]
    for bit in halving(quads):
        offsets += [offset ^ bit for offset in offsets]
    return offsets


def whole_table(quads, place_ref, parts, gathered):
    own = CB // quads
    pieces = LANES // own
    for offset, part in zip(place_offsets(quads), parts):
        gathered[place_ref[0] ^ offset] = part
    lane = lanes_of(gathered.shape[1:])
    bands = []
    for piece in range(pieces):
        columns = []
        for first in range(0, quads, pieces):
            block = None
            for near in range(pieces):
                part = turned(gathered[first + near], (near - piece) * own)
                block = part if block is None else jnp.where(lane < near * own, block, part)
            columns.append(block)
        bands.append(jnp.concatenate(columns, axis=2))
    return jnp.concatenate(bands, axis=1)


def blend_of(col_iota, at, lower):
    return jnp.where(col_iota == at, lower, jnp.where(col_iota == at + 1, 1.0 - lower, 0.0))


def picked_by(pieces, hot):
    twice = jnp.concatenate([hot, hot], axis=0)
    return jnp.dot(pieces, twice, preferred_element_type=jnp.float32)


def blended(picked, blend, field):
    size = blend.shape[0]
    return jnp.sum(picked[field * size : (field + 1) * size] * blend, axis=0, keepdims=True)


def solid_table(value, across, own):
    window = unpack_own(value.reshape(CH, across * own // LANES, LANES), own)
    return jnp.concatenate(halves(window.reshape(CH * across, LANES).T[:own]), axis=1)


def velocity_table(value, across, own):
    tall = across * own // LANES
    count = packed_rows(across, 1, SUBLANES, own)
    (inner,) = unpack(value[:count], 1, across, SUBLANES, own)
    outer = unpack_own(value[count:].reshape(2, tall, LANES), own)
    row = lax.broadcasted_iota(jnp.int32, inner.shape, 1)
    above = jnp.concatenate([inner[1:], outer[1:]], axis=0)
    below = jnp.concatenate([outer[:1], inner[:-1]], axis=0)
    after = jnp.where(row == across - 1, 0.0, pltpu.roll(inner, across - 1, 1))
    before = jnp.where(row == 0, 0.0, pltpu.roll(inner, 1, 1))
    fields = (
        -0.5 * (above - below),
        -0.5 * (after - before),
        -0.5 * (turned(inner, -1) - turned(inner, 1)),
    )
    columns = [field.reshape(CH * across, LANES).T[:own] for field in fields]
    return jnp.concatenate(halves(jnp.concatenate(columns, axis=0)), axis=1)


def chunk_sums(quads, place_ref, table, offsets, fields, cell_ref, weight_ref, row_iota, span):
    across, own = quads * CA, CB // quads
    hot = one_hot(row_iota, row_of(cell_ref, span, across))
    lower = weight_ref[0:1, span]
    picked = picked_by(table, hot)
    col_iota = lax.broadcasted_iota(jnp.int32, (own, picked.shape[1]), 0)
    sums = [0.0] * fields
    for index, offset in enumerate(offsets):
        at = cell_ref[3:4, span] - (place_ref[0] ^ offset) * own
        blend = blend_of(col_iota, at, lower)
        for field in range(fields):
            sums[field] += blended(picked, blend, fields * index + field)
    return sums


def store_sums(chunk, table, offsets, fields, quads, place_ref, cell_ref, weight_ref, earlier, out_ref):
    row_iota = short_iota((CH * quads * CA, chunk))
    for first in range(0, weight_ref.shape[1], chunk):
        span = pl.ds(first, chunk)
        sums = chunk_sums(
            quads, place_ref, table, offsets, fields, cell_ref, weight_ref, row_iota, span
        )
        for field, value in enumerate(sums):
            one = pl.ds(field, 1)
            for partial in earlier:
                value = value + partial[one, span]
            out_ref[one, span] = value


def solid_kernel(quads, chunk, place_ref, cell_ref, weight_ref, held_ref, out_ref):
    across, own = quads * CA, CB // quads
    half = quads // 2
    tables = [solid_table(held_ref[index], across, own) for index in range(half)]
    store_sums(
        chunk,
        jnp.concatenate(tables, axis=0),
        place_offsets(quads)[:half],
        1,
        quads,
        place_ref,
        cell_ref,
        weight_ref,
        [],
        out_ref,
    )


def sampled_kernel(quads, chunk, offset, index, place_ref, cell_ref, weight_ref, held_ref, *refs):
    *earlier, out_ref = refs
    table = velocity_table(held_ref[index], quads * CA, CB // quads)
    store_sums(
        chunk, table, [offset], 3, quads, place_ref, cell_ref, weight_ref, earlier, out_ref
    )


def drag_kernel(quads, chunk, place_ref, count_ref, cell_ref, weight_ref, volume_ref, *refs):
    velocity_ref, solid_ref, sampled_ref, held_ref, got_ref = refs[:5]
    pressure_ref, drag_ref, gathered = refs[5:]
    across, own = quads * CA, CB // quads
    half = quads // 2
    frame = held_ref.shape[1]
    tables = []
    for index in range(half):
        got = got_ref[index]
        tables += [velocity_table(got[:frame], across, own), solid_table(got[frame:], across, own)]
    table = jnp.concatenate(tables, axis=0)
    row_iota = short_iota((CH * across, chunk))
    for first in range(0, weight_ref.shape[1], chunk):
        span = pl.ds(first, chunk)
        *sums, solid = chunk_sums(
            quads,
            place_ref,
            table,
            place_offsets(quads)[half:],
            4,
            cell_ref,
            weight_ref,
            row_iota,
            span,
        )
        factor = mass_of(count_ref, volume_ref, first, span)
        factor = factor * (1.0 + (solid + solid_ref[0:1, span])) ** 2
        for component, value in enumerate(sums):
            one = pl.ds(component, 1)
            drag_ref[one, span] = factor * (
                value + sampled_ref[one, span] - velocity_ref[one, span]
            )
    shape = gathered.shape[1:]
    count = CH * shape[1]
    parts = [
        ref[index][:count].reshape(shape) for ref in (held_ref, got_ref) for index in range(half)
    ]
    pressure = whole_table(quads, place_ref, parts, gathered)
    mine = pltpu.roll(pressure, lax.rem(across - place_ref[0] * CA, across), 1)
    pressure_ref[...] = mine[:, :CA]


def body(grain_cell, grain_count, grain_weight, grain_volume, grain_velocity):
    quads = lax.axis_size("quad")
    slabs = lax.axis_size("slab")
    grains = grain_weight.shape[0]
    across = quads * CA
    own = CB // quads
    tall = across * own // LANES
    place = lax.axis_index("quad").astype(jnp.int32).reshape(1)
    level = lax.axis_index("slab").astype(jnp.int32).reshape(1)
    weight = grain_weight.reshape(1, grains)
    volume = grain_volume.reshape(1, grains)

    grain_chunk = min(grains, 512)

    def cells(*shape):
        return jax.ShapeDtypeStruct(shape, jnp.float32)

    def over_quad(step, value):
        pairs = [(index, index ^ step) for index in range(quads)]
        return lax.ppermute(value, "quad", pairs)

    def swapped(distance, matching, value):
        lower = [
            index
            for index in range(slabs - distance)
            if (index // distance) % 2 == matching
        ]
        pairs = [(index, index + distance) for index in lower]
        return lax.ppermute(value, "slab", pairs + [(high, low) for low, high in pairs])

    *early, last = halving(quads)

    def nearly_all(value):
        held = value[None]
        for bit in early:
            held = jnp.concatenate([held, over_quad(bit, held)], axis=0)
        return held

    def pinned(value):
        return pltpu.with_memory_space_constraint(value, pltpu.HBM)

    kept, sent = pl.pallas_call(
        functools.partial(deposit_kernel, quads, min(grains, 2048)),
        out_shape=[cells(quads // 2, packed_rows(across, 2, reach(0), own), LANES)] * 2,
        in_specs=[SMEM, SMEM] + [HBM] * 4,
        out_specs=[VMEM] * 2,
        scratch_shapes=[
            pltpu.VMEM((4, grains), jnp.int32),
            pltpu.VMEM((1, grains), jnp.float32),
            pltpu.VMEM((1, grains), jnp.float32),
            pltpu.VMEM((3, grains), jnp.float32),
            pltpu.SemaphoreType.DMA((4,)),
        ],
        compiler_params=LIMIT,
        name="deposit",
    )(
        place,
        grain_count,
        pinned(grain_cell),
        pinned(weight),
        pinned(volume),
        pinned(grain_velocity),
    )

    bit = 1
    got = over_quad(bit, sent)
    while kept.shape[0] > 1:
        bit *= 2
        total = kept + got
        kept, sent = total[0::2], total[1::2]
        got = over_quad(bit, sent)
    *coefs, solid = pl.pallas_call(
        functools.partial(coefficient_kernel, quads),
        out_shape=[
            cells(packed_rows(across, 2, reach(distance), own), LANES)
            for distance in range(1, DEPTH + 1)
        ]
        + [cells(CH * tall, LANES)],
        in_specs=[SMEM] + [VMEM] * 2,
        out_specs=[VMEM] * (DEPTH + 1),
        compiler_params=LIMIT,
        name="coefficients",
    )(place, kept, got)

    stack = [coefs[0]] + [
        swapped(distance, matching, coefs[distance - 1])
        for distance, matching in swap_plan(DEPTH)
    ]
    solids = nearly_all(solid)
    solid_sampled = pl.pallas_call(
        functools.partial(solid_kernel, quads, grain_chunk),
        out_shape=cells(1, grains),
        in_specs=[SMEM] + [VMEM] * 3,
        out_specs=VMEM,
        compiler_params=LIMIT,
        cost_estimate=pl.CostEstimate(
            flops=8 * own * CH * across * grains, bytes_accessed=2**20, transcendentals=0
        ),
        name="solid",
    )(place, grain_cell, weight, solids)
    stack, solid_sampled = lax.optimization_barrier((stack, solid_sampled))

    window = pltpu.VMEM((CH * len(stack), across, LANES), jnp.float32)
    mine = pl.pallas_call(
        functools.partial(relax_kernel, quads),
        out_shape=cells(packed_rows(across, 1, SUBLANES, own) + 2 * tall, LANES),
        in_specs=[SMEM] + [VMEM] * len(stack),
        out_specs=VMEM,
        scratch_shapes=[window] * 4,
        compiler_params=LIMIT,
        name="relax",
    )(level, *stack)

    def sampled_from(held, index, *earlier):
        return pl.pallas_call(
            functools.partial(
                sampled_kernel, quads, grain_chunk, place_offsets(quads)[index], index
            ),
            out_shape=cells(3, grains),
            in_specs=[SMEM] + [VMEM] * (3 + len(earlier)),
            out_specs=VMEM,
            compiler_params=LIMIT,
            cost_estimate=pl.CostEstimate(
                flops=12 * own * CH * across * grains, bytes_accessed=2**20, transcendentals=0
            ),
            name="sampled",
        )(place, grain_cell, weight, held, *earlier)

    held = mine[None]
    partial = sampled_from(held, 0)
    for bit in early:
        known = held.shape[0]
        held = jnp.concatenate([held, over_quad(bit, held)], axis=0)
        held, partial = lax.optimization_barrier((held, partial))
        for index in range(known, held.shape[0]):
            partial = sampled_from(held, index, partial)
    got = over_quad(last, jnp.concatenate([held, solids], axis=1))
    pressure, drag = pl.pallas_call(
        functools.partial(drag_kernel, quads, grain_chunk),
        out_shape=[cells(CH, CA, CB), cells(3, grains)],
        in_specs=[SMEM] * 2 + [VMEM] * 8,
        out_specs=[VMEM] * 2,
        scratch_shapes=[pltpu.VMEM((quads, CH, tall, LANES), jnp.float32)],
        compiler_params=LIMIT,
        name="drag",
    )(
        place,
        grain_count,
        grain_cell,
        weight,
        volume,
        grain_velocity,
        solid_sampled,
        partial,
        held,
        got,
    )
    return pressure, drag


def solution(mesh):
    placed = (
        P(None, ("slab", "quad")),
        P(("slab", "quad")),
        P(("slab", "quad")),
        P(("slab", "quad")),
        P(None, ("slab", "quad")),
    )
    return jax.shard_map(
        body,
        mesh=mesh,
        in_specs=placed,
        out_specs=(P("slab", "quad", None), P(None, ("slab", "quad"))),
        check_vma=False,
    )
```

```python
import functools

import jax
import jax.numpy as jnp
from jax import lax
from jax.experimental import pallas as pl
from jax.experimental.pallas import tpu as pltpu
from jax.sharding import PartitionSpec as P

CH = 4
CA = 16
CB = 256
ITERS = 12
LANES = 128
SUBLANES = 8
DEPTH = 2
FIRST = CH * DEPTH + 1

damping = 0.05
source_gain = 4.0

VMEM = pl.BlockSpec(memory_space=pltpu.VMEM)
SMEM = pl.BlockSpec(memory_space=pltpu.SMEM)
HBM = pl.BlockSpec(memory_space=pltpu.HBM)
LIMIT = pltpu.CompilerParams(vmem_limit_bytes=48 * 1024 * 1024)


def reach(distance):
    needed = ITERS - 1 - CH * (max(distance, 1) - 1)
    return 1 << (needed - 1).bit_length()


def lanes_of(shape):
    return lax.broadcasted_iota(jnp.int32, shape, len(shape) - 1)


def turned(value, shift):
    shift %= LANES
    return pltpu.roll(value, shift, value.ndim - 1) if shift else value


def pack_own(window, own):
    pieces = LANES // own
    tall = window.shape[1] // pieces
    lane = lanes_of((window.shape[0], tall, LANES))
    result = window[:, :tall]
    for piece in range(1, pieces):
        part = turned(window[:, piece * tall : (piece + 1) * tall], piece * own)
        result = jnp.where(lane < piece * own, result, part)
    return result


def unpack_own(packed, own):
    pieces = LANES // own
    return jnp.concatenate([turned(packed, -piece * own) for piece in range(pieces)], axis=1)


def strip_plan(across, fields, halo):
    rows = across * 2 * halo // LANES
    return (1, rows) if rows >= SUBLANES else (fields, rows * fields)


def packed_rows(across, fields, halo, own):
    shared, rows = strip_plan(across, fields, halo)
    return fields * CH * across * own // LANES + (fields // shared) * CH * rows


def pack(windows, halo, own):
    across = windows[0].shape[1]
    shared, rows = strip_plan(across, len(windows), halo)
    pieces = [pack_own(window, own) for window in windows]
    lane = lanes_of(windows[0].shape)
    joined = [
        jnp.where(lane >= LANES - halo, window, turned(window, LANES - 2 * halo - own))
        for window in windows
    ]
    lane = lanes_of((CH, rows, LANES))
    for first in range(0, len(windows), shared):
        strip, at = None, 0
        for value in joined[first : first + shared]:
            for row in range(0, across, rows):
                part = turned(value[:, row : row + rows], at + 2 * halo)
                strip = part if strip is None else jnp.where(lane < at, strip, part)
                at += 2 * halo
        pieces.append(strip)
    return jnp.concatenate([piece.reshape(-1, LANES) for piece in pieces], axis=0)


def unpack(value, fields, across, halo, own):
    shared, rows = strip_plan(across, fields, halo)
    tall = across * own // LANES
    count = fields * CH * tall
    owned = value[:count].reshape(fields, CH, tall, LANES)
    strips = value[count:].reshape(fields // shared, CH, rows, LANES)
    lane = lanes_of((CH, rows, LANES))
    windows = []
    for field in range(fields):
        window = unpack_own(owned[field], own)
        strip = strips[field // shared]
        at = (field % shared) * across // rows * 2 * halo
        blocks = []
        for row in range(0, across, rows):
            right = turned(strip, own - at)
            left = turned(strip, -2 * halo - at)
            block = jnp.where(lane < own + halo, right, 0.0)
            block = jnp.where(lane >= LANES - halo, left, block)
            blocks.append(jnp.where(lane < own, window[:, row : row + rows], block))
            at += 2 * halo
        windows.append(jnp.concatenate(blocks, axis=1))
    return windows


def halves(value):
    high = value.astype(jnp.bfloat16)
    low = (value - high.astype(jnp.float32)).astype(jnp.bfloat16)
    return high, low


def short_iota(shape):
    return lax.broadcasted_iota(jnp.int32, shape, 0).astype(jnp.int16)


def row_of(cell_ref, span, across):
    return cell_ref[1:2, span] * across + cell_ref[0:1, span] * CA + cell_ref[2:3, span]


def one_hot(rows, index):
    one, zero = jnp.bfloat16(1), jnp.bfloat16(0)
    return jnp.where(rows == index.astype(jnp.int16), one, zero)


def mass_of(count_ref, volume_ref, first, span):
    volume = volume_ref[0:1, span]
    slot = lax.broadcasted_iota(jnp.int32, volume.shape, 1) + first
    return jnp.where(slot < count_ref[0], volume, 0.0)


def grain_kernel(quads, count_ref, *refs):
    sources, out_ref, targets, sems = refs[:4], refs[4], refs[5:9], refs[9]
    copies = [
        pltpu.make_async_copy(source, target, sems.at[index])
        for index, (source, target) in enumerate(zip(sources, targets))
    ]
    for copy in copies:
        copy.start()
    for copy in copies:
        copy.wait()
    cell_ref, weight_ref, volume_ref, velocity_ref = targets
    span = pl.ds(0, weight_ref.shape[1])
    mass = mass_of(count_ref, volume_ref, 0, span)
    flat = row_of(cell_ref, span, quads * CA) * CB + cell_ref[3:4, span]
    out_ref[0:1, :] = flat.astype(jnp.float32)
    out_ref[1:2, :] = weight_ref[...]
    out_ref[2:3, :] = mass
    out_ref[3:4, :] = mass * velocity_ref[0:1, span]


def deposit_into(total, quads, chunk, place_ref, grain_ref):
    own = CB // quads
    halo = reach(0)
    rows = CH * quads * CA
    size = own + 2 * halo
    row_iota = short_iota((rows, chunk))
    iota = lax.broadcasted_iota(jnp.int32, (size, chunk), 0)
    col_iota = jnp.where(iota < own + halo, iota, iota - size).astype(jnp.int16)
    for first in range(0, grain_ref.shape[1], chunk):
        span = pl.ds(first, chunk)
        flat = grain_ref[0:1, span]
        row = jnp.floor(flat * (1.0 / CB))
        col = (flat - row * CB).astype(jnp.int32) - place_ref[0] * own
        lower = grain_ref[1:2, span]
        upper = 1.0 - lower
        hot = one_hot(row_iota, row.astype(jnp.int32))
        at_lower = col_iota == col.astype(jnp.int16)
        at_upper = col_iota == (col + 1).astype(jnp.int16)
        parts = []
        for amount in (grain_ref[2:3, span], grain_ref[3:4, span]):
            for low, high in zip(halves(amount * lower), halves(amount * upper)):
                parts.append(jnp.where(at_lower, low, jnp.where(at_upper, high, jnp.bfloat16(0))))
        product = lax.dot_general(
            jnp.concatenate(parts, axis=0),
            hot,
            (((1,), (1,)), ((), ())),
            preferred_element_type=jnp.float32,
        )
        total = product if total is None else total + product
    return total


def deposit_kernel(quads, chunk, place_ref, grain_ref, *refs):
    *earlier, out_ref = refs
    total = earlier[0][...] if earlier else None
    out_ref[...] = deposit_into(total, quads, chunk, place_ref, grain_ref)


def coefficient_kernel(quads, chunk, place_ref, *refs):
    half = quads // 2
    grains, total_ref, outs, solid_ref = refs[:half], refs[half], refs[half + 1 : -1], refs[-1]
    across, own = quads * CA, CB // quads
    total = total_ref[...]
    for grain_ref in grains:
        total = deposit_into(total, quads, chunk, place_ref, grain_ref)
    halo = reach(0)
    size = own + 2 * halo
    windows = []
    for base in range(0, 4 * size, 2 * size):
        field = total[base : base + size] + total[base + size : base + 2 * size]
        gap = jnp.zeros((LANES - size, field.shape[1]), jnp.float32)
        field = jnp.concatenate([field[: own + halo], gap, field[own + halo :]], axis=0)
        windows.append(field.T.reshape(CH, across, LANES))
    solid, moment = windows
    solid_ref[...] = pack_own(solid, own).reshape(solid_ref.shape)
    lane = lanes_of(solid.shape)
    column = jnp.where(lane < (LANES + own) // 2, lane, lane - LANES) + place_ref[0] * own
    inside = (column >= 0) & (column < CB)
    voidage = 1.0 / (1.0 + solid)
    scale = 1.0 / (6.0 * voidage + damping)
    offset = jnp.where(inside, source_gain * moment * scale, 0.0)
    gain = jnp.where(inside, voidage * scale, 0.0)
    for distance, out in enumerate(outs):
        out[...] = pack((offset, gain), reach(distance + 1), own)


def sweep_over(sweeps, layers, across, old, new, offset_ref, gain_ref):
    row = lax.broadcasted_iota(jnp.int32, (across, LANES), 0)
    for sweep in range(1, sweeps + 1):
        for layer in range(sweep, layers - sweep):
            centre = old[layer]
            total = old[layer - 1] + old[layer + 1]
            total = total + turned(centre, 1) + turned(centre, -1)
            total = total + jnp.where(row == 0, 0.0, pltpu.roll(centre, 1, 0))
            total = total + jnp.where(row == across - 1, 0.0, pltpu.roll(centre, across - 1, 0))
            new[layer] = offset_ref[layer] + gain_ref[layer] * total
        old, new = new, old
    return old


def slot_of(slab, distance, matching):
    upward = lax.rem(lax.div(slab, distance), 2) ^ matching
    return distance * (1 - 2 * upward)


def swap_plan(depth):
    return [(distance, matching) for distance in range(1, depth + 1) for matching in range(2)]


def framed(last, first, own):
    inner = pack([last[first : first + CH]], SUBLANES, own)
    outer = [pack_own(last[layer : layer + 1], own)[0] for layer in (first - 1, first + CH)]
    return jnp.concatenate([inner] + outer, axis=0)


def relax_kernel(quads, slab_ref, own_ref, *refs):
    *parts, out_ref, offset_ref, gain_ref, even_ref, odd_ref = refs
    across, own = quads * CA, CB // quads
    layers = CH * (1 + len(parts))
    plan = [(DEPTH, own_ref, 1)] + [
        (DEPTH + slot_of(slab_ref[0], distance, matching), part, distance)
        for part, (distance, matching) in zip(parts, swap_plan(DEPTH))
    ]
    for slot, part, distance in plan:
        span = pl.ds(slot * CH, CH)
        offset, gain = unpack(part[...], 2, across, reach(distance), own)
        offset_ref[span] = offset
        even_ref[span] = offset
        gain_ref[span] = gain
    sweeps = min(FIRST, ITERS) - 1
    last = sweep_over(sweeps, layers, across, even_ref, odd_ref, offset_ref, gain_ref)
    if FIRST < ITERS:
        out_ref[...] = pack([last[DEPTH * CH : (DEPTH + 1) * CH]], SUBLANES, own)
    else:
        out_ref[...] = framed(last, DEPTH * CH, own)


def finish_kernel(quads, slab_ref, offset_ref, gain_ref, *refs):
    *parts, out_ref, even_ref, odd_ref = refs
    across, own = quads * CA, CB // quads
    slots = [1] + [1 + slot_of(slab_ref[0], *swap) for swap in swap_plan(1)]
    for slot, pressure in zip(slots, parts):
        (even_ref[pl.ds(slot * CH, CH)],) = unpack(pressure[...], 1, across, SUBLANES, own)
    near = pl.ds((DEPTH - 1) * CH, 3 * CH)
    last = sweep_over(
        ITERS - FIRST,
        3 * CH,
        across,
        even_ref,
        odd_ref,
        offset_ref.at[near],
        gain_ref.at[near],
    )
    out_ref[...] = framed(last, CH, own)


def halving(quads):
    return [1 << bit for bit in reversed(range(quads.bit_length() - 1))]


def place_offsets(quads):
    offsets = [0]
    for bit in halving(quads):
        offsets += [offset ^ bit for offset in offsets]
    return offsets


def blend_of(col_iota, at, lower):
    return jnp.where(col_iota == at, lower, jnp.where(col_iota == at + 1, 1.0 - lower, 0.0))


def picked_by(pieces, hot):
    twice = jnp.concatenate([hot, hot], axis=0)
    return jnp.dot(pieces, twice, preferred_element_type=jnp.float32)


def blended(picked, blend, field):
    size = blend.shape[0]
    return jnp.sum(picked[field * size : (field + 1) * size] * blend, axis=0, keepdims=True)


def solid_table(value, across, own):
    window = unpack_own(value.reshape(CH, across * own // LANES, LANES), own)
    return jnp.concatenate(halves(window.reshape(CH * across, LANES).T[:own]), axis=1)


def velocity_table(value, across, own):
    tall = across * own // LANES
    count = packed_rows(across, 1, SUBLANES, own)
    (inner,) = unpack(value[:count], 1, across, SUBLANES, own)
    outer = unpack_own(value[count:].reshape(2, tall, LANES), own)
    row = lax.broadcasted_iota(jnp.int32, inner.shape, 1)
    above = jnp.concatenate([inner[1:], outer[1:]], axis=0)
    below = jnp.concatenate([outer[:1], inner[:-1]], axis=0)
    after = jnp.where(row == across - 1, 0.0, pltpu.roll(inner, across - 1, 1))
    before = jnp.where(row == 0, 0.0, pltpu.roll(inner, 1, 1))
    fields = (
        -0.5 * (above - below),
        -0.5 * (after - before),
        -0.5 * (turned(inner, -1) - turned(inner, 1)),
    )
    columns = [field.reshape(CH * across, LANES).T[:own] for field in fields]
    return jnp.concatenate(halves(jnp.concatenate(columns, axis=0)), axis=1)


def chunk_sums(quads, place_ref, table, offsets, fields, cell_ref, weight_ref, row_iota, span):
    across, own = quads * CA, CB // quads
    hot = one_hot(row_iota, row_of(cell_ref, span, across))
    lower = weight_ref[0:1, span]
    picked = picked_by(table, hot)
    col_iota = lax.broadcasted_iota(jnp.int32, (own, picked.shape[1]), 0)
    sums = [0.0] * fields
    for index, offset in enumerate(offsets):
        at = cell_ref[3:4, span] - (place_ref[0] ^ offset) * own
        blend = blend_of(col_iota, at, lower)
        for field in range(fields):
            sums[field] += blended(picked, blend, fields * index + field)
    return sums


def store_sums(chunk, table, offsets, fields, quads, place_ref, cell_ref, weight_ref, earlier, out_ref):
    row_iota = short_iota((CH * quads * CA, chunk))
    for first in range(0, weight_ref.shape[1], chunk):
        span = pl.ds(first, chunk)
        sums = chunk_sums(
            quads, place_ref, table, offsets, fields, cell_ref, weight_ref, row_iota, span
        )
        for field, value in enumerate(sums):
            one = pl.ds(field, 1)
            for partial in earlier:
                value = value + partial[one, span]
            out_ref[one, span] = value


def solid_kernel(quads, chunk, place_ref, cell_ref, weight_ref, held_ref, out_ref):
    across, own = quads * CA, CB // quads
    half = quads // 2
    tables = [solid_table(held_ref[index], across, own) for index in range(half)]
    store_sums(
        chunk,
        jnp.concatenate(tables, axis=0),
        place_offsets(quads)[:half],
        1,
        quads,
        place_ref,
        cell_ref,
        weight_ref,
        [],
        out_ref,
    )


def sampled_kernel(quads, chunk, offset, index, place_ref, cell_ref, weight_ref, held_ref, *refs):
    *earlier, out_ref = refs
    table = velocity_table(held_ref[index], quads * CA, CB // quads)
    store_sums(
        chunk, table, [offset], 3, quads, place_ref, cell_ref, weight_ref, earlier, out_ref
    )


def drag_kernel(quads, chunk, place_ref, count_ref, cell_ref, weight_ref, volume_ref, *refs):
    velocity_ref, solid_ref, sampled_ref, held_ref, got_ref = refs[:5]
    pressure_ref, drag_ref, gathered = refs[5:]
    across, own = quads * CA, CB // quads
    half = quads // 2
    frame = held_ref.shape[1]
    tables = []
    for index in range(half):
        got = got_ref[index]
        tables += [velocity_table(got[:frame], across, own), solid_table(got[frame:], across, own)]
    table = jnp.concatenate(tables, axis=0)
    row_iota = short_iota((CH * across, chunk))
    for first in range(0, weight_ref.shape[1], chunk):
        span = pl.ds(first, chunk)
        *sums, solid = chunk_sums(
            quads,
            place_ref,
            table,
            place_offsets(quads)[half:],
            4,
            cell_ref,
            weight_ref,
            row_iota,
            span,
        )
        factor = mass_of(count_ref, volume_ref, first, span)
        factor = factor * (1.0 + (solid + solid_ref[0:1, span])) ** 2
        for component, value in enumerate(sums):
            one = pl.ds(component, 1)
            drag_ref[one, span] = factor * (
                value + sampled_ref[one, span] - velocity_ref[one, span]
            )
    shape = gathered.shape[1:]
    count = CH * shape[1]
    parts = [
        ref[index][:count].reshape(shape) for ref in (held_ref, got_ref) for index in range(half)
    ]
    for offset, part in zip(place_offsets(quads), parts):
        gathered[place_ref[0] ^ offset] = part
    bands = shape[1] // CA
    band = pl.ds(pl.multiple_of(lax.rem(place_ref[0], bands) * CA, SUBLANES), CA)
    back = lax.rem(LANES - lax.div(place_ref[0], bands) * own, LANES)
    lane = lanes_of((CH, CA, LANES))
    pieces = LANES // own
    for first in range(0, quads, pieces):
        block = None
        for near in range(pieces):
            part = pltpu.roll(gathered[first + near, :, band, :], lax.rem(back + near * own, LANES), 2)
            block = part if block is None else jnp.where(lane < near * own, block, part)
        pressure_ref[:, :, first * own : first * own + LANES] = block


def body(grain_cell, grain_count, grain_weight, grain_volume, grain_velocity):
    quads = lax.axis_size("quad")
    slabs = lax.axis_size("slab")
    grains = grain_weight.shape[0]
    across = quads * CA
    own = CB // quads
    tall = across * own // LANES
    place = lax.axis_index("quad").astype(jnp.int32).reshape(1)
    level = lax.axis_index("slab").astype(jnp.int32).reshape(1)
    weight = grain_weight.reshape(1, grains)
    volume = grain_volume.reshape(1, grains)

    grain_chunk = min(grains, 512)

    def cells(*shape):
        return jax.ShapeDtypeStruct(shape, jnp.float32)

    def over_quad(step, value):
        pairs = [(index, index ^ step) for index in range(quads)]
        return lax.ppermute(value, "quad", pairs)

    def swapped(distance, matching, value):
        lower = [
            index
            for index in range(slabs - distance)
            if (index // distance) % 2 == matching
        ]
        pairs = [(index, index + distance) for index in lower]
        return lax.ppermute(value, "slab", pairs + [(high, low) for low, high in pairs])

    *early, last = halving(quads)

    def nearly_all(value):
        held = value[None]
        for bit in early:
            held = jnp.concatenate([held, over_quad(bit, held)], axis=0)
        return held

    def pinned(value):
        return pltpu.with_memory_space_constraint(value, pltpu.HBM)

    packed_grains = pl.pallas_call(
        functools.partial(grain_kernel, quads),
        out_shape=cells(4, grains),
        in_specs=[SMEM] + [HBM] * 4,
        out_specs=VMEM,
        scratch_shapes=[
            pltpu.VMEM((4, grains), jnp.int32),
            pltpu.VMEM((1, grains), jnp.float32),
            pltpu.VMEM((1, grains), jnp.float32),
            pltpu.VMEM((3, grains), jnp.float32),
            pltpu.SemaphoreType.DMA((4,)),
        ],
        compiler_params=LIMIT,
        name="grains",
    )(
        grain_count,
        pinned(grain_cell),
        pinned(weight),
        pinned(volume),
        pinned(grain_velocity),
    )
    half = quads // 2
    others = [over_quad(step, packed_grains) for step in reversed(range(1, quads))][::-1]
    size = own + 2 * reach(0)
    deposit_chunk = min(grains, 2048)
    total = None
    for arrived in [packed_grains] + others[: half - 1]:
        earlier = [] if total is None else [total]
        total = pl.pallas_call(
            functools.partial(deposit_kernel, quads, deposit_chunk),
            out_shape=cells(4 * size, CH * across),
            in_specs=[SMEM] + [VMEM] * (1 + len(earlier)),
            out_specs=VMEM,
            compiler_params=LIMIT,
            cost_estimate=pl.CostEstimate(
                flops=8 * size * CH * across * grains, bytes_accessed=2**20, transcendentals=0
            ),
            name="deposit",
        )(place, arrived, *earlier)
    *coefs, solid = pl.pallas_call(
        functools.partial(coefficient_kernel, quads, deposit_chunk),
        out_shape=[
            cells(packed_rows(across, 2, reach(distance), own), LANES)
            for distance in range(1, DEPTH + 1)
        ]
        + [cells(CH * tall, LANES)],
        in_specs=[SMEM] + [VMEM] * (half + 1),
        out_specs=[VMEM] * (DEPTH + 1),
        compiler_params=LIMIT,
        name="coefficients",
    )(place, *others[half - 1 :], total)

    stack = [coefs[0]] + [
        swapped(distance, matching, coefs[distance - 1])
        for distance, matching in swap_plan(DEPTH)
    ]
    stack[-1], solid = lax.optimization_barrier((stack[-1], solid))
    solids = nearly_all(solid)
    frame = cells(packed_rows(across, 1, SUBLANES, own) + 2 * tall, LANES)
    layers = CH * len(stack)
    two_rounds = FIRST < ITERS
    window = cells(layers, across, LANES)
    centre, offset, gain = pl.pallas_call(
        functools.partial(relax_kernel, quads),
        out_shape=[
            cells(packed_rows(across, 1, SUBLANES, own), LANES) if two_rounds else frame,
            window,
            window,
        ],
        in_specs=[SMEM] + [VMEM] * len(stack),
        out_specs=[VMEM] * 3,
        scratch_shapes=[pltpu.VMEM(window.shape, window.dtype)] * 2,
        compiler_params=LIMIT,
        name="relax",
    )(level, *stack)
    centre, solids = lax.optimization_barrier((centre, solids))
    solid_sampled = pl.pallas_call(
        functools.partial(solid_kernel, quads, grain_chunk),
        out_shape=cells(1, grains),
        in_specs=[SMEM] + [VMEM] * 3,
        out_specs=VMEM,
        compiler_params=LIMIT,
        cost_estimate=pl.CostEstimate(
            flops=8 * own * CH * across * grains, bytes_accessed=2**20, transcendentals=0
        ),
        name="solid",
    )(place, grain_cell, weight, solids)

    mine = centre
    if two_rounds:
        pressures = [centre] + [swapped(*swap, centre) for swap in swap_plan(1)]
        pressures, solid_sampled = lax.optimization_barrier((pressures, solid_sampled))
        mine = pl.pallas_call(
            functools.partial(finish_kernel, quads),
            out_shape=frame,
            in_specs=[SMEM] + [VMEM] * 5,
            out_specs=VMEM,
            scratch_shapes=[pltpu.VMEM((3 * CH, across, LANES), jnp.float32)] * 2,
            compiler_params=LIMIT,
            name="finish",
        )(level, offset, gain, *pressures)

    def sampled_from(held, index, *earlier):
        return pl.pallas_call(
            functools.partial(
                sampled_kernel, quads, grain_chunk, place_offsets(quads)[index], index
            ),
            out_shape=cells(3, grains),
            in_specs=[SMEM] + [VMEM] * (3 + len(earlier)),
            out_specs=VMEM,
            compiler_params=LIMIT,
            cost_estimate=pl.CostEstimate(
                flops=12 * own * CH * across * grains, bytes_accessed=2**20, transcendentals=0
            ),
            name="sampled",
        )(place, grain_cell, weight, held, *earlier)

    held = mine[None]
    partial = sampled_from(held, 0)
    for bit in early:
        known = held.shape[0]
        held = jnp.concatenate([held, over_quad(bit, held)], axis=0)
        held, partial = lax.optimization_barrier((held, partial))
        for index in range(known, held.shape[0]):
            partial = sampled_from(held, index, partial)
    got = over_quad(last, jnp.concatenate([held, solids], axis=1))
    pressure, drag = pl.pallas_call(
        functools.partial(drag_kernel, quads, grain_chunk),
        out_shape=[cells(CH, CA, CB), cells(3, grains)],
        in_specs=[SMEM] * 2 + [VMEM] * 8,
        out_specs=[VMEM] * 2,
        scratch_shapes=[pltpu.VMEM((quads, CH, tall, LANES), jnp.float32)],
        compiler_params=LIMIT,
        name="drag",
    )(
        place,
        grain_count,
        grain_cell,
        weight,
        volume,
        grain_velocity,
        solid_sampled,
        partial,
        held,
        got,
    )
    return pressure, drag


def solution(mesh):
    placed = (
        P(None, ("slab", "quad")),
        P(("slab", "quad")),
        P(("slab", "quad")),
        P(("slab", "quad")),
        P(None, ("slab", "quad")),
    )
    return jax.shard_map(
        body,
        mesh=mesh,
        in_specs=placed,
        out_specs=(P("slab", "quad", None), P(None, ("slab", "quad"))),
        check_vma=False,
    )
```

```python
import functools

import jax
import jax.numpy as jnp
from jax import lax
from jax.experimental import pallas as pl
from jax.experimental.pallas import tpu as pltpu
from jax.sharding import PartitionSpec as P

CH = 4
CA = 16
CB = 256
ITERS = 12
LANES = 128
SUBLANES = 8
DEPTH = 2
FIRST = CH * DEPTH + 1

damping = 0.05
source_gain = 4.0

VMEM = pl.BlockSpec(memory_space=pltpu.VMEM)
SMEM = pl.BlockSpec(memory_space=pltpu.SMEM)
HBM = pl.BlockSpec(memory_space=pltpu.HBM)
LIMIT = pltpu.CompilerParams(vmem_limit_bytes=48 * 1024 * 1024)


def reach(distance):
    needed = ITERS - 1 - CH * (max(distance, 1) - 1)
    return 1 << (needed - 1).bit_length()


def lanes_of(shape):
    return lax.broadcasted_iota(jnp.int32, shape, len(shape) - 1)


def turned(value, shift):
    shift %= LANES
    return pltpu.roll(value, shift, value.ndim - 1) if shift else value


def pack_own(window, own):
    pieces = LANES // own
    tall = window.shape[1] // pieces
    lane = lanes_of((window.shape[0], tall, LANES))
    result = window[:, :tall]
    for piece in range(1, pieces):
        part = turned(window[:, piece * tall : (piece + 1) * tall], piece * own)
        result = jnp.where(lane < piece * own, result, part)
    return result


def unpack_own(packed, own):
    pieces = LANES // own
    return jnp.concatenate([turned(packed, -piece * own) for piece in range(pieces)], axis=1)


def strip_plan(across, fields, halo):
    rows = across * 2 * halo // LANES
    return (1, rows) if rows >= SUBLANES else (fields, rows * fields)


def packed_rows(across, fields, halo, own):
    shared, rows = strip_plan(across, fields, halo)
    return fields * CH * across * own // LANES + (fields // shared) * CH * rows


def pack(windows, halo, own):
    across = windows[0].shape[1]
    shared, rows = strip_plan(across, len(windows), halo)
    pieces = [pack_own(window, own) for window in windows]
    lane = lanes_of(windows[0].shape)
    joined = [
        jnp.where(lane >= LANES - halo, window, turned(window, LANES - 2 * halo - own))
        for window in windows
    ]
    lane = lanes_of((CH, rows, LANES))
    for first in range(0, len(windows), shared):
        strip, at = None, 0
        for value in joined[first : first + shared]:
            for row in range(0, across, rows):
                part = turned(value[:, row : row + rows], at + 2 * halo)
                strip = part if strip is None else jnp.where(lane < at, strip, part)
                at += 2 * halo
        pieces.append(strip)
    return jnp.concatenate([piece.reshape(-1, LANES) for piece in pieces], axis=0)


def unpack(value, fields, across, halo, own):
    shared, rows = strip_plan(across, fields, halo)
    tall = across * own // LANES
    count = fields * CH * tall
    owned = value[:count].reshape(fields, CH, tall, LANES)
    strips = value[count:].reshape(fields // shared, CH, rows, LANES)
    lane = lanes_of((CH, rows, LANES))
    windows = []
    for field in range(fields):
        window = unpack_own(owned[field], own)
        strip = strips[field // shared]
        at = (field % shared) * across // rows * 2 * halo
        blocks = []
        for row in range(0, across, rows):
            right = turned(strip, own - at)
            left = turned(strip, -2 * halo - at)
            block = jnp.where(lane < own + halo, right, 0.0)
            block = jnp.where(lane >= LANES - halo, left, block)
            blocks.append(jnp.where(lane < own, window[:, row : row + rows], block))
            at += 2 * halo
        windows.append(jnp.concatenate(blocks, axis=1))
    return windows


def halves(value):
    high = value.astype(jnp.bfloat16)
    low = (value - high.astype(jnp.float32)).astype(jnp.bfloat16)
    return high, low


def short_iota(shape):
    return lax.broadcasted_iota(jnp.int32, shape, 0).astype(jnp.int16)


def row_of(cell_ref, span, across):
    return cell_ref[1:2, span] * across + cell_ref[0:1, span] * CA + cell_ref[2:3, span]


def one_hot(rows, index):
    one, zero = jnp.bfloat16(1), jnp.bfloat16(0)
    return jnp.where(rows == index.astype(jnp.int16), one, zero)


def mass_of(count_ref, volume_ref, first, span):
    volume = volume_ref[0:1, span]
    slot = lax.broadcasted_iota(jnp.int32, volume.shape, 1) + first
    return jnp.where(slot < count_ref[0], volume, 0.0)


def grain_kernel(quads, count_ref, *refs):
    sources, out_ref, targets, sems = refs[:4], refs[4], refs[5:9], refs[9]
    copies = [
        pltpu.make_async_copy(source, target, sems.at[index])
        for index, (source, target) in enumerate(zip(sources, targets))
    ]
    for copy in copies:
        copy.start()
    for copy in copies:
        copy.wait()
    cell_ref, weight_ref, volume_ref, velocity_ref = targets
    span = pl.ds(0, weight_ref.shape[1])
    mass = mass_of(count_ref, volume_ref, 0, span)
    flat = row_of(cell_ref, span, quads * CA) * CB + cell_ref[3:4, span]
    out_ref[0:1, :] = flat.astype(jnp.float32)
    out_ref[1:2, :] = weight_ref[...]
    out_ref[2:3, :] = mass
    out_ref[3:4, :] = mass * velocity_ref[0:1, span]


def deposit_into(total, quads, chunk, place_ref, grain_ref):
    own = CB // quads
    halo = reach(0)
    rows = CH * quads * CA
    size = own + 2 * halo
    row_iota = short_iota((rows, chunk))
    iota = lax.broadcasted_iota(jnp.int32, (size, chunk), 0)
    col_iota = jnp.where(iota < own + halo, iota, iota - size).astype(jnp.int16)
    for first in range(0, grain_ref.shape[1], chunk):
        span = pl.ds(first, chunk)
        flat = grain_ref[0:1, span]
        row = jnp.floor(flat * (1.0 / CB))
        col = (flat - row * CB).astype(jnp.int32) - place_ref[0] * own
        lower = grain_ref[1:2, span]
        upper = 1.0 - lower
        hot = one_hot(row_iota, row.astype(jnp.int32))
        at_lower = col_iota == col.astype(jnp.int16)
        at_upper = col_iota == (col + 1).astype(jnp.int16)
        parts = []
        for amount in (grain_ref[2:3, span], grain_ref[3:4, span]):
            for low, high in zip(halves(amount * lower), halves(amount * upper)):
                parts.append(jnp.where(at_lower, low, jnp.where(at_upper, high, jnp.bfloat16(0))))
        product = lax.dot_general(
            jnp.concatenate(parts, axis=0),
            hot,
            (((1,), (1,)), ((), ())),
            preferred_element_type=jnp.float32,
        )
        total = product if total is None else total + product
    return total


def deposit_kernel(quads, chunk, place_ref, grain_ref, *refs):
    *earlier, out_ref = refs
    total = earlier[0][...] if earlier else None
    out_ref[...] = deposit_into(total, quads, chunk, place_ref, grain_ref)


def coefficient_kernel(quads, chunk, place_ref, *refs):
    grain_ref, total_ref, *outs, solid_ref = refs
    across, own = quads * CA, CB // quads
    total = deposit_into(total_ref[...], quads, chunk, place_ref, grain_ref)
    halo = reach(0)
    size = own + 2 * halo
    windows = []
    for base in range(0, 4 * size, 2 * size):
        field = total[base : base + size] + total[base + size : base + 2 * size]
        gap = jnp.zeros((LANES - size, field.shape[1]), jnp.float32)
        field = jnp.concatenate([field[: own + halo], gap, field[own + halo :]], axis=0)
        windows.append(field.T.reshape(CH, across, LANES))
    solid, moment = windows
    solid_ref[...] = pack_own(solid, own).reshape(solid_ref.shape)
    lane = lanes_of(solid.shape)
    column = jnp.where(lane < (LANES + own) // 2, lane, lane - LANES) + place_ref[0] * own
    inside = (column >= 0) & (column < CB)
    voidage = 1.0 / (1.0 + solid)
    scale = 1.0 / (6.0 * voidage + damping)
    offset = jnp.where(inside, source_gain * moment * scale, 0.0)
    gain = jnp.where(inside, voidage * scale, 0.0)
    for distance, out in enumerate(outs):
        out[...] = pack((offset, gain), reach(distance + 1), own)


def sweep_over(sweeps, layers, across, old, new, spare, offset_ref, gain_ref):
    row = lax.broadcasted_iota(jnp.int32, (across, LANES), 0)
    for sweep in range(1, sweeps + 1):
        for layer in range(sweep, layers - sweep):
            centre = old[layer]
            total = old[layer - 1] + old[layer + 1]
            total = total + turned(centre, 1) + turned(centre, -1)
            total = total + jnp.where(row == 0, 0.0, pltpu.roll(centre, 1, 0))
            total = total + jnp.where(row == across - 1, 0.0, pltpu.roll(centre, across - 1, 0))
            new[layer] = offset_ref[layer] + gain_ref[layer] * total
        old, new, spare = new, spare, new
    return old


def slot_of(slab, distance, matching):
    upward = lax.rem(lax.div(slab, distance), 2) ^ matching
    return distance * (1 - 2 * upward)


def swap_plan(depth):
    return [(distance, matching) for distance in range(1, depth + 1) for matching in range(2)]


def framed(last, first, own):
    inner = pack([last[first : first + CH]], SUBLANES, own)
    outer = [pack_own(last[layer : layer + 1], own)[0] for layer in (first - 1, first + CH)]
    return jnp.concatenate([inner] + outer, axis=0)


def relax_kernel(quads, slab_ref, own_ref, *refs):
    *parts, out_ref, offset_ref, gain_ref, even_ref, odd_ref = refs
    across, own = quads * CA, CB // quads
    layers = CH * (1 + len(parts))
    plan = [(DEPTH, own_ref, 1)] + [
        (DEPTH + slot_of(slab_ref[0], distance, matching), part, distance)
        for part, (distance, matching) in zip(parts, swap_plan(DEPTH))
    ]
    for slot, part, distance in plan:
        span = pl.ds(slot * CH, CH)
        offset, gain = unpack(part[...], 2, across, reach(distance), own)
        offset_ref[span] = offset
        gain_ref[span] = gain
    last = sweep_over(
        FIRST - 1, layers, across, offset_ref, even_ref, odd_ref, offset_ref, gain_ref
    )
    out_ref[...] = pack([last[DEPTH * CH : (DEPTH + 1) * CH]], SUBLANES, own)


def finish_kernel(quads, slab_ref, offset_ref, gain_ref, *refs):
    *parts, out_ref, even_ref, odd_ref = refs
    across, own = quads * CA, CB // quads
    slots = [1] + [1 + slot_of(slab_ref[0], *swap) for swap in swap_plan(1)]
    for slot, pressure in zip(slots, parts):
        (even_ref[pl.ds(slot * CH, CH)],) = unpack(pressure[...], 1, across, SUBLANES, own)
    near = pl.ds((DEPTH - 1) * CH, 3 * CH)
    last = sweep_over(
        ITERS - FIRST,
        3 * CH,
        across,
        even_ref,
        odd_ref,
        even_ref,
        offset_ref.at[near],
        gain_ref.at[near],
    )
    out_ref[...] = framed(last, CH, own)


def halving(quads):
    return [1 << bit for bit in reversed(range(quads.bit_length() - 1))]


def place_offsets(quads):
    offsets = [0]
    for bit in halving(quads):
        offsets += [offset ^ bit for offset in offsets]
    return offsets


def blend_of(col_iota, at, lower):
    return jnp.where(col_iota == at, lower, jnp.where(col_iota == at + 1, 1.0 - lower, 0.0))


def picked_by(pieces, hot):
    twice = jnp.concatenate([hot, hot], axis=0)
    return jnp.dot(pieces, twice, preferred_element_type=jnp.float32)


def blended(picked, blend, field):
    size = blend.shape[0]
    return jnp.sum(picked[field * size : (field + 1) * size] * blend, axis=0, keepdims=True)


def solid_table(value, across, own):
    window = unpack_own(value.reshape(CH, across * own // LANES, LANES), own)
    return jnp.concatenate(halves(window.reshape(CH * across, LANES).T[:own]), axis=1)


def velocity_table(value, across, own):
    tall = across * own // LANES
    count = packed_rows(across, 1, SUBLANES, own)
    (inner,) = unpack(value[:count], 1, across, SUBLANES, own)
    outer = unpack_own(value[count:].reshape(2, tall, LANES), own)
    row = lax.broadcasted_iota(jnp.int32, inner.shape, 1)
    above = jnp.concatenate([inner[1:], outer[1:]], axis=0)
    below = jnp.concatenate([outer[:1], inner[:-1]], axis=0)
    after = jnp.where(row == across - 1, 0.0, pltpu.roll(inner, across - 1, 1))
    before = jnp.where(row == 0, 0.0, pltpu.roll(inner, 1, 1))
    fields = (
        -0.5 * (above - below),
        -0.5 * (after - before),
        -0.5 * (turned(inner, -1) - turned(inner, 1)),
    )
    columns = [field.reshape(CH * across, LANES).T[:own] for field in fields]
    return jnp.concatenate(halves(jnp.concatenate(columns, axis=0)), axis=1)


def chunk_sums(quads, place_ref, table, offsets, fields, cell_ref, weight_ref, row_iota, span):
    across, own = quads * CA, CB // quads
    hot = one_hot(row_iota, row_of(cell_ref, span, across))
    lower = weight_ref[0:1, span]
    picked = picked_by(table, hot)
    col_iota = lax.broadcasted_iota(jnp.int32, (own, picked.shape[1]), 0)
    sums = [0.0] * fields
    for index, offset in enumerate(offsets):
        at = cell_ref[3:4, span] - (place_ref[0] ^ offset) * own
        blend = blend_of(col_iota, at, lower)
        for field in range(fields):
            sums[field] += blended(picked, blend, fields * index + field)
    return sums


def store_sums(chunk, table, offsets, fields, quads, place_ref, cell_ref, weight_ref, earlier, out_ref):
    row_iota = short_iota((CH * quads * CA, chunk))
    for first in range(0, weight_ref.shape[1], chunk):
        span = pl.ds(first, chunk)
        sums = chunk_sums(
            quads, place_ref, table, offsets, fields, cell_ref, weight_ref, row_iota, span
        )
        for field, value in enumerate(sums):
            one = pl.ds(field, 1)
            for partial in earlier:
                value = value + partial[one, span]
            out_ref[one, span] = value


def solid_kernel(quads, chunk, place_ref, cell_ref, weight_ref, held_ref, out_ref):
    across, own = quads * CA, CB // quads
    half = quads // 2
    tables = [solid_table(held_ref[index], across, own) for index in range(half)]
    store_sums(
        chunk,
        jnp.concatenate(tables, axis=0),
        place_offsets(quads)[:half],
        1,
        quads,
        place_ref,
        cell_ref,
        weight_ref,
        [],
        out_ref,
    )


def sampled_kernel(quads, chunk, offset, index, place_ref, cell_ref, weight_ref, held_ref, *refs):
    *earlier, out_ref = refs
    table = velocity_table(held_ref[index], quads * CA, CB // quads)
    store_sums(
        chunk, table, [offset], 3, quads, place_ref, cell_ref, weight_ref, earlier, out_ref
    )


def drag_kernel(quads, chunk, place_ref, count_ref, cell_ref, weight_ref, volume_ref, *refs):
    velocity_ref, solid_ref, sampled_ref, held_ref, got_ref = refs[:5]
    pressure_ref, drag_ref, gathered = refs[5:]
    across, own = quads * CA, CB // quads
    half = quads // 2
    frame = held_ref.shape[1]
    tables = []
    for index in range(half):
        got = got_ref[index]
        tables += [velocity_table(got[:frame], across, own), solid_table(got[frame:], across, own)]
    table = jnp.concatenate(tables, axis=0)
    row_iota = short_iota((CH * across, chunk))
    for first in range(0, weight_ref.shape[1], chunk):
        span = pl.ds(first, chunk)
        *sums, solid = chunk_sums(
            quads,
            place_ref,
            table,
            place_offsets(quads)[half:],
            4,
            cell_ref,
            weight_ref,
            row_iota,
            span,
        )
        factor = mass_of(count_ref, volume_ref, first, span)
        factor = factor * (1.0 + (solid + solid_ref[0:1, span])) ** 2
        for component, value in enumerate(sums):
            one = pl.ds(component, 1)
            drag_ref[one, span] = factor * (
                value + sampled_ref[one, span] - velocity_ref[one, span]
            )
    shape = gathered.shape[1:]
    count = CH * shape[1]
    parts = [
        ref[index][:count].reshape(shape) for ref in (held_ref, got_ref) for index in range(half)
    ]
    for offset, part in zip(place_offsets(quads), parts):
        gathered[place_ref[0] ^ offset] = part
    bands = shape[1] // CA
    band = pl.ds(pl.multiple_of(lax.rem(place_ref[0], bands) * CA, SUBLANES), CA)
    back = lax.rem(LANES - lax.div(place_ref[0], bands) * own, LANES)
    lane = lanes_of((CH, CA, LANES))
    pieces = LANES // own
    for first in range(0, quads, pieces):
        block = None
        for near in range(pieces):
            part = pltpu.roll(gathered[first + near, :, band, :], lax.rem(back + near * own, LANES), 2)
            block = part if block is None else jnp.where(lane < near * own, block, part)
        pressure_ref[:, :, first * own : first * own + LANES] = block


def body(grain_cell, grain_count, grain_weight, grain_volume, grain_velocity):
    quads = lax.axis_size("quad")
    slabs = lax.axis_size("slab")
    grains = grain_weight.shape[0]
    across = quads * CA
    own = CB // quads
    tall = across * own // LANES
    place = lax.axis_index("quad").astype(jnp.int32).reshape(1)
    level = lax.axis_index("slab").astype(jnp.int32).reshape(1)
    weight = grain_weight.reshape(1, grains)
    volume = grain_volume.reshape(1, grains)

    grain_chunk = min(grains, 512)

    def cells(*shape):
        return jax.ShapeDtypeStruct(shape, jnp.float32)

    def over_quad(step, value):
        pairs = [(index, index ^ step) for index in range(quads)]
        return lax.ppermute(value, "quad", pairs)

    def swapped(distance, matching, value):
        lower = [
            index
            for index in range(slabs - distance)
            if (index // distance) % 2 == matching
        ]
        pairs = [(index, index + distance) for index in lower]
        return lax.ppermute(value, "slab", pairs + [(high, low) for low, high in pairs])

    *early, last = halving(quads)

    def nearly_all(value):
        held = value[None]
        for bit in early:
            held = jnp.concatenate([held, over_quad(bit, held)], axis=0)
        return held

    def pinned(value):
        return pltpu.with_memory_space_constraint(value, pltpu.HBM)

    packed_grains = pl.pallas_call(
        functools.partial(grain_kernel, quads),
        out_shape=cells(4, grains),
        in_specs=[SMEM] + [HBM] * 4,
        out_specs=VMEM,
        scratch_shapes=[
            pltpu.VMEM((4, grains), jnp.int32),
            pltpu.VMEM((1, grains), jnp.float32),
            pltpu.VMEM((1, grains), jnp.float32),
            pltpu.VMEM((3, grains), jnp.float32),
            pltpu.SemaphoreType.DMA((4,)),
        ],
        compiler_params=LIMIT,
        name="grains",
    )(
        grain_count,
        pinned(grain_cell),
        pinned(weight),
        pinned(volume),
        pinned(grain_velocity),
    )
    packs = [packed_grains]
    for bit in halving(quads):
        packs += [over_quad(bit, pack) for pack in packs]
    half = quads // 2
    packs = [packs[half * (index % 2) + index // 2] for index in range(quads)]
    size = own + 2 * reach(0)
    deposit_chunk = min(grains, 2048)
    total = None
    for arrived in packs[:-1]:
        earlier = [] if total is None else [total]
        total = pl.pallas_call(
            functools.partial(deposit_kernel, quads, deposit_chunk),
            out_shape=cells(4 * size, CH * across),
            in_specs=[SMEM] + [VMEM] * (1 + len(earlier)),
            out_specs=VMEM,
            compiler_params=LIMIT,
            cost_estimate=pl.CostEstimate(
                flops=8 * size * CH * across * grains, bytes_accessed=2**20, transcendentals=0
            ),
            name="deposit",
        )(place, arrived, *earlier)
    *coefs, solid = pl.pallas_call(
        functools.partial(coefficient_kernel, quads, deposit_chunk),
        out_shape=[
            cells(packed_rows(across, 2, reach(distance), own), LANES)
            for distance in range(1, DEPTH + 1)
        ]
        + [cells(CH * tall, LANES)],
        in_specs=[SMEM] + [VMEM] * 2,
        out_specs=[VMEM] * (DEPTH + 1),
        compiler_params=LIMIT,
        name="coefficients",
    )(place, packs[-1], total)

    stack = [coefs[0]] + [
        swapped(distance, matching, coefs[distance - 1])
        for distance, matching in swap_plan(DEPTH)
    ]
    stack[-1], solid = lax.optimization_barrier((stack[-1], solid))
    solids = nearly_all(solid)
    frame = cells(packed_rows(across, 1, SUBLANES, own) + 2 * tall, LANES)
    layers = CH * len(stack)
    window = cells(layers, across, LANES)
    centre, offset, gain = pl.pallas_call(
        functools.partial(relax_kernel, quads),
        out_shape=[
            cells(packed_rows(across, 1, SUBLANES, own), LANES),
            window,
            window,
        ],
        in_specs=[SMEM] + [VMEM] * len(stack),
        out_specs=[VMEM] * 3,
        scratch_shapes=[pltpu.VMEM(window.shape, window.dtype)] * 2,
        compiler_params=LIMIT,
        name="relax",
    )(level, *stack)
    centre, solids = lax.optimization_barrier((centre, solids))
    solid_sampled = pl.pallas_call(
        functools.partial(solid_kernel, quads, grain_chunk),
        out_shape=cells(1, grains),
        in_specs=[SMEM] + [VMEM] * 3,
        out_specs=VMEM,
        compiler_params=LIMIT,
        cost_estimate=pl.CostEstimate(
            flops=8 * own * CH * across * grains, bytes_accessed=2**20, transcendentals=0
        ),
        name="solid",
    )(place, grain_cell, weight, solids)

    pressures = [centre] + [swapped(*swap, centre) for swap in swap_plan(1)]
    pressures, solid_sampled = lax.optimization_barrier((pressures, solid_sampled))
    mine = pl.pallas_call(
        functools.partial(finish_kernel, quads),
        out_shape=frame,
        in_specs=[SMEM] + [VMEM] * 5,
        out_specs=VMEM,
        scratch_shapes=[pltpu.VMEM((3 * CH, across, LANES), jnp.float32)] * 2,
        compiler_params=LIMIT,
        name="finish",
    )(level, offset, gain, *pressures)

    def sampled_from(held, index, *earlier):
        return pl.pallas_call(
            functools.partial(
                sampled_kernel, quads, grain_chunk, place_offsets(quads)[index], index
            ),
            out_shape=cells(3, grains),
            in_specs=[SMEM] + [VMEM] * (3 + len(earlier)),
            out_specs=VMEM,
            compiler_params=LIMIT,
            cost_estimate=pl.CostEstimate(
                flops=12 * own * CH * across * grains, bytes_accessed=2**20, transcendentals=0
            ),
            name="sampled",
        )(place, grain_cell, weight, held, *earlier)

    held = mine[None]
    partial = sampled_from(held, 0)
    for bit in early:
        known = held.shape[0]
        held = jnp.concatenate([held, over_quad(bit, held)], axis=0)
        held, partial = lax.optimization_barrier((held, partial))
        for index in range(known, held.shape[0]):
            partial = sampled_from(held, index, partial)
    got = over_quad(last, jnp.concatenate([held, solids], axis=1))
    pressure, drag = pl.pallas_call(
        functools.partial(drag_kernel, quads, grain_chunk),
        out_shape=[cells(CH, CA, CB), cells(3, grains)],
        in_specs=[SMEM] * 2 + [VMEM] * 8,
        out_specs=[VMEM] * 2,
        scratch_shapes=[pltpu.VMEM((quads, CH, tall, LANES), jnp.float32)],
        compiler_params=LIMIT,
        name="drag",
    )(
        place,
        grain_count,
        grain_cell,
        weight,
        volume,
        grain_velocity,
        solid_sampled,
        partial,
        held,
        got,
    )
    return pressure, drag


def solution(mesh):
    placed = (
        P(None, ("slab", "quad")),
        P(("slab", "quad")),
        P(("slab", "quad")),
        P(("slab", "quad")),
        P(None, ("slab", "quad")),
    )
    return jax.shard_map(
        body,
        mesh=mesh,
        in_specs=placed,
        out_specs=(P("slab", "quad", None), P(None, ("slab", "quad"))),
        check_vma=False,
    )
```

```python
import functools

import jax
import jax.numpy as jnp
from jax import lax
from jax.experimental import pallas as pl
from jax.experimental.pallas import tpu as pltpu
from jax.sharding import PartitionSpec as P

CH = 4
CA = 16
CB = 256
ITERS = 12
LANES = 128
SUBLANES = 8
DEPTH = 2
FIRST = CH * DEPTH + 1

damping = 0.05
source_gain = 4.0

VMEM = pl.BlockSpec(memory_space=pltpu.VMEM)
SMEM = pl.BlockSpec(memory_space=pltpu.SMEM)
HBM = pl.BlockSpec(memory_space=pltpu.HBM)
LIMIT = pltpu.CompilerParams(vmem_limit_bytes=48 * 1024 * 1024)


def reach(distance):
    needed = ITERS - 1 - CH * (max(distance, 1) - 1)
    return 1 << (needed - 1).bit_length()


def lanes_of(shape):
    return lax.broadcasted_iota(jnp.int32, shape, len(shape) - 1)


def turned(value, shift):
    shift %= LANES
    return pltpu.roll(value, shift, value.ndim - 1) if shift else value


def pack_own(window, own):
    pieces = LANES // own
    tall = window.shape[1] // pieces
    lane = lanes_of((window.shape[0], tall, LANES))
    result = window[:, :tall]
    for piece in range(1, pieces):
        part = turned(window[:, piece * tall : (piece + 1) * tall], piece * own)
        result = jnp.where(lane < piece * own, result, part)
    return result


def unpack_own(packed, own):
    pieces = LANES // own
    return jnp.concatenate([turned(packed, -piece * own) for piece in range(pieces)], axis=1)


def strip_plan(across, fields, halo):
    rows = across * 2 * halo // LANES
    return (1, rows) if rows >= SUBLANES else (fields, rows * fields)


def packed_rows(across, fields, halo, own):
    shared, rows = strip_plan(across, fields, halo)
    return fields * CH * across * own // LANES + (fields // shared) * CH * rows


def pack(windows, halo, own):
    across = windows[0].shape[1]
    shared, rows = strip_plan(across, len(windows), halo)
    pieces = [pack_own(window, own) for window in windows]
    lane = lanes_of(windows[0].shape)
    joined = [
        jnp.where(lane >= LANES - halo, window, turned(window, LANES - 2 * halo - own))
        for window in windows
    ]
    lane = lanes_of((CH, rows, LANES))
    for first in range(0, len(windows), shared):
        strip, at = None, 0
        for value in joined[first : first + shared]:
            for row in range(0, across, rows):
                part = turned(value[:, row : row + rows], at + 2 * halo)
                strip = part if strip is None else jnp.where(lane < at, strip, part)
                at += 2 * halo
        pieces.append(strip)
    return jnp.concatenate([piece.reshape(-1, LANES) for piece in pieces], axis=0)


def unpack(value, fields, across, halo, own):
    shared, rows = strip_plan(across, fields, halo)
    tall = across * own // LANES
    count = fields * CH * tall
    owned = value[:count].reshape(fields, CH, tall, LANES)
    strips = value[count:].reshape(fields // shared, CH, rows, LANES)
    lane = lanes_of((CH, rows, LANES))
    windows = []
    for field in range(fields):
        window = unpack_own(owned[field], own)
        strip = strips[field // shared]
        at = (field % shared) * across // rows * 2 * halo
        blocks = []
        for row in range(0, across, rows):
            right = turned(strip, own - at)
            left = turned(strip, -2 * halo - at)
            block = jnp.where(lane < own + halo, right, 0.0)
            block = jnp.where(lane >= LANES - halo, left, block)
            blocks.append(jnp.where(lane < own, window[:, row : row + rows], block))
            at += 2 * halo
        windows.append(jnp.concatenate(blocks, axis=1))
    return windows


def halves(value):
    high = value.astype(jnp.bfloat16)
    low = (value - high.astype(jnp.float32)).astype(jnp.bfloat16)
    return high, low


def short_iota(shape):
    return lax.broadcasted_iota(jnp.int32, shape, 0).astype(jnp.int16)


def row_of(cell_ref, span, across):
    return cell_ref[1:2, span] * across + cell_ref[0:1, span] * CA + cell_ref[2:3, span]


def one_hot(rows, index):
    one, zero = jnp.bfloat16(1), jnp.bfloat16(0)
    return jnp.where(rows == index.astype(jnp.int16), one, zero)


def mass_of(count_ref, volume_ref, first, span):
    volume = volume_ref[0:1, span]
    slot = lax.broadcasted_iota(jnp.int32, volume.shape, 1) + first
    return jnp.where(slot < count_ref[0], volume, 0.0)


def grain_kernel(quads, count_ref, *refs):
    sources, out_ref, targets, sems = refs[:4], refs[4], refs[5:9], refs[9]
    copies = [
        pltpu.make_async_copy(source, target, sems.at[index])
        for index, (source, target) in enumerate(zip(sources, targets))
    ]
    for copy in copies:
        copy.start()
    for copy in copies:
        copy.wait()
    cell_ref, weight_ref, volume_ref, velocity_ref = targets
    span = pl.ds(0, weight_ref.shape[1])
    mass = mass_of(count_ref, volume_ref, 0, span)
    flat = row_of(cell_ref, span, quads * CA) * CB + cell_ref[3:4, span]
    out_ref[0:1, :] = flat.astype(jnp.float32)
    out_ref[1:2, :] = weight_ref[...]
    out_ref[2:3, :] = mass
    out_ref[3:4, :] = mass * velocity_ref[0:1, span]


def deposit_into(total, quads, chunk, place_ref, grain_ref):
    own = CB // quads
    halo = reach(0)
    rows = CH * quads * CA
    size = own + 2 * halo
    row_iota = short_iota((rows, chunk))
    iota = lax.broadcasted_iota(jnp.int32, (size, chunk), 0)
    col_iota = jnp.where(iota < own + halo, iota, iota - size).astype(jnp.int16)
    for first in range(0, grain_ref.shape[1], chunk):
        span = pl.ds(first, chunk)
        flat = grain_ref[0:1, span]
        row = jnp.floor(flat * (1.0 / CB))
        col = (flat - row * CB).astype(jnp.int32) - place_ref[0] * own
        lower = grain_ref[1:2, span]
        upper = 1.0 - lower
        hot = one_hot(row_iota, row.astype(jnp.int32))
        at_lower = col_iota == col.astype(jnp.int16)
        at_upper = col_iota == (col + 1).astype(jnp.int16)
        parts = []
        for amount in (grain_ref[2:3, span], grain_ref[3:4, span]):
            for low, high in zip(halves(amount * lower), halves(amount * upper)):
                parts.append(jnp.where(at_lower, low, jnp.where(at_upper, high, jnp.bfloat16(0))))
        product = lax.dot_general(
            jnp.concatenate(parts, axis=0),
            hot,
            (((1,), (1,)), ((), ())),
            preferred_element_type=jnp.float32,
        )
        total = product if total is None else total + product
    return total


def deposit_kernel(quads, chunk, place_ref, grain_ref, *refs):
    *earlier, out_ref = refs
    total = earlier[0][...] if earlier else None
    out_ref[...] = deposit_into(total, quads, chunk, place_ref, grain_ref)


def coefficient_kernel(quads, chunk, place_ref, *refs):
    grain_ref, total_ref, *outs, solid_ref = refs
    across, own = quads * CA, CB // quads
    total = deposit_into(total_ref[...], quads, chunk, place_ref, grain_ref)
    halo = reach(0)
    size = own + 2 * halo
    windows = []
    for base in range(0, 4 * size, 2 * size):
        field = total[base : base + size] + total[base + size : base + 2 * size]
        gap = jnp.zeros((LANES - size, field.shape[1]), jnp.float32)
        field = jnp.concatenate([field[: own + halo], gap, field[own + halo :]], axis=0)
        windows.append(field.T.reshape(CH, across, LANES))
    solid, moment = windows
    solid_ref[...] = pack_own(solid, own).reshape(solid_ref.shape)
    lane = lanes_of(solid.shape)
    column = jnp.where(lane < (LANES + own) // 2, lane, lane - LANES) + place_ref[0] * own
    inside = (column >= 0) & (column < CB)
    voidage = 1.0 / (1.0 + solid)
    scale = 1.0 / (6.0 * voidage + damping)
    offset = jnp.where(inside, source_gain * moment * scale, 0.0)
    gain = jnp.where(inside, voidage * scale, 0.0)
    for distance, out in enumerate(outs):
        out[...] = pack((offset, gain), reach(distance + 1), own)


def sweep_over(sweeps, layers, across, old, new, spare, offset_ref, gain_ref):
    row = lax.broadcasted_iota(jnp.int32, (across, LANES), 0)
    for sweep in range(1, sweeps + 1):
        for layer in range(sweep, layers - sweep):
            centre = old[layer]
            total = old[layer - 1] + old[layer + 1]
            total = total + turned(centre, 1) + turned(centre, -1)
            total = total + jnp.where(row == 0, 0.0, pltpu.roll(centre, 1, 0))
            total = total + jnp.where(row == across - 1, 0.0, pltpu.roll(centre, across - 1, 0))
            new[layer] = offset_ref[layer] + gain_ref[layer] * total
        old, new, spare = new, spare, new
    return old


def slot_of(slab, distance, matching):
    upward = lax.rem(lax.div(slab, distance), 2) ^ matching
    return distance * (1 - 2 * upward)


def swap_plan(depth):
    return [(distance, matching) for distance in range(1, depth + 1) for matching in range(2)]


def framed(last, first, own):
    inner = pack([last[first : first + CH]], SUBLANES, own)
    outer = [pack_own(last[layer : layer + 1], own)[0] for layer in (first - 1, first + CH)]
    return jnp.concatenate([inner] + outer, axis=0)


def relax_kernel(quads, slab_ref, own_ref, *refs):
    *parts, out_ref, offset_ref, gain_ref, even_ref, odd_ref = refs
    across, own = quads * CA, CB // quads
    layers = CH * (1 + len(parts))
    plan = [(DEPTH, own_ref, 1)] + [
        (DEPTH + slot_of(slab_ref[0], distance, matching), part, distance)
        for part, (distance, matching) in zip(parts, swap_plan(DEPTH))
    ]
    for slot, part, distance in plan:
        span = pl.ds(slot * CH, CH)
        offset, gain = unpack(part[...], 2, across, reach(distance), own)
        offset_ref[span] = offset
        gain_ref[span] = gain
    last = sweep_over(
        FIRST - 1, layers, across, offset_ref, even_ref, odd_ref, offset_ref, gain_ref
    )
    out_ref[...] = pack([last[DEPTH * CH : (DEPTH + 1) * CH]], SUBLANES, own)


def finish_kernel(quads, slab_ref, offset_ref, gain_ref, *refs):
    *parts, out_ref, even_ref, odd_ref = refs
    across, own = quads * CA, CB // quads
    slots = [1] + [1 + slot_of(slab_ref[0], *swap) for swap in swap_plan(1)[::-1]]
    for slot, pressure in zip(slots, parts):
        (even_ref[pl.ds(slot * CH, CH)],) = unpack(pressure[...], 1, across, SUBLANES, own)
    near = pl.ds((DEPTH - 1) * CH, 3 * CH)
    last = sweep_over(
        ITERS - FIRST,
        3 * CH,
        across,
        even_ref,
        odd_ref,
        even_ref,
        offset_ref.at[near],
        gain_ref.at[near],
    )
    out_ref[...] = framed(last, CH, own)


def halving(quads):
    return [1 << bit for bit in reversed(range(quads.bit_length() - 1))]


def place_offsets(quads):
    offsets = [0]
    for bit in halving(quads):
        offsets += [offset ^ bit for offset in offsets]
    return offsets


def blend_of(col_iota, at, lower):
    return jnp.where(col_iota == at, lower, jnp.where(col_iota == at + 1, 1.0 - lower, 0.0))


def picked_by(pieces, hot):
    twice = jnp.concatenate([hot, hot], axis=0)
    return jnp.dot(pieces, twice, preferred_element_type=jnp.float32)


def blended(picked, blend, field):
    size = blend.shape[0]
    return jnp.sum(picked[field * size : (field + 1) * size] * blend, axis=0, keepdims=True)


def solid_table(value, across, own):
    window = unpack_own(value.reshape(CH, across * own // LANES, LANES), own)
    return jnp.concatenate(halves(window.reshape(CH * across, LANES).T[:own]), axis=1)


def velocity_table(value, across, own):
    tall = across * own // LANES
    count = packed_rows(across, 1, SUBLANES, own)
    (inner,) = unpack(value[:count], 1, across, SUBLANES, own)
    outer = unpack_own(value[count:].reshape(2, tall, LANES), own)
    row = lax.broadcasted_iota(jnp.int32, inner.shape, 1)
    above = jnp.concatenate([inner[1:], outer[1:]], axis=0)
    below = jnp.concatenate([outer[:1], inner[:-1]], axis=0)
    after = jnp.where(row == across - 1, 0.0, pltpu.roll(inner, across - 1, 1))
    before = jnp.where(row == 0, 0.0, pltpu.roll(inner, 1, 1))
    fields = (
        -0.5 * (above - below),
        -0.5 * (after - before),
        -0.5 * (turned(inner, -1) - turned(inner, 1)),
    )
    columns = [field.reshape(CH * across, LANES).T[:own] for field in fields]
    return jnp.concatenate(halves(jnp.concatenate(columns, axis=0)), axis=1)


def chunk_sums(quads, place_ref, table, offsets, fields, cell_ref, weight_ref, row_iota, span):
    across, own = quads * CA, CB // quads
    hot = one_hot(row_iota, row_of(cell_ref, span, across))
    lower = weight_ref[0:1, span]
    picked = picked_by(table, hot)
    col_iota = lax.broadcasted_iota(jnp.int32, (own, picked.shape[1]), 0)
    sums = [0.0] * fields
    for index, offset in enumerate(offsets):
        at = cell_ref[3:4, span] - (place_ref[0] ^ offset) * own
        blend = blend_of(col_iota, at, lower)
        for field in range(fields):
            sums[field] += blended(picked, blend, fields * index + field)
    return sums


def store_sums(chunk, table, offsets, fields, quads, place_ref, cell_ref, weight_ref, earlier, out_ref):
    row_iota = short_iota((CH * quads * CA, chunk))
    for first in range(0, weight_ref.shape[1], chunk):
        span = pl.ds(first, chunk)
        sums = chunk_sums(
            quads, place_ref, table, offsets, fields, cell_ref, weight_ref, row_iota, span
        )
        for field, value in enumerate(sums):
            one = pl.ds(field, 1)
            for partial in earlier:
                value = value + partial[one, span]
            out_ref[one, span] = value


def solid_kernel(quads, chunk, place_ref, cell_ref, weight_ref, held_ref, out_ref):
    across, own = quads * CA, CB // quads
    half = quads // 2
    tables = [solid_table(held_ref[index], across, own) for index in range(half)]
    store_sums(
        chunk,
        jnp.concatenate(tables, axis=0),
        place_offsets(quads)[:half],
        1,
        quads,
        place_ref,
        cell_ref,
        weight_ref,
        [],
        out_ref,
    )


def sampled_kernel(quads, chunk, offset, index, place_ref, cell_ref, weight_ref, held_ref, *refs):
    *earlier, out_ref = refs
    table = velocity_table(held_ref[index], quads * CA, CB // quads)
    store_sums(
        chunk, table, [offset], 3, quads, place_ref, cell_ref, weight_ref, earlier, out_ref
    )


def drag_kernel(quads, chunk, place_ref, count_ref, cell_ref, weight_ref, volume_ref, *refs):
    velocity_ref, solid_ref, sampled_ref, held_ref, got_ref = refs[:5]
    pressure_ref, drag_ref, gathered = refs[5:]
    across, own = quads * CA, CB // quads
    half = quads // 2
    frame = held_ref.shape[1]
    tables = []
    for index in range(half):
        got = got_ref[index]
        tables += [velocity_table(got[:frame], across, own), solid_table(got[frame:], across, own)]
    table = jnp.concatenate(tables, axis=0)
    row_iota = short_iota((CH * across, chunk))
    for first in range(0, weight_ref.shape[1], chunk):
        span = pl.ds(first, chunk)
        *sums, solid = chunk_sums(
            quads,
            place_ref,
            table,
            place_offsets(quads)[half:],
            4,
            cell_ref,
            weight_ref,
            row_iota,
            span,
        )
        factor = mass_of(count_ref, volume_ref, first, span)
        factor = factor * (1.0 + (solid + solid_ref[0:1, span])) ** 2
        for component, value in enumerate(sums):
            one = pl.ds(component, 1)
            drag_ref[one, span] = factor * (
                value + sampled_ref[one, span] - velocity_ref[one, span]
            )
    shape = gathered.shape[1:]
    count = CH * shape[1]
    parts = [
        ref[index][:count].reshape(shape) for ref in (held_ref, got_ref) for index in range(half)
    ]
    for offset, part in zip(place_offsets(quads), parts):
        gathered[place_ref[0] ^ offset] = part
    bands = shape[1] // CA
    band = pl.ds(pl.multiple_of(lax.rem(place_ref[0], bands) * CA, SUBLANES), CA)
    back = lax.rem(LANES - lax.div(place_ref[0], bands) * own, LANES)
    lane = lanes_of((CH, CA, LANES))
    pieces = LANES // own
    for first in range(0, quads, pieces):
        block = None
        for near in range(pieces):
            part = pltpu.roll(gathered[first + near, :, band, :], lax.rem(back + near * own, LANES), 2)
            block = part if block is None else jnp.where(lane < near * own, block, part)
        pressure_ref[:, :, first * own : first * own + LANES] = block


def body(grain_cell, grain_count, grain_weight, grain_volume, grain_velocity):
    quads = lax.axis_size("quad")
    slabs = lax.axis_size("slab")
    grains = grain_weight.shape[0]
    across = quads * CA
    own = CB // quads
    tall = across * own // LANES
    place = lax.axis_index("quad").astype(jnp.int32).reshape(1)
    level = lax.axis_index("slab").astype(jnp.int32).reshape(1)
    weight = grain_weight.reshape(1, grains)
    volume = grain_volume.reshape(1, grains)

    grain_chunk = min(grains, 512)

    def cells(*shape):
        return jax.ShapeDtypeStruct(shape, jnp.float32)

    def over_quad(step, value):
        pairs = [(index, index ^ step) for index in range(quads)]
        return lax.ppermute(value, "quad", pairs)

    def swapped(distance, matching, value):
        lower = [
            index
            for index in range(slabs - distance)
            if (index // distance) % 2 == matching
        ]
        pairs = [(index, index + distance) for index in lower]
        return lax.ppermute(value, "slab", pairs + [(high, low) for low, high in pairs])

    *early, last = halving(quads)

    def nearly_all(value):
        held = value[None]
        for bit in early:
            held = jnp.concatenate([held, over_quad(bit, held)], axis=0)
        return held

    def pinned(value):
        return pltpu.with_memory_space_constraint(value, pltpu.HBM)

    packed_grains = pl.pallas_call(
        functools.partial(grain_kernel, quads),
        out_shape=cells(4, grains),
        in_specs=[SMEM] + [HBM] * 4,
        out_specs=VMEM,
        scratch_shapes=[
            pltpu.VMEM((4, grains), jnp.int32),
            pltpu.VMEM((1, grains), jnp.float32),
            pltpu.VMEM((1, grains), jnp.float32),
            pltpu.VMEM((3, grains), jnp.float32),
            pltpu.SemaphoreType.DMA((4,)),
        ],
        compiler_params=LIMIT,
        name="grains",
    )(
        grain_count,
        pinned(grain_cell),
        pinned(weight),
        pinned(volume),
        pinned(grain_velocity),
    )
    packs = [packed_grains]
    for bit in early:
        packs += [over_quad(bit, pack) for pack in packs]
    size = own + 2 * reach(0)
    deposit_chunk = min(grains, 2048)
    total = None

    def deposited(total, arrived):
        earlier = [] if total is None else [total]
        return pl.pallas_call(
            functools.partial(deposit_kernel, quads, deposit_chunk),
            out_shape=cells(4 * size, CH * across),
            in_specs=[SMEM] + [VMEM] * (1 + len(earlier)),
            out_specs=VMEM,
            compiler_params=LIMIT,
            cost_estimate=pl.CostEstimate(
                flops=8 * size * CH * across * grains, bytes_accessed=2**20, transcendentals=0
            ),
            name="deposit",
        )(place, arrived, *earlier)

    for index, pack in enumerate(packs):
        if index:
            pack, total = lax.optimization_barrier((pack, total))
        arriving = over_quad(last, pack)
        total = deposited(total, pack)
        if index < len(packs) - 1:
            total = deposited(total, arriving)
    *coefs, solid = pl.pallas_call(
        functools.partial(coefficient_kernel, quads, deposit_chunk),
        out_shape=[
            cells(packed_rows(across, 2, reach(distance), own), LANES)
            for distance in range(1, DEPTH + 1)
        ]
        + [cells(CH * tall, LANES)],
        in_specs=[SMEM] + [VMEM] * 2,
        out_specs=[VMEM] * (DEPTH + 1),
        compiler_params=LIMIT,
        name="coefficients",
    )(place, arriving, total)

    stack = [coefs[0]] + [
        swapped(distance, matching, coefs[distance - 1])
        for distance, matching in swap_plan(DEPTH)
    ]
    stack[-1], solid = lax.optimization_barrier((stack[-1], solid))
    solids = nearly_all(solid)
    frame = cells(packed_rows(across, 1, SUBLANES, own) + 2 * tall, LANES)
    layers = CH * len(stack)
    window = cells(layers, across, LANES)
    centre, offset, gain = pl.pallas_call(
        functools.partial(relax_kernel, quads),
        out_shape=[
            cells(packed_rows(across, 1, SUBLANES, own), LANES),
            window,
            window,
        ],
        in_specs=[SMEM] + [VMEM] * len(stack),
        out_specs=[VMEM] * 3,
        scratch_shapes=[pltpu.VMEM(window.shape, window.dtype)] * 2,
        compiler_params=LIMIT,
        name="relax",
    )(level, *stack)
    centre, solids = lax.optimization_barrier((centre, solids))
    solid_sampled = pl.pallas_call(
        functools.partial(solid_kernel, quads, grain_chunk),
        out_shape=cells(1, grains),
        in_specs=[SMEM] + [VMEM] * 3,
        out_specs=VMEM,
        compiler_params=LIMIT,
        cost_estimate=pl.CostEstimate(
            flops=8 * own * CH * across * grains, bytes_accessed=2**20, transcendentals=0
        ),
        name="solid",
    )(place, grain_cell, weight, solids)

    pressures = [centre] + [swapped(*swap, centre) for swap in swap_plan(1)[::-1]]
    pressures, solid_sampled = lax.optimization_barrier((pressures, solid_sampled))
    mine = pl.pallas_call(
        functools.partial(finish_kernel, quads),
        out_shape=frame,
        in_specs=[SMEM] + [VMEM] * 5,
        out_specs=VMEM,
        scratch_shapes=[pltpu.VMEM((3 * CH, across, LANES), jnp.float32)] * 2,
        compiler_params=LIMIT,
        name="finish",
    )(level, offset, gain, *pressures)

    def sampled_from(held, index, *earlier):
        return pl.pallas_call(
            functools.partial(
                sampled_kernel, quads, grain_chunk, place_offsets(quads)[index], index
            ),
            out_shape=cells(3, grains),
            in_specs=[SMEM] + [VMEM] * (3 + len(earlier)),
            out_specs=VMEM,
            compiler_params=LIMIT,
            cost_estimate=pl.CostEstimate(
                flops=12 * own * CH * across * grains, bytes_accessed=2**20, transcendentals=0
            ),
            name="sampled",
        )(place, grain_cell, weight, held, *earlier)

    held = mine[None]
    partial = sampled_from(held, 0)
    for bit in early:
        known = held.shape[0]
        held = jnp.concatenate([held, over_quad(bit, held)], axis=0)
        held, partial = lax.optimization_barrier((held, partial))
        for index in range(known, held.shape[0]):
            partial = sampled_from(held, index, partial)
    got = over_quad(last, jnp.concatenate([held, solids], axis=1))
    pressure, drag = pl.pallas_call(
        functools.partial(drag_kernel, quads, grain_chunk),
        out_shape=[cells(CH, CA, CB), cells(3, grains)],
        in_specs=[SMEM] * 2 + [VMEM] * 8,
        out_specs=[VMEM] * 2,
        scratch_shapes=[pltpu.VMEM((quads, CH, tall, LANES), jnp.float32)],
        compiler_params=LIMIT,
        name="drag",
    )(
        place,
        grain_count,
        grain_cell,
        weight,
        volume,
        grain_velocity,
        solid_sampled,
        partial,
        held,
        got,
    )
    return pressure, drag


def solution(mesh):
    placed = (
        P(None, ("slab", "quad")),
        P(("slab", "quad")),
        P(("slab", "quad")),
        P(("slab", "quad")),
        P(None, ("slab", "quad")),
    )
    return jax.shard_map(
        body,
        mesh=mesh,
        in_specs=placed,
        out_specs=(P("slab", "quad", None), P(None, ("slab", "quad"))),
        check_vma=False,
    )
```

```python
import functools

import jax
import jax.numpy as jnp
from jax import lax
from jax.experimental import pallas as pl
from jax.experimental.pallas import tpu as pltpu
from jax.sharding import PartitionSpec as P

CH = 4
CA = 16
CB = 256
ITERS = 12
LANES = 128
SUBLANES = 8
DEPTH = 2
FIRST = CH * DEPTH + 1

damping = 0.05
source_gain = 4.0

VMEM = pl.BlockSpec(memory_space=pltpu.VMEM)
SMEM = pl.BlockSpec(memory_space=pltpu.SMEM)
HBM = pl.BlockSpec(memory_space=pltpu.HBM)
LIMIT = pltpu.CompilerParams(vmem_limit_bytes=48 * 1024 * 1024)


def reach(distance):
    needed = ITERS - 1 - CH * (max(distance, 1) - 1)
    return 1 << (needed - 1).bit_length()


def lanes_of(shape):
    return lax.broadcasted_iota(jnp.int32, shape, len(shape) - 1)


def turned(value, shift):
    shift %= LANES
    return pltpu.roll(value, shift, value.ndim - 1) if shift else value


def pack_own(window, own):
    pieces = LANES // own
    tall = window.shape[1] // pieces
    lane = lanes_of((window.shape[0], tall, LANES))
    result = window[:, :tall]
    for piece in range(1, pieces):
        part = turned(window[:, piece * tall : (piece + 1) * tall], piece * own)
        result = jnp.where(lane < piece * own, result, part)
    return result


def unpack_own(packed, own):
    pieces = LANES // own
    return jnp.concatenate([turned(packed, -piece * own) for piece in range(pieces)], axis=1)


def strip_plan(across, fields, halo):
    rows = across * 2 * halo // LANES
    return (1, rows) if rows >= SUBLANES else (fields, rows * fields)


def packed_rows(across, fields, halo, own):
    shared, rows = strip_plan(across, fields, halo)
    return fields * CH * across * own // LANES + (fields // shared) * CH * rows


def pack(windows, halo, own):
    across = windows[0].shape[1]
    shared, rows = strip_plan(across, len(windows), halo)
    pieces = [pack_own(window, own) for window in windows]
    lane = lanes_of(windows[0].shape)
    joined = [
        jnp.where(lane >= LANES - halo, window, turned(window, LANES - 2 * halo - own))
        for window in windows
    ]
    lane = lanes_of((CH, rows, LANES))
    for first in range(0, len(windows), shared):
        strip, at = None, 0
        for value in joined[first : first + shared]:
            for row in range(0, across, rows):
                part = turned(value[:, row : row + rows], at + 2 * halo)
                strip = part if strip is None else jnp.where(lane < at, strip, part)
                at += 2 * halo
        pieces.append(strip)
    return jnp.concatenate([piece.reshape(-1, LANES) for piece in pieces], axis=0)


def unpack(value, fields, across, halo, own):
    shared, rows = strip_plan(across, fields, halo)
    tall = across * own // LANES
    count = fields * CH * tall
    owned = value[:count].reshape(fields, CH, tall, LANES)
    strips = value[count:].reshape(fields // shared, CH, rows, LANES)
    lane = lanes_of((CH, rows, LANES))
    windows = []
    for field in range(fields):
        window = unpack_own(owned[field], own)
        strip = strips[field // shared]
        at = (field % shared) * across // rows * 2 * halo
        blocks = []
        for row in range(0, across, rows):
            right = turned(strip, own - at)
            left = turned(strip, -2 * halo - at)
            block = jnp.where(lane < own + halo, right, 0.0)
            block = jnp.where(lane >= LANES - halo, left, block)
            blocks.append(jnp.where(lane < own, window[:, row : row + rows], block))
            at += 2 * halo
        windows.append(jnp.concatenate(blocks, axis=1))
    return windows


def halves(value):
    high = value.astype(jnp.bfloat16)
    low = (value - high.astype(jnp.float32)).astype(jnp.bfloat16)
    return high, low


def short_iota(shape):
    return lax.broadcasted_iota(jnp.int32, shape, 0).astype(jnp.int16)


def row_of(cell_ref, span, across):
    return cell_ref[1:2, span] * across + cell_ref[0:1, span] * CA + cell_ref[2:3, span]


def one_hot(rows, index):
    one, zero = jnp.bfloat16(1), jnp.bfloat16(0)
    return jnp.where(rows == index.astype(jnp.int16), one, zero)


def mass_of(count_ref, volume_ref, first, span):
    volume = volume_ref[0:1, span]
    slot = lax.broadcasted_iota(jnp.int32, volume.shape, 1) + first
    return jnp.where(slot < count_ref[0], volume, 0.0)


def grain_kernel(quads, count_ref, *refs):
    sources, out_ref, targets, sems = refs[:4], refs[4], refs[5:9], refs[9]
    copies = [
        pltpu.make_async_copy(source, target, sems.at[index])
        for index, (source, target) in enumerate(zip(sources, targets))
    ]
    for copy in copies:
        copy.start()
    for copy in copies:
        copy.wait()
    cell_ref, weight_ref, volume_ref, velocity_ref = targets
    span = pl.ds(0, weight_ref.shape[1])
    mass = mass_of(count_ref, volume_ref, 0, span)
    flat = row_of(cell_ref, span, quads * CA) * CB + cell_ref[3:4, span]
    out_ref[0:1, :] = flat.astype(jnp.float32)
    out_ref[1:2, :] = weight_ref[...]
    out_ref[2:3, :] = mass
    out_ref[3:4, :] = mass * velocity_ref[0:1, span]


def deposit_into(total, quads, chunk, place_ref, grain_ref):
    own = CB // quads
    halo = reach(0)
    rows = CH * quads * CA
    size = own + 2 * halo
    row_iota = short_iota((rows, chunk))
    iota = lax.broadcasted_iota(jnp.int32, (size, chunk), 0)
    col_iota = jnp.where(iota < own + halo, iota, iota - size).astype(jnp.int16)
    for first in range(0, grain_ref.shape[1], chunk):
        span = pl.ds(first, chunk)
        flat = grain_ref[0:1, span]
        row = jnp.floor(flat * (1.0 / CB))
        col = (flat - row * CB).astype(jnp.int32) - place_ref[0] * own
        lower = grain_ref[1:2, span]
        upper = 1.0 - lower
        hot = one_hot(row_iota, row.astype(jnp.int32))
        at_lower = col_iota == col.astype(jnp.int16)
        at_upper = col_iota == (col + 1).astype(jnp.int16)
        parts = []
        for amount in (grain_ref[2:3, span], grain_ref[3:4, span]):
            for low, high in zip(halves(amount * lower), halves(amount * upper)):
                parts.append(jnp.where(at_lower, low, jnp.where(at_upper, high, jnp.bfloat16(0))))
        product = lax.dot_general(
            jnp.concatenate(parts, axis=0),
            hot,
            (((1,), (1,)), ((), ())),
            preferred_element_type=jnp.float32,
        )
        total = product if total is None else total + product
    return total


def deposit_kernel(quads, chunk, place_ref, grain_ref, *refs):
    *earlier, out_ref = refs
    total = earlier[0][...] if earlier else None
    out_ref[...] = deposit_into(total, quads, chunk, place_ref, grain_ref)


def coefficient_kernel(quads, chunk, place_ref, *refs):
    grain_ref, total_ref, *outs, solid_ref = refs
    across, own = quads * CA, CB // quads
    total = deposit_into(total_ref[...], quads, chunk, place_ref, grain_ref)
    halo = reach(0)
    size = own + 2 * halo
    windows = []
    for base in range(0, 4 * size, 2 * size):
        field = total[base : base + size] + total[base + size : base + 2 * size]
        gap = jnp.zeros((LANES - size, field.shape[1]), jnp.float32)
        field = jnp.concatenate([field[: own + halo], gap, field[own + halo :]], axis=0)
        windows.append(field.T.reshape(CH, across, LANES))
    solid, moment = windows
    solid_ref[...] = pack_own(solid, own).reshape(solid_ref.shape)
    lane = lanes_of(solid.shape)
    column = jnp.where(lane < (LANES + own) // 2, lane, lane - LANES) + place_ref[0] * own
    inside = (column >= 0) & (column < CB)
    voidage = 1.0 / (1.0 + solid)
    scale = 1.0 / (6.0 * voidage + damping)
    offset = jnp.where(inside, source_gain * moment * scale, 0.0)
    gain = jnp.where(inside, voidage * scale, 0.0)
    for distance, out in enumerate(outs):
        out[...] = pack((offset, gain), reach(distance + 1), own)


def sweep_over(sweeps, layers, across, old, new, spare, offset_ref, gain_ref):
    row = lax.broadcasted_iota(jnp.int32, (across, LANES), 0)
    for sweep in range(1, sweeps + 1):
        for layer in range(sweep, layers - sweep):
            centre = old[layer]
            total = old[layer - 1] + old[layer + 1]
            total = total + turned(centre, 1) + turned(centre, -1)
            total = total + jnp.where(row == 0, 0.0, pltpu.roll(centre, 1, 0))
            total = total + jnp.where(row == across - 1, 0.0, pltpu.roll(centre, across - 1, 0))
            new[layer] = offset_ref[layer] + gain_ref[layer] * total
        old, new, spare = new, spare, new
    return old


def slot_of(slab, distance, matching):
    upward = lax.rem(lax.div(slab, distance), 2) ^ matching
    return distance * (1 - 2 * upward)


def swap_plan(depth):
    return [(distance, matching) for distance in range(1, depth + 1) for matching in (1, 0)]


def framed(last, first, own):
    inner = pack([last[first : first + CH]], SUBLANES, own)
    outer = [pack_own(last[layer : layer + 1], own)[0] for layer in (first - 1, first + CH)]
    return jnp.concatenate([inner] + outer, axis=0)


def relax_kernel(quads, slab_ref, own_ref, *refs):
    *parts, out_ref, offset_ref, gain_ref, even_ref, odd_ref = refs
    across, own = quads * CA, CB // quads
    layers = CH * (1 + len(parts))
    plan = [(DEPTH, own_ref, 1)] + [
        (DEPTH + slot_of(slab_ref[0], distance, matching), part, distance)
        for part, (distance, matching) in zip(parts, swap_plan(DEPTH))
    ]
    for slot, part, distance in plan:
        span = pl.ds(slot * CH, CH)
        offset, gain = unpack(part[...], 2, across, reach(distance), own)
        offset_ref[span] = offset
        gain_ref[span] = gain
    last = sweep_over(
        FIRST - 1, layers, across, offset_ref, even_ref, odd_ref, offset_ref, gain_ref
    )
    out_ref[...] = pack([last[DEPTH * CH : (DEPTH + 1) * CH]], SUBLANES, own)


def finish_kernel(quads, slab_ref, offset_ref, gain_ref, *refs):
    *parts, out_ref, even_ref, odd_ref = refs
    across, own = quads * CA, CB // quads
    slots = [1] + [1 + slot_of(slab_ref[0], *swap) for swap in swap_plan(1)]
    for slot, pressure in zip(slots, parts):
        (even_ref[pl.ds(slot * CH, CH)],) = unpack(pressure[...], 1, across, SUBLANES, own)
    near = pl.ds((DEPTH - 1) * CH, 3 * CH)
    last = sweep_over(
        ITERS - FIRST,
        3 * CH,
        across,
        even_ref,
        odd_ref,
        even_ref,
        offset_ref.at[near],
        gain_ref.at[near],
    )
    out_ref[...] = framed(last, CH, own)


def halving(quads):
    return [1 << bit for bit in reversed(range(quads.bit_length() - 1))]


def place_offsets(quads):
    offsets = [0]
    for bit in halving(quads):
        offsets += [offset ^ bit for offset in offsets]
    return offsets


def blend_of(col_iota, at, lower):
    return jnp.where(col_iota == at, lower, jnp.where(col_iota == at + 1, 1.0 - lower, 0.0))


def picked_by(pieces, hot):
    twice = jnp.concatenate([hot, hot], axis=0)
    return jnp.dot(pieces, twice, preferred_element_type=jnp.float32)


def blended(picked, blend, field):
    size = blend.shape[0]
    return jnp.sum(picked[field * size : (field + 1) * size] * blend, axis=0, keepdims=True)


def solid_table(value, across, own):
    window = unpack_own(value.reshape(CH, across * own // LANES, LANES), own)
    return jnp.concatenate(halves(window.reshape(CH * across, LANES).T[:own]), axis=1)


def velocity_table(value, across, own):
    tall = across * own // LANES
    count = packed_rows(across, 1, SUBLANES, own)
    (inner,) = unpack(value[:count], 1, across, SUBLANES, own)
    outer = unpack_own(value[count:].reshape(2, tall, LANES), own)
    row = lax.broadcasted_iota(jnp.int32, inner.shape, 1)
    above = jnp.concatenate([inner[1:], outer[1:]], axis=0)
    below = jnp.concatenate([outer[:1], inner[:-1]], axis=0)
    after = jnp.where(row == across - 1, 0.0, pltpu.roll(inner, across - 1, 1))
    before = jnp.where(row == 0, 0.0, pltpu.roll(inner, 1, 1))
    fields = (
        -0.5 * (above - below),
        -0.5 * (after - before),
        -0.5 * (turned(inner, -1) - turned(inner, 1)),
    )
    columns = [field.reshape(CH * across, LANES).T[:own] for field in fields]
    return jnp.concatenate(halves(jnp.concatenate(columns, axis=0)), axis=1)


def chunk_sums(quads, place_ref, table, offsets, fields, cell_ref, weight_ref, row_iota, span):
    across, own = quads * CA, CB // quads
    hot = one_hot(row_iota, row_of(cell_ref, span, across))
    lower = weight_ref[0:1, span]
    picked = picked_by(table, hot)
    col_iota = lax.broadcasted_iota(jnp.int32, (own, picked.shape[1]), 0)
    sums = [0.0] * fields
    for index, offset in enumerate(offsets):
        at = cell_ref[3:4, span] - (place_ref[0] ^ offset) * own
        blend = blend_of(col_iota, at, lower)
        for field in range(fields):
            sums[field] += blended(picked, blend, fields * index + field)
    return sums


def store_sums(chunk, table, offsets, fields, quads, place_ref, cell_ref, weight_ref, earlier, out_ref):
    row_iota = short_iota((CH * quads * CA, chunk))
    for first in range(0, weight_ref.shape[1], chunk):
        span = pl.ds(first, chunk)
        sums = chunk_sums(
            quads, place_ref, table, offsets, fields, cell_ref, weight_ref, row_iota, span
        )
        for field, value in enumerate(sums):
            one = pl.ds(field, 1)
            for partial in earlier:
                value = value + partial[one, span]
            out_ref[one, span] = value


def solid_kernel(quads, chunk, place_ref, cell_ref, weight_ref, held_ref, out_ref):
    across, own = quads * CA, CB // quads
    half = quads // 2
    tables = [solid_table(held_ref[index], across, own) for index in range(half)]
    store_sums(
        chunk,
        jnp.concatenate(tables, axis=0),
        place_offsets(quads)[:half],
        1,
        quads,
        place_ref,
        cell_ref,
        weight_ref,
        [],
        out_ref,
    )


def sampled_kernel(quads, chunk, offset, index, place_ref, cell_ref, weight_ref, held_ref, *refs):
    *earlier, out_ref = refs
    table = velocity_table(held_ref[index], quads * CA, CB // quads)
    store_sums(
        chunk, table, [offset], 3, quads, place_ref, cell_ref, weight_ref, earlier, out_ref
    )


def drag_kernel(quads, chunk, place_ref, count_ref, cell_ref, weight_ref, volume_ref, *refs):
    velocity_ref, solid_ref, sampled_ref, held_ref, got_ref = refs[:5]
    pressure_ref, drag_ref, gathered = refs[5:]
    across, own = quads * CA, CB // quads
    half = quads // 2
    frame = held_ref.shape[1]
    tables = []
    for index in range(half):
        got = got_ref[index]
        tables += [velocity_table(got[:frame], across, own), solid_table(got[frame:], across, own)]
    table = jnp.concatenate(tables, axis=0)
    row_iota = short_iota((CH * across, chunk))
    for first in range(0, weight_ref.shape[1], chunk):
        span = pl.ds(first, chunk)
        *sums, solid = chunk_sums(
            quads,
            place_ref,
            table,
            place_offsets(quads)[half:],
            4,
            cell_ref,
            weight_ref,
            row_iota,
            span,
        )
        factor = mass_of(count_ref, volume_ref, first, span)
        factor = factor * (1.0 + (solid + solid_ref[0:1, span])) ** 2
        for component, value in enumerate(sums):
            one = pl.ds(component, 1)
            drag_ref[one, span] = factor * (
                value + sampled_ref[one, span] - velocity_ref[one, span]
            )
    shape = gathered.shape[1:]
    count = CH * shape[1]
    parts = [
        ref[index][:count].reshape(shape) for ref in (held_ref, got_ref) for index in range(half)
    ]
    for offset, part in zip(place_offsets(quads), parts):
        gathered[place_ref[0] ^ offset] = part
    bands = shape[1] // CA
    band = pl.ds(pl.multiple_of(lax.rem(place_ref[0], bands) * CA, SUBLANES), CA)
    back = lax.rem(LANES - lax.div(place_ref[0], bands) * own, LANES)
    lane = lanes_of((CH, CA, LANES))
    pieces = LANES // own
    for first in range(0, quads, pieces):
        block = None
        for near in range(pieces):
            part = pltpu.roll(gathered[first + near, :, band, :], lax.rem(back + near * own, LANES), 2)
            block = part if block is None else jnp.where(lane < near * own, block, part)
        pressure_ref[:, :, first * own : first * own + LANES] = block


def body(grain_cell, grain_count, grain_weight, grain_volume, grain_velocity):
    quads = lax.axis_size("quad")
    slabs = lax.axis_size("slab")
    grains = grain_weight.shape[0]
    across = quads * CA
    own = CB // quads
    tall = across * own // LANES
    place = lax.axis_index("quad").astype(jnp.int32).reshape(1)
    level = lax.axis_index("slab").astype(jnp.int32).reshape(1)
    weight = grain_weight.reshape(1, grains)
    volume = grain_volume.reshape(1, grains)

    grain_chunk = min(grains, 512)

    def cells(*shape):
        return jax.ShapeDtypeStruct(shape, jnp.float32)

    def over_quad(step, value):
        pairs = [(index, index ^ step) for index in range(quads)]
        return lax.ppermute(value, "quad", pairs)

    def swapped(distance, matching, value):
        lower = [
            index
            for index in range(slabs - distance)
            if (index // distance) % 2 == matching
        ]
        pairs = [(index, index + distance) for index in lower]
        return lax.ppermute(value, "slab", pairs + [(high, low) for low, high in pairs])

    *early, last = halving(quads)

    def nearly_all(value):
        held = value[None]
        for bit in early:
            held = jnp.concatenate([held, over_quad(bit, held)], axis=0)
        return held

    def pinned(value):
        return pltpu.with_memory_space_constraint(value, pltpu.HBM)

    packed_grains = pl.pallas_call(
        functools.partial(grain_kernel, quads),
        out_shape=cells(4, grains),
        in_specs=[SMEM] + [HBM] * 4,
        out_specs=VMEM,
        scratch_shapes=[
            pltpu.VMEM((4, grains), jnp.int32),
            pltpu.VMEM((1, grains), jnp.float32),
            pltpu.VMEM((1, grains), jnp.float32),
            pltpu.VMEM((3, grains), jnp.float32),
            pltpu.SemaphoreType.DMA((4,)),
        ],
        compiler_params=LIMIT,
        name="grains",
    )(
        grain_count,
        pinned(grain_cell),
        pinned(weight),
        pinned(volume),
        pinned(grain_velocity),
    )
    packs = [packed_grains]
    for bit in early:
        packs += [over_quad(bit, pack) for pack in packs]
    size = own + 2 * reach(0)
    deposit_chunk = min(grains, 2048)
    total = None

    def deposited(total, arrived):
        earlier = [] if total is None else [total]
        return pl.pallas_call(
            functools.partial(deposit_kernel, quads, deposit_chunk),
            out_shape=cells(4 * size, CH * across),
            in_specs=[SMEM] + [VMEM] * (1 + len(earlier)),
            out_specs=VMEM,
            compiler_params=LIMIT,
            cost_estimate=pl.CostEstimate(
                flops=8 * size * CH * across * grains, bytes_accessed=2**20, transcendentals=0
            ),
            name="deposit",
        )(place, arrived, *earlier)

    for index, pack in enumerate(packs):
        if index:
            pack, total = lax.optimization_barrier((pack, total))
        arriving = over_quad(last, pack)
        total = deposited(total, pack)
        if index < len(packs) - 1:
            total = deposited(total, arriving)
    *coefs, solid = pl.pallas_call(
        functools.partial(coefficient_kernel, quads, deposit_chunk),
        out_shape=[
            cells(packed_rows(across, 2, reach(distance), own), LANES)
            for distance in range(1, DEPTH + 1)
        ]
        + [cells(CH * tall, LANES)],
        in_specs=[SMEM] + [VMEM] * 2,
        out_specs=[VMEM] * (DEPTH + 1),
        compiler_params=LIMIT,
        name="coefficients",
    )(place, arriving, total)

    stack = [coefs[0]] + [
        swapped(distance, matching, coefs[distance - 1])
        for distance, matching in swap_plan(DEPTH)
    ]
    stack[1], solid = lax.optimization_barrier((stack[1], solid))
    solids = nearly_all(solid)
    frame = cells(packed_rows(across, 1, SUBLANES, own) + 2 * tall, LANES)
    layers = CH * len(stack)
    window = cells(layers, across, LANES)
    centre, offset, gain = pl.pallas_call(
        functools.partial(relax_kernel, quads),
        out_shape=[
            cells(packed_rows(across, 1, SUBLANES, own), LANES),
            window,
            window,
        ],
        in_specs=[SMEM] + [VMEM] * len(stack),
        out_specs=[VMEM] * 3,
        scratch_shapes=[pltpu.VMEM(window.shape, window.dtype)] * 2,
        compiler_params=LIMIT,
        name="relax",
    )(level, *stack)
    centre, solids = lax.optimization_barrier((centre, solids))
    solid_sampled = pl.pallas_call(
        functools.partial(solid_kernel, quads, grain_chunk),
        out_shape=cells(1, grains),
        in_specs=[SMEM] + [VMEM] * 3,
        out_specs=VMEM,
        compiler_params=LIMIT,
        cost_estimate=pl.CostEstimate(
            flops=8 * own * CH * across * grains, bytes_accessed=2**20, transcendentals=0
        ),
        name="solid",
    )(place, grain_cell, weight, solids)

    pressures = [centre] + [swapped(*swap, centre) for swap in swap_plan(1)]
    pressures, solid_sampled = lax.optimization_barrier((pressures, solid_sampled))
    mine = pl.pallas_call(
        functools.partial(finish_kernel, quads),
        out_shape=frame,
        in_specs=[SMEM] + [VMEM] * 5,
        out_specs=VMEM,
        scratch_shapes=[pltpu.VMEM((3 * CH, across, LANES), jnp.float32)] * 2,
        compiler_params=LIMIT,
        name="finish",
    )(level, offset, gain, *pressures)

    def sampled_from(held, index, *earlier):
        return pl.pallas_call(
            functools.partial(
                sampled_kernel, quads, grain_chunk, place_offsets(quads)[index], index
            ),
            out_shape=cells(3, grains),
            in_specs=[SMEM] + [VMEM] * (3 + len(earlier)),
            out_specs=VMEM,
            compiler_params=LIMIT,
            cost_estimate=pl.CostEstimate(
                flops=12 * own * CH * across * grains, bytes_accessed=2**20, transcendentals=0
            ),
            name="sampled",
        )(place, grain_cell, weight, held, *earlier)

    held = mine[None]
    partial = sampled_from(held, 0)
    for bit in early:
        known = held.shape[0]
        held = jnp.concatenate([held, over_quad(bit, held)], axis=0)
        held, partial = lax.optimization_barrier((held, partial))
        for index in range(known, held.shape[0]):
            partial = sampled_from(held, index, partial)
    got = over_quad(last, jnp.concatenate([held, solids], axis=1))
    pressure, drag = pl.pallas_call(
        functools.partial(drag_kernel, quads, grain_chunk),
        out_shape=[cells(CH, CA, CB), cells(3, grains)],
        in_specs=[SMEM] * 2 + [VMEM] * 8,
        out_specs=[VMEM] * 2,
        scratch_shapes=[pltpu.VMEM((quads, CH, tall, LANES), jnp.float32)],
        compiler_params=LIMIT,
        name="drag",
    )(
        place,
        grain_count,
        grain_cell,
        weight,
        volume,
        grain_velocity,
        solid_sampled,
        partial,
        held,
        got,
    )
    return pressure, drag


def solution(mesh):
    placed = (
        P(None, ("slab", "quad")),
        P(("slab", "quad")),
        P(("slab", "quad")),
        P(("slab", "quad")),
        P(None, ("slab", "quad")),
    )
    return jax.shard_map(
        body,
        mesh=mesh,
        in_specs=placed,
        out_specs=(P("slab", "quad", None), P(None, ("slab", "quad"))),
        check_vma=False,
    )
```

```python
import functools

import jax
import jax.numpy as jnp
from jax import lax
from jax.experimental import pallas as pl
from jax.experimental.pallas import tpu as pltpu
from jax.sharding import PartitionSpec as P

CH = 4
CA = 16
CB = 256
ITERS = 12
LANES = 128
SUBLANES = 8
DEPTH = 2
FIRST = CH * DEPTH + 1

damping = 0.05
source_gain = 4.0

VMEM = pl.BlockSpec(memory_space=pltpu.VMEM)
SMEM = pl.BlockSpec(memory_space=pltpu.SMEM)
HBM = pl.BlockSpec(memory_space=pltpu.HBM)
LIMIT = pltpu.CompilerParams(vmem_limit_bytes=48 * 1024 * 1024)


def reach(distance):
    needed = ITERS - 1 - CH * (max(distance, 1) - 1)
    return 1 << (needed - 1).bit_length()


def lanes_of(shape):
    return lax.broadcasted_iota(jnp.int32, shape, len(shape) - 1)


def turned(value, shift):
    shift %= LANES
    return pltpu.roll(value, shift, value.ndim - 1) if shift else value


def pack_own(window, own):
    pieces = LANES // own
    tall = window.shape[1] // pieces
    lane = lanes_of((window.shape[0], tall, LANES))
    result = window[:, :tall]
    for piece in range(1, pieces):
        part = turned(window[:, piece * tall : (piece + 1) * tall], piece * own)
        result = jnp.where(lane < piece * own, result, part)
    return result


def unpack_own(packed, own):
    pieces = LANES // own
    return jnp.concatenate([turned(packed, -piece * own) for piece in range(pieces)], axis=1)


def strip_plan(across, fields, halo):
    rows = across * 2 * halo // LANES
    return (1, rows) if rows >= SUBLANES else (fields, rows * fields)


def packed_rows(across, fields, halo, own):
    shared, rows = strip_plan(across, fields, halo)
    return fields * CH * across * own // LANES + (fields // shared) * CH * rows


def pack(windows, halo, own):
    across = windows[0].shape[1]
    shared, rows = strip_plan(across, len(windows), halo)
    pieces = [pack_own(window, own) for window in windows]
    lane = lanes_of(windows[0].shape)
    joined = [
        jnp.where(lane >= LANES - halo, window, turned(window, LANES - 2 * halo - own))
        for window in windows
    ]
    lane = lanes_of((CH, rows, LANES))
    for first in range(0, len(windows), shared):
        strip, at = None, 0
        for value in joined[first : first + shared]:
            for row in range(0, across, rows):
                part = turned(value[:, row : row + rows], at + 2 * halo)
                strip = part if strip is None else jnp.where(lane < at, strip, part)
                at += 2 * halo
        pieces.append(strip)
    return jnp.concatenate([piece.reshape(-1, LANES) for piece in pieces], axis=0)


def unpack(value, fields, across, halo, own):
    shared, rows = strip_plan(across, fields, halo)
    tall = across * own // LANES
    count = fields * CH * tall
    owned = value[:count].reshape(fields, CH, tall, LANES)
    strips = value[count:].reshape(fields // shared, CH, rows, LANES)
    lane = lanes_of((CH, rows, LANES))
    windows = []
    for field in range(fields):
        window = unpack_own(owned[field], own)
        strip = strips[field // shared]
        at = (field % shared) * across // rows * 2 * halo
        blocks = []
        for row in range(0, across, rows):
            right = turned(strip, own - at)
            left = turned(strip, -2 * halo - at)
            block = jnp.where(lane < own + halo, right, 0.0)
            block = jnp.where(lane >= LANES - halo, left, block)
            blocks.append(jnp.where(lane < own, window[:, row : row + rows], block))
            at += 2 * halo
        windows.append(jnp.concatenate(blocks, axis=1))
    return windows


def halves(value):
    high = value.astype(jnp.bfloat16)
    low = (value - high.astype(jnp.float32)).astype(jnp.bfloat16)
    return high, low


def short_iota(shape):
    return lax.broadcasted_iota(jnp.int32, shape, 0).astype(jnp.int16)


def row_of(cell_ref, span, across):
    return cell_ref[1:2, span] * across + cell_ref[0:1, span] * CA + cell_ref[2:3, span]


def one_hot(rows, index):
    one, zero = jnp.bfloat16(1), jnp.bfloat16(0)
    return jnp.where(rows == index.astype(jnp.int16), one, zero)


def mass_of(count_ref, volume_ref, first, span):
    volume = volume_ref[0:1, span]
    slot = lax.broadcasted_iota(jnp.int32, volume.shape, 1) + first
    return jnp.where(slot < count_ref[0], volume, 0.0)


def grain_kernel(quads, count_ref, *refs):
    sources, out_ref, targets, sems = refs[:4], refs[4], refs[5:9], refs[9]
    copies = [
        pltpu.make_async_copy(source, target, sems.at[index])
        for index, (source, target) in enumerate(zip(sources, targets))
    ]
    for copy in copies:
        copy.start()
    for copy in copies:
        copy.wait()
    cell_ref, weight_ref, volume_ref, velocity_ref = targets
    span = pl.ds(0, weight_ref.shape[1])
    mass = mass_of(count_ref, volume_ref, 0, span)
    flat = row_of(cell_ref, span, quads * CA) * CB + cell_ref[3:4, span]
    out_ref[0:1, :] = flat.astype(jnp.float32)
    out_ref[1:2, :] = weight_ref[...]
    out_ref[2:3, :] = mass
    out_ref[3:4, :] = mass * velocity_ref[0:1, span]


def deposit_into(total, quads, chunk, place_ref, grain_ref):
    own = CB // quads
    halo = reach(0)
    rows = CH * quads * CA
    size = own + 2 * halo
    row_iota = short_iota((rows, chunk))
    iota = lax.broadcasted_iota(jnp.int32, (size, chunk), 0)
    col_iota = jnp.where(iota < own + halo, iota, iota - size).astype(jnp.int16)
    for first in range(0, grain_ref.shape[1], chunk):
        span = pl.ds(first, chunk)
        flat = grain_ref[0:1, span]
        row = jnp.floor(flat * (1.0 / CB))
        col = (flat - row * CB).astype(jnp.int32) - place_ref[0] * own
        lower = grain_ref[1:2, span]
        upper = 1.0 - lower
        hot = one_hot(row_iota, row.astype(jnp.int32))
        at_lower = col_iota == col.astype(jnp.int16)
        at_upper = col_iota == (col + 1).astype(jnp.int16)
        parts = []
        for amount in (grain_ref[2:3, span], grain_ref[3:4, span]):
            for low, high in zip(halves(amount * lower), halves(amount * upper)):
                parts.append(jnp.where(at_lower, low, jnp.where(at_upper, high, jnp.bfloat16(0))))
        product = lax.dot_general(
            jnp.concatenate(parts, axis=0),
            hot,
            (((1,), (1,)), ((), ())),
            preferred_element_type=jnp.float32,
        )
        total = product if total is None else total + product
    return total


def deposit_kernel(quads, chunk, place_ref, grain_ref, *refs):
    *earlier, out_ref = refs
    total = earlier[0][...] if earlier else None
    out_ref[...] = deposit_into(total, quads, chunk, place_ref, grain_ref)


def coefficient_kernel(quads, chunk, place_ref, *refs):
    grain_ref, total_ref, *outs, solid_ref = refs
    across, own = quads * CA, CB // quads
    total = deposit_into(total_ref[...], quads, chunk, place_ref, grain_ref)
    halo = reach(0)
    size = own + 2 * halo
    windows = []
    for base in range(0, 4 * size, 2 * size):
        field = total[base : base + size] + total[base + size : base + 2 * size]
        gap = jnp.zeros((LANES - size, field.shape[1]), jnp.float32)
        field = jnp.concatenate([field[: own + halo], gap, field[own + halo :]], axis=0)
        windows.append(field.T.reshape(CH, across, LANES))
    solid, moment = windows
    solid_ref[...] = pack_own(solid, own).reshape(solid_ref.shape)
    lane = lanes_of(solid.shape)
    column = jnp.where(lane < (LANES + own) // 2, lane, lane - LANES) + place_ref[0] * own
    inside = (column >= 0) & (column < CB)
    voidage = 1.0 / (1.0 + solid)
    scale = 1.0 / (6.0 * voidage + damping)
    offset = jnp.where(inside, source_gain * moment * scale, 0.0)
    gain = jnp.where(inside, voidage * scale, 0.0)
    for distance, out in enumerate(outs):
        out[...] = pack((offset, gain), reach(distance + 1), own)


def sweep_over(sweeps, layers, across, old, new, spare, offset_ref, gain_ref):
    row = lax.broadcasted_iota(jnp.int32, (across, LANES), 0)
    for sweep in range(1, sweeps + 1):
        for layer in range(sweep, layers - sweep):
            centre = old[layer]
            total = old[layer - 1] + old[layer + 1]
            total = total + turned(centre, 1) + turned(centre, -1)
            total = total + jnp.where(row == 0, 0.0, pltpu.roll(centre, 1, 0))
            total = total + jnp.where(row == across - 1, 0.0, pltpu.roll(centre, across - 1, 0))
            new[layer] = offset_ref[layer] + gain_ref[layer] * total
        old, new, spare = new, spare, new
    return old


def slot_of(slab, distance, matching):
    upward = lax.rem(lax.div(slab, distance), 2) ^ matching
    return distance * (1 - 2 * upward)


def swap_plan(depth):
    return [(distance, matching) for distance in range(1, depth + 1) for matching in ((1, 0) if distance == 1 else (0, 1))]


def framed(last, first, own):
    inner = pack([last[first : first + CH]], SUBLANES, own)
    outer = [pack_own(last[layer : layer + 1], own)[0] for layer in (first - 1, first + CH)]
    return jnp.concatenate([inner] + outer, axis=0)


def relax_kernel(quads, slab_ref, own_ref, *refs):
    *parts, out_ref, offset_ref, gain_ref, even_ref, odd_ref = refs
    across, own = quads * CA, CB // quads
    layers = CH * (1 + len(parts))
    plan = [(DEPTH, own_ref, 1)] + [
        (DEPTH + slot_of(slab_ref[0], distance, matching), part, distance)
        for part, (distance, matching) in zip(parts, swap_plan(DEPTH))
    ]
    for slot, part, distance in plan:
        span = pl.ds(slot * CH, CH)
        offset, gain = unpack(part[...], 2, across, reach(distance), own)
        offset_ref[span] = offset
        gain_ref[span] = gain
    last = sweep_over(
        FIRST - 1, layers, across, offset_ref, even_ref, odd_ref, offset_ref, gain_ref
    )
    out_ref[...] = pack([last[DEPTH * CH : (DEPTH + 1) * CH]], SUBLANES, own)


def finish_kernel(quads, slab_ref, offset_ref, gain_ref, *refs):
    *parts, out_ref, even_ref, odd_ref = refs
    across, own = quads * CA, CB // quads
    slots = [1] + [1 + slot_of(slab_ref[0], *swap) for swap in swap_plan(1)]
    for slot, pressure in zip(slots, parts):
        (even_ref[pl.ds(slot * CH, CH)],) = unpack(pressure[...], 1, across, SUBLANES, own)
    near = pl.ds((DEPTH - 1) * CH, 3 * CH)
    last = sweep_over(
        ITERS - FIRST,
        3 * CH,
        across,
        even_ref,
        odd_ref,
        even_ref,
        offset_ref.at[near],
        gain_ref.at[near],
    )
    out_ref[...] = framed(last, CH, own)


def halving(quads):
    return [1 << bit for bit in reversed(range(quads.bit_length() - 1))]


def place_offsets(quads):
    offsets = [0]
    for bit in halving(quads):
        offsets += [offset ^ bit for offset in offsets]
    return offsets


def blend_of(col_iota, at, lower):
    return jnp.where(col_iota == at, lower, jnp.where(col_iota == at + 1, 1.0 - lower, 0.0))


def picked_by(pieces, hot):
    twice = jnp.concatenate([hot, hot], axis=0)
    return jnp.dot(pieces, twice, preferred_element_type=jnp.float32)


def blended(picked, blend, field):
    size = blend.shape[0]
    return jnp.sum(picked[field * size : (field + 1) * size] * blend, axis=0, keepdims=True)


def solid_table(value, across, own):
    window = unpack_own(value.reshape(CH, across * own // LANES, LANES), own)
    return jnp.concatenate(halves(window.reshape(CH * across, LANES).T[:own]), axis=1)


def velocity_table(value, across, own):
    tall = across * own // LANES
    count = packed_rows(across, 1, SUBLANES, own)
    (inner,) = unpack(value[:count], 1, across, SUBLANES, own)
    outer = unpack_own(value[count:].reshape(2, tall, LANES), own)
    row = lax.broadcasted_iota(jnp.int32, inner.shape, 1)
    above = jnp.concatenate([inner[1:], outer[1:]], axis=0)
    below = jnp.concatenate([outer[:1], inner[:-1]], axis=0)
    after = jnp.where(row == across - 1, 0.0, pltpu.roll(inner, across - 1, 1))
    before = jnp.where(row == 0, 0.0, pltpu.roll(inner, 1, 1))
    fields = (
        -0.5 * (above - below),
        -0.5 * (after - before),
        -0.5 * (turned(inner, -1) - turned(inner, 1)),
    )
    columns = [field.reshape(CH * across, LANES).T[:own] for field in fields]
    return jnp.concatenate(halves(jnp.concatenate(columns, axis=0)), axis=1)


def chunk_sums(quads, place_ref, table, offsets, fields, cell_ref, weight_ref, row_iota, span):
    across, own = quads * CA, CB // quads
    hot = one_hot(row_iota, row_of(cell_ref, span, across))
    lower = weight_ref[0:1, span]
    picked = picked_by(table, hot)
    col_iota = lax.broadcasted_iota(jnp.int32, (own, picked.shape[1]), 0)
    sums = [0.0] * fields
    for index, offset in enumerate(offsets):
        at = cell_ref[3:4, span] - (place_ref[0] ^ offset) * own
        blend = blend_of(col_iota, at, lower)
        for field in range(fields):
            sums[field] += blended(picked, blend, fields * index + field)
    return sums


def store_sums(chunk, table, offsets, fields, quads, place_ref, cell_ref, weight_ref, earlier, out_ref):
    row_iota = short_iota((CH * quads * CA, chunk))
    for first in range(0, weight_ref.shape[1], chunk):
        span = pl.ds(first, chunk)
        sums = chunk_sums(
            quads, place_ref, table, offsets, fields, cell_ref, weight_ref, row_iota, span
        )
        for field, value in enumerate(sums):
            one = pl.ds(field, 1)
            for partial in earlier:
                value = value + partial[one, span]
            out_ref[one, span] = value


def solid_kernel(quads, chunk, place_ref, cell_ref, weight_ref, held_ref, out_ref):
    across, own = quads * CA, CB // quads
    half = quads // 2
    tables = [solid_table(held_ref[index], across, own) for index in range(half)]
    store_sums(
        chunk,
        jnp.concatenate(tables, axis=0),
        place_offsets(quads)[:half],
        1,
        quads,
        place_ref,
        cell_ref,
        weight_ref,
        [],
        out_ref,
    )


def sampled_kernel(quads, chunk, offset, index, place_ref, cell_ref, weight_ref, held_ref, *refs):
    *earlier, out_ref = refs
    table = velocity_table(held_ref[index], quads * CA, CB // quads)
    store_sums(
        chunk, table, [offset], 3, quads, place_ref, cell_ref, weight_ref, earlier, out_ref
    )


def drag_kernel(quads, chunk, place_ref, count_ref, cell_ref, weight_ref, volume_ref, *refs):
    velocity_ref, solid_ref, sampled_ref, held_ref, got_ref = refs[:5]
    pressure_ref, drag_ref, gathered = refs[5:]
    across, own = quads * CA, CB // quads
    half = quads // 2
    frame = held_ref.shape[1]
    tables = []
    for index in range(half):
        got = got_ref[index]
        tables += [velocity_table(got[:frame], across, own), solid_table(got[frame:], across, own)]
    table = jnp.concatenate(tables, axis=0)
    row_iota = short_iota((CH * across, chunk))
    for first in range(0, weight_ref.shape[1], chunk):
        span = pl.ds(first, chunk)
        *sums, solid = chunk_sums(
            quads,
            place_ref,
            table,
            place_offsets(quads)[half:],
            4,
            cell_ref,
            weight_ref,
            row_iota,
            span,
        )
        factor = mass_of(count_ref, volume_ref, first, span)
        factor = factor * (1.0 + (solid + solid_ref[0:1, span])) ** 2
        for component, value in enumerate(sums):
            one = pl.ds(component, 1)
            drag_ref[one, span] = factor * (
                value + sampled_ref[one, span] - velocity_ref[one, span]
            )
    shape = gathered.shape[1:]
    count = CH * shape[1]
    parts = [
        ref[index][:count].reshape(shape) for ref in (held_ref, got_ref) for index in range(half)
    ]
    for offset, part in zip(place_offsets(quads), parts):
        gathered[place_ref[0] ^ offset] = part
    bands = shape[1] // CA
    band = pl.ds(pl.multiple_of(lax.rem(place_ref[0], bands) * CA, SUBLANES), CA)
    back = lax.rem(LANES - lax.div(place_ref[0], bands) * own, LANES)
    lane = lanes_of((CH, CA, LANES))
    pieces = LANES // own
    for first in range(0, quads, pieces):
        block = None
        for near in range(pieces):
            part = pltpu.roll(gathered[first + near, :, band, :], lax.rem(back + near * own, LANES), 2)
            block = part if block is None else jnp.where(lane < near * own, block, part)
        pressure_ref[:, :, first * own : first * own + LANES] = block


def body(grain_cell, grain_count, grain_weight, grain_volume, grain_velocity):
    quads = lax.axis_size("quad")
    slabs = lax.axis_size("slab")
    grains = grain_weight.shape[0]
    across = quads * CA
    own = CB // quads
    tall = across * own // LANES
    place = lax.axis_index("quad").astype(jnp.int32).reshape(1)
    level = lax.axis_index("slab").astype(jnp.int32).reshape(1)
    weight = grain_weight.reshape(1, grains)
    volume = grain_volume.reshape(1, grains)

    grain_chunk = min(grains, 512)

    def cells(*shape):
        return jax.ShapeDtypeStruct(shape, jnp.float32)

    def over_quad(step, value):
        pairs = [(index, index ^ step) for index in range(quads)]
        return lax.ppermute(value, "quad", pairs)

    def swapped(distance, matching, value):
        lower = [
            index
            for index in range(slabs - distance)
            if (index // distance) % 2 == matching
        ]
        pairs = [(index, index + distance) for index in lower]
        return lax.ppermute(value, "slab", pairs + [(high, low) for low, high in pairs])

    *early, last = halving(quads)

    def nearly_all(value):
        held = value[None]
        for bit in early:
            held = jnp.concatenate([held, over_quad(bit, held)], axis=0)
        return held

    def pinned(value):
        return pltpu.with_memory_space_constraint(value, pltpu.HBM)

    packed_grains = pl.pallas_call(
        functools.partial(grain_kernel, quads),
        out_shape=cells(4, grains),
        in_specs=[SMEM] + [HBM] * 4,
        out_specs=VMEM,
        scratch_shapes=[
            pltpu.VMEM((4, grains), jnp.int32),
            pltpu.VMEM((1, grains), jnp.float32),
            pltpu.VMEM((1, grains), jnp.float32),
            pltpu.VMEM((3, grains), jnp.float32),
            pltpu.SemaphoreType.DMA((4,)),
        ],
        compiler_params=LIMIT,
        name="grains",
    )(
        grain_count,
        pinned(grain_cell),
        pinned(weight),
        pinned(volume),
        pinned(grain_velocity),
    )
    packs = [packed_grains]
    for bit in early:
        packs += [over_quad(bit, pack) for pack in packs]
    size = own + 2 * reach(0)
    deposit_chunk = min(grains, 2048)
    total = None

    def deposited(total, arrived):
        earlier = [] if total is None else [total]
        return pl.pallas_call(
            functools.partial(deposit_kernel, quads, deposit_chunk),
            out_shape=cells(4 * size, CH * across),
            in_specs=[SMEM] + [VMEM] * (1 + len(earlier)),
            out_specs=VMEM,
            compiler_params=LIMIT,
            cost_estimate=pl.CostEstimate(
                flops=8 * size * CH * across * grains, bytes_accessed=2**20, transcendentals=0
            ),
            name="deposit",
        )(place, arrived, *earlier)

    for index, pack in enumerate(packs):
        if index:
            pack, total = lax.optimization_barrier((pack, total))
        arriving = over_quad(last, pack)
        total = deposited(total, pack)
        if index < len(packs) - 1:
            total = deposited(total, arriving)
    *coefs, solid = pl.pallas_call(
        functools.partial(coefficient_kernel, quads, deposit_chunk),
        out_shape=[
            cells(packed_rows(across, 2, reach(distance), own), LANES)
            for distance in range(1, DEPTH + 1)
        ]
        + [cells(CH * tall, LANES)],
        in_specs=[SMEM] + [VMEM] * 2,
        out_specs=[VMEM] * (DEPTH + 1),
        compiler_params=LIMIT,
        name="coefficients",
    )(place, arriving, total)

    stack = [coefs[0]] + [
        swapped(distance, matching, coefs[distance - 1])
        for distance, matching in swap_plan(DEPTH)
    ]
    stack[1], solid = lax.optimization_barrier((stack[1], solid))
    solids = nearly_all(solid)
    frame = cells(packed_rows(across, 1, SUBLANES, own) + 2 * tall, LANES)
    layers = CH * len(stack)
    window = cells(layers, across, LANES)
    centre, offset, gain = pl.pallas_call(
        functools.partial(relax_kernel, quads),
        out_shape=[
            cells(packed_rows(across, 1, SUBLANES, own), LANES),
            window,
            window,
        ],
        in_specs=[SMEM] + [VMEM] * len(stack),
        out_specs=[VMEM] * 3,
        scratch_shapes=[pltpu.VMEM(window.shape, window.dtype)] * 2,
        compiler_params=LIMIT,
        name="relax",
    )(level, *stack)
    centre, solids = lax.optimization_barrier((centre, solids))
    solid_sampled = pl.pallas_call(
        functools.partial(solid_kernel, quads, grain_chunk),
        out_shape=cells(1, grains),
        in_specs=[SMEM] + [VMEM] * 3,
        out_specs=VMEM,
        compiler_params=LIMIT,
        cost_estimate=pl.CostEstimate(
            flops=8 * own * CH * across * grains, bytes_accessed=2**20, transcendentals=0
        ),
        name="solid",
    )(place, grain_cell, weight, solids)

    pressures = [centre] + [swapped(*swap, centre) for swap in swap_plan(1)]
    pressures, solid_sampled = lax.optimization_barrier((pressures, solid_sampled))
    mine = pl.pallas_call(
        functools.partial(finish_kernel, quads),
        out_shape=frame,
        in_specs=[SMEM] + [VMEM] * 5,
        out_specs=VMEM,
        scratch_shapes=[pltpu.VMEM((3 * CH, across, LANES), jnp.float32)] * 2,
        compiler_params=LIMIT,
        name="finish",
    )(level, offset, gain, *pressures)

    def sampled_from(held, index, *earlier):
        return pl.pallas_call(
            functools.partial(
                sampled_kernel, quads, grain_chunk, place_offsets(quads)[index], index
            ),
            out_shape=cells(3, grains),
            in_specs=[SMEM] + [VMEM] * (3 + len(earlier)),
            out_specs=VMEM,
            compiler_params=LIMIT,
            cost_estimate=pl.CostEstimate(
                flops=12 * own * CH * across * grains, bytes_accessed=2**20, transcendentals=0
            ),
            name="sampled",
        )(place, grain_cell, weight, held, *earlier)

    held = mine[None]
    partial = sampled_from(held, 0)
    for bit in early:
        known = held.shape[0]
        held = jnp.concatenate([held, over_quad(bit, held)], axis=0)
        held, partial = lax.optimization_barrier((held, partial))
        for index in range(known, held.shape[0]):
            partial = sampled_from(held, index, partial)
    got = over_quad(last, jnp.concatenate([held, solids], axis=1))
    pressure, drag = pl.pallas_call(
        functools.partial(drag_kernel, quads, grain_chunk),
        out_shape=[cells(CH, CA, CB), cells(3, grains)],
        in_specs=[SMEM] * 2 + [VMEM] * 8,
        out_specs=[VMEM] * 2,
        scratch_shapes=[pltpu.VMEM((quads, CH, tall, LANES), jnp.float32)],
        compiler_params=LIMIT,
        name="drag",
    )(
        place,
        grain_count,
        grain_cell,
        weight,
        volume,
        grain_velocity,
        solid_sampled,
        partial,
        held,
        got,
    )
    return pressure, drag


def solution(mesh):
    placed = (
        P(None, ("slab", "quad")),
        P(("slab", "quad")),
        P(("slab", "quad")),
        P(("slab", "quad")),
        P(None, ("slab", "quad")),
    )
    return jax.shard_map(
        body,
        mesh=mesh,
        in_specs=placed,
        out_specs=(P("slab", "quad", None), P(None, ("slab", "quad"))),
        check_vma=False,
    )
```

```python
import functools

import jax
import jax.numpy as jnp
from jax import lax
from jax.experimental import pallas as pl
from jax.experimental.pallas import tpu as pltpu
from jax.sharding import PartitionSpec as P

CH = 4
CA = 16
CB = 256
ITERS = 12
LANES = 128
SUBLANES = 8
DEPTH = 2
FIRST = CH * DEPTH + 1

damping = 0.05
source_gain = 4.0

VMEM = pl.BlockSpec(memory_space=pltpu.VMEM)
SMEM = pl.BlockSpec(memory_space=pltpu.SMEM)
HBM = pl.BlockSpec(memory_space=pltpu.HBM)
LIMIT = pltpu.CompilerParams(vmem_limit_bytes=48 * 1024 * 1024)


def reach(distance):
    needed = ITERS - 1 - CH * (max(distance, 1) - 1)
    return 1 << (needed - 1).bit_length()


def lanes_of(shape):
    return lax.broadcasted_iota(jnp.int32, shape, len(shape) - 1)


def turned(value, shift):
    shift %= LANES
    return pltpu.roll(value, shift, value.ndim - 1) if shift else value


def pack_own(window, own):
    pieces = LANES // own
    tall = window.shape[1] // pieces
    lane = lanes_of((window.shape[0], tall, LANES))
    result = window[:, :tall]
    for piece in range(1, pieces):
        part = turned(window[:, piece * tall : (piece + 1) * tall], piece * own)
        result = jnp.where(lane < piece * own, result, part)
    return result


def unpack_own(packed, own):
    pieces = LANES // own
    return jnp.concatenate([turned(packed, -piece * own) for piece in range(pieces)], axis=1)


def strip_plan(across, fields, halo):
    rows = across * 2 * halo // LANES
    return (1, rows) if rows >= SUBLANES else (fields, rows * fields)


def packed_rows(across, fields, halo, own):
    shared, rows = strip_plan(across, fields, halo)
    return fields * CH * across * own // LANES + (fields // shared) * CH * rows


def pack(windows, halo, own):
    across = windows[0].shape[1]
    shared, rows = strip_plan(across, len(windows), halo)
    pieces = [pack_own(window, own) for window in windows]
    lane = lanes_of(windows[0].shape)
    joined = [
        jnp.where(lane >= LANES - halo, window, turned(window, LANES - 2 * halo - own))
        for window in windows
    ]
    lane = lanes_of((CH, rows, LANES))
    for first in range(0, len(windows), shared):
        strip, at = None, 0
        for value in joined[first : first + shared]:
            for row in range(0, across, rows):
                part = turned(value[:, row : row + rows], at + 2 * halo)
                strip = part if strip is None else jnp.where(lane < at, strip, part)
                at += 2 * halo
        pieces.append(strip)
    return jnp.concatenate([piece.reshape(-1, LANES) for piece in pieces], axis=0)


def unpack(value, fields, across, halo, own):
    shared, rows = strip_plan(across, fields, halo)
    tall = across * own // LANES
    count = fields * CH * tall
    owned = value[:count].reshape(fields, CH, tall, LANES)
    strips = value[count:].reshape(fields // shared, CH, rows, LANES)
    lane = lanes_of((CH, rows, LANES))
    windows = []
    for field in range(fields):
        window = unpack_own(owned[field], own)
        strip = strips[field // shared]
        at = (field % shared) * across // rows * 2 * halo
        blocks = []
        for row in range(0, across, rows):
            right = turned(strip, own - at)
            left = turned(strip, -2 * halo - at)
            block = jnp.where(lane < own + halo, right, 0.0)
            block = jnp.where(lane >= LANES - halo, left, block)
            blocks.append(jnp.where(lane < own, window[:, row : row + rows], block))
            at += 2 * halo
        windows.append(jnp.concatenate(blocks, axis=1))
    return windows


def halves(value):
    high = value.astype(jnp.bfloat16)
    low = (value - high.astype(jnp.float32)).astype(jnp.bfloat16)
    return high, low


def short_iota(shape):
    return lax.broadcasted_iota(jnp.int32, shape, 0).astype(jnp.int16)


def row_of(cell_ref, span, across):
    return cell_ref[1:2, span] * across + cell_ref[0:1, span] * CA + cell_ref[2:3, span]


def one_hot(rows, index):
    one, zero = jnp.bfloat16(1), jnp.bfloat16(0)
    return jnp.where(rows == index.astype(jnp.int16), one, zero)


def mass_of(count_ref, volume_ref, first, span):
    volume = volume_ref[0:1, span]
    slot = lax.broadcasted_iota(jnp.int32, volume.shape, 1) + first
    return jnp.where(slot < count_ref[0], volume, 0.0)


def grain_kernel(quads, count_ref, *refs):
    sources, out_ref, targets, sems = refs[:4], refs[4], refs[5:9], refs[9]
    copies = [
        pltpu.make_async_copy(source, target, sems.at[index])
        for index, (source, target) in enumerate(zip(sources, targets))
    ]
    for copy in copies:
        copy.start()
    for copy in copies:
        copy.wait()
    cell_ref, weight_ref, volume_ref, velocity_ref = targets
    span = pl.ds(0, weight_ref.shape[1])
    mass = mass_of(count_ref, volume_ref, 0, span)
    flat = row_of(cell_ref, span, quads * CA) * CB + cell_ref[3:4, span]
    out_ref[0:1, :] = flat.astype(jnp.float32)
    out_ref[1:2, :] = weight_ref[...]
    out_ref[2:3, :] = mass
    out_ref[3:4, :] = mass * velocity_ref[0:1, span]


def deposit_into(total, quads, chunk, place_ref, grain_ref):
    own = CB // quads
    halo = reach(0)
    rows = CH * quads * CA
    size = own + 2 * halo
    row_iota = short_iota((rows, chunk))
    iota = lax.broadcasted_iota(jnp.int32, (size, chunk), 0)
    col_iota = jnp.where(iota < own + halo, iota, iota - size).astype(jnp.int16)
    for first in range(0, grain_ref.shape[1], chunk):
        span = pl.ds(first, chunk)
        flat = grain_ref[0:1, span]
        row = jnp.floor(flat * (1.0 / CB))
        col = (flat - row * CB).astype(jnp.int32) - place_ref[0] * own
        lower = grain_ref[1:2, span]
        upper = 1.0 - lower
        hot = one_hot(row_iota, row.astype(jnp.int32))
        at_lower = col_iota == col.astype(jnp.int16)
        at_upper = col_iota == (col + 1).astype(jnp.int16)
        parts = []
        for amount in (grain_ref[2:3, span], grain_ref[3:4, span]):
            for low, high in zip(halves(amount * lower), halves(amount * upper)):
                parts.append(jnp.where(at_lower, low, jnp.where(at_upper, high, jnp.bfloat16(0))))
        product = lax.dot_general(
            jnp.concatenate(parts, axis=0),
            hot,
            (((1,), (1,)), ((), ())),
            preferred_element_type=jnp.float32,
        )
        total = product if total is None else total + product
    return total


def deposit_kernel(quads, chunk, place_ref, grain_ref, *refs):
    *earlier, out_ref = refs
    total = earlier[0][...] if earlier else None
    out_ref[...] = deposit_into(total, quads, chunk, place_ref, grain_ref)


def coefficient_kernel(quads, chunk, place_ref, *refs):
    grain_ref, total_ref, *outs, solid_ref = refs
    across, own = quads * CA, CB // quads
    total = deposit_into(total_ref[...], quads, chunk, place_ref, grain_ref)
    halo = reach(0)
    size = own + 2 * halo
    windows = []
    for base in range(0, 4 * size, 2 * size):
        field = total[base : base + size] + total[base + size : base + 2 * size]
        gap = jnp.zeros((LANES - size, field.shape[1]), jnp.float32)
        field = jnp.concatenate([field[: own + halo], gap, field[own + halo :]], axis=0)
        windows.append(field.T.reshape(CH, across, LANES))
    solid, moment = windows
    solid_ref[...] = pack_own(solid, own).reshape(solid_ref.shape)
    lane = lanes_of(solid.shape)
    column = jnp.where(lane < (LANES + own) // 2, lane, lane - LANES) + place_ref[0] * own
    inside = (column >= 0) & (column < CB)
    voidage = 1.0 / (1.0 + solid)
    scale = 1.0 / (6.0 * voidage + damping)
    offset = jnp.where(inside, source_gain * moment * scale, 0.0)
    gain = jnp.where(inside, voidage * scale, 0.0)
    for distance, out in enumerate(outs):
        out[...] = pack((offset, gain), reach(distance + 1), own)


def sweep_over(sweeps, layers, across, old, new, spare, offset_ref, gain_ref):
    row = lax.broadcasted_iota(jnp.int32, (across, LANES), 0)
    for sweep in range(1, sweeps + 1):
        for layer in range(sweep, layers - sweep):
            centre = old[layer]
            total = old[layer - 1] + old[layer + 1]
            total = total + turned(centre, 1) + turned(centre, -1)
            total = total + jnp.where(row == 0, 0.0, pltpu.roll(centre, 1, 0))
            total = total + jnp.where(row == across - 1, 0.0, pltpu.roll(centre, across - 1, 0))
            new[layer] = offset_ref[layer] + gain_ref[layer] * total
        old, new, spare = new, spare, new
    return old


def slot_of(slab, distance, matching):
    upward = lax.rem(lax.div(slab, distance), 2) ^ matching
    return distance * (1 - 2 * upward)


def swap_plan(depth):
    return [(distance, matching) for distance in range(1, depth + 1) for matching in ((1, 0) if distance == 1 else (0, 1))]


def framed(last, first, own):
    inner = pack([last[first : first + CH]], SUBLANES, own)
    outer = [pack_own(last[layer : layer + 1], own)[0] for layer in (first - 1, first + CH)]
    return jnp.concatenate([inner] + outer, axis=0)


def relax_kernel(quads, slab_ref, own_ref, *refs):
    *parts, out_ref, offset_ref, gain_ref, even_ref, odd_ref = refs
    across, own = quads * CA, CB // quads
    layers = CH * (1 + len(parts))
    plan = [(DEPTH, own_ref, 1)] + [
        (DEPTH + slot_of(slab_ref[0], distance, matching), part, distance)
        for part, (distance, matching) in zip(parts, swap_plan(DEPTH))
    ]
    for slot, part, distance in plan:
        span = pl.ds(slot * CH, CH)
        offset, gain = unpack(part[...], 2, across, reach(distance), own)
        offset_ref[span] = offset
        gain_ref[span] = gain
    last = sweep_over(
        FIRST - 1, layers, across, offset_ref, even_ref, odd_ref, offset_ref, gain_ref
    )
    out_ref[...] = pack([last[DEPTH * CH : (DEPTH + 1) * CH]], SUBLANES, own)


def finish_kernel(quads, slab_ref, offset_ref, gain_ref, *refs):
    *parts, out_ref, even_ref, odd_ref = refs
    across, own = quads * CA, CB // quads
    slots = [1] + [1 + slot_of(slab_ref[0], *swap) for swap in swap_plan(1)]
    for slot, pressure in zip(slots, parts):
        (even_ref[pl.ds(slot * CH, CH)],) = unpack(pressure[...], 1, across, SUBLANES, own)
    near = pl.ds((DEPTH - 1) * CH, 3 * CH)
    last = sweep_over(
        ITERS - FIRST,
        3 * CH,
        across,
        even_ref,
        odd_ref,
        even_ref,
        offset_ref.at[near],
        gain_ref.at[near],
    )
    out_ref[...] = framed(last, CH, own)


def halving(quads):
    return [1 << bit for bit in reversed(range(quads.bit_length() - 1))]


def place_offsets(quads):
    offsets = [0]
    for bit in halving(quads):
        offsets += [offset ^ bit for offset in offsets]
    return offsets


def blend_of(col_iota, at, lower):
    return jnp.where(col_iota == at, lower, jnp.where(col_iota == at + 1, 1.0 - lower, 0.0))


def picked_by(pieces, hot):
    twice = jnp.concatenate([hot, hot], axis=0)
    return jnp.dot(pieces, twice, preferred_element_type=jnp.float32)


def blended(picked, blend, field):
    size = blend.shape[0]
    return jnp.sum(picked[field * size : (field + 1) * size] * blend, axis=0, keepdims=True)


def solid_table(value, across, own):
    window = unpack_own(value.reshape(CH, across * own // LANES, LANES), own)
    return jnp.concatenate(halves(window.reshape(CH * across, LANES).T[:own]), axis=1)


def velocity_table(value, across, own):
    tall = across * own // LANES
    count = packed_rows(across, 1, SUBLANES, own)
    (inner,) = unpack(value[:count], 1, across, SUBLANES, own)
    outer = unpack_own(value[count:].reshape(2, tall, LANES), own)
    row = lax.broadcasted_iota(jnp.int32, inner.shape, 1)
    above = jnp.concatenate([inner[1:], outer[1:]], axis=0)
    below = jnp.concatenate([outer[:1], inner[:-1]], axis=0)
    after = jnp.where(row == across - 1, 0.0, pltpu.roll(inner, across - 1, 1))
    before = jnp.where(row == 0, 0.0, pltpu.roll(inner, 1, 1))
    fields = (
        -0.5 * (above - below),
        -0.5 * (after - before),
        -0.5 * (turned(inner, -1) - turned(inner, 1)),
    )
    columns = [field.reshape(CH * across, LANES).T[:own] for field in fields]
    return jnp.concatenate(halves(jnp.concatenate(columns, axis=0)), axis=1)


def chunk_sums(quads, place_ref, table, offsets, fields, cell_ref, weight_ref, row_iota, span):
    across, own = quads * CA, CB // quads
    hot = one_hot(row_iota, row_of(cell_ref, span, across))
    lower = weight_ref[0:1, span]
    picked = picked_by(table, hot)
    col_iota = lax.broadcasted_iota(jnp.int32, (own, picked.shape[1]), 0)
    sums = [0.0] * fields
    for index, offset in enumerate(offsets):
        at = cell_ref[3:4, span] - (place_ref[0] ^ offset) * own
        blend = blend_of(col_iota, at, lower)
        for field in range(fields):
            sums[field] += blended(picked, blend, fields * index + field)
    return sums


def store_sums(chunk, table, offsets, fields, quads, place_ref, cell_ref, weight_ref, earlier, out_ref):
    row_iota = short_iota((CH * quads * CA, chunk))
    for first in range(0, weight_ref.shape[1], chunk):
        span = pl.ds(first, chunk)
        sums = chunk_sums(
            quads, place_ref, table, offsets, fields, cell_ref, weight_ref, row_iota, span
        )
        for field, value in enumerate(sums):
            one = pl.ds(field, 1)
            for partial in earlier:
                value = value + partial[one, span]
            out_ref[one, span] = value


def solid_kernel(quads, chunk, place_ref, cell_ref, weight_ref, held_ref, out_ref):
    across, own = quads * CA, CB // quads
    half = quads // 2
    tables = [solid_table(held_ref[index], across, own) for index in range(half)]
    store_sums(
        chunk,
        jnp.concatenate(tables, axis=0),
        place_offsets(quads)[:half],
        1,
        quads,
        place_ref,
        cell_ref,
        weight_ref,
        [],
        out_ref,
    )


def sampled_kernel(quads, chunk, offset, index, place_ref, cell_ref, weight_ref, held_ref, *refs):
    *earlier, out_ref = refs
    table = velocity_table(held_ref[index], quads * CA, CB // quads)
    store_sums(
        chunk, table, [offset], 3, quads, place_ref, cell_ref, weight_ref, earlier, out_ref
    )


def drag_kernel(quads, chunk, place_ref, count_ref, cell_ref, weight_ref, volume_ref, *refs):
    velocity_ref, solid_ref, sampled_ref, held_ref, got_ref = refs[:5]
    pressure_ref, drag_ref, gathered = refs[5:]
    across, own = quads * CA, CB // quads
    half = quads // 2
    frame = held_ref.shape[1]
    tables = []
    for index in range(half):
        got = got_ref[index]
        tables += [velocity_table(got[:frame], across, own), solid_table(got[frame:], across, own)]
    table = jnp.concatenate(tables, axis=0)
    row_iota = short_iota((CH * across, chunk))
    for first in range(0, weight_ref.shape[1], chunk):
        span = pl.ds(first, chunk)
        *sums, solid = chunk_sums(
            quads,
            place_ref,
            table,
            place_offsets(quads)[half:],
            4,
            cell_ref,
            weight_ref,
            row_iota,
            span,
        )
        factor = mass_of(count_ref, volume_ref, first, span)
        factor = factor * (1.0 + (solid + solid_ref[0:1, span])) ** 2
        for component, value in enumerate(sums):
            one = pl.ds(component, 1)
            drag_ref[one, span] = factor * (
                value + sampled_ref[one, span] - velocity_ref[one, span]
            )
    shape = gathered.shape[1:]
    count = CH * shape[1]
    parts = [
        ref[index][:count].reshape(shape) for ref in (held_ref, got_ref) for index in range(half)
    ]
    for offset, part in zip(place_offsets(quads), parts):
        gathered[place_ref[0] ^ offset] = part
    bands = shape[1] // CA
    band = pl.ds(pl.multiple_of(lax.rem(place_ref[0], bands) * CA, SUBLANES), CA)
    back = lax.rem(LANES - lax.div(place_ref[0], bands) * own, LANES)
    lane = lanes_of((CH, CA, LANES))
    pieces = LANES // own
    for first in range(0, quads, pieces):
        block = None
        for near in range(pieces):
            part = pltpu.roll(gathered[first + near, :, band, :], lax.rem(back + near * own, LANES), 2)
            block = part if block is None else jnp.where(lane < near * own, block, part)
        pressure_ref[:, :, first * own : first * own + LANES] = block


def body(grain_cell, grain_count, grain_weight, grain_volume, grain_velocity):
    quads = lax.axis_size("quad")
    slabs = lax.axis_size("slab")
    grains = grain_weight.shape[0]
    across = quads * CA
    own = CB // quads
    tall = across * own // LANES
    place = lax.axis_index("quad").astype(jnp.int32).reshape(1)
    level = lax.axis_index("slab").astype(jnp.int32).reshape(1)
    weight = grain_weight.reshape(1, grains)
    volume = grain_volume.reshape(1, grains)

    grain_chunk = min(grains, 1024)

    def cells(*shape):
        return jax.ShapeDtypeStruct(shape, jnp.float32)

    def over_quad(step, value):
        pairs = [(index, index ^ step) for index in range(quads)]
        return lax.ppermute(value, "quad", pairs)

    def swapped(distance, matching, value):
        lower = [
            index
            for index in range(slabs - distance)
            if (index // distance) % 2 == matching
        ]
        pairs = [(index, index + distance) for index in lower]
        return lax.ppermute(value, "slab", pairs + [(high, low) for low, high in pairs])

    *early, last = halving(quads)

    def nearly_all(value):
        held = value[None]
        for bit in early:
            held = jnp.concatenate([held, over_quad(bit, held)], axis=0)
        return held

    def pinned(value):
        return pltpu.with_memory_space_constraint(value, pltpu.HBM)

    packed_grains = pl.pallas_call(
        functools.partial(grain_kernel, quads),
        out_shape=cells(4, grains),
        in_specs=[SMEM] + [HBM] * 4,
        out_specs=VMEM,
        scratch_shapes=[
            pltpu.VMEM((4, grains), jnp.int32),
            pltpu.VMEM((1, grains), jnp.float32),
            pltpu.VMEM((1, grains), jnp.float32),
            pltpu.VMEM((3, grains), jnp.float32),
            pltpu.SemaphoreType.DMA((4,)),
        ],
        compiler_params=LIMIT,
        name="grains",
    )(
        grain_count,
        pinned(grain_cell),
        pinned(weight),
        pinned(volume),
        pinned(grain_velocity),
    )
    packs = [packed_grains]
    for bit in early:
        packs += [over_quad(bit, pack) for pack in packs]
    size = own + 2 * reach(0)
    deposit_chunk = min(grains, 2048)
    total = None

    def deposited(total, arrived):
        earlier = [] if total is None else [total]
        return pl.pallas_call(
            functools.partial(deposit_kernel, quads, deposit_chunk),
            out_shape=cells(4 * size, CH * across),
            in_specs=[SMEM] + [VMEM] * (1 + len(earlier)),
            out_specs=VMEM,
            compiler_params=LIMIT,
            cost_estimate=pl.CostEstimate(
                flops=8 * size * CH * across * grains, bytes_accessed=2**20, transcendentals=0
            ),
            name="deposit",
        )(place, arrived, *earlier)

    for index, pack in enumerate(packs):
        if index:
            pack, total = lax.optimization_barrier((pack, total))
        arriving = over_quad(last, pack)
        total = deposited(total, pack)
        if index < len(packs) - 1:
            total = deposited(total, arriving)
    *coefs, solid = pl.pallas_call(
        functools.partial(coefficient_kernel, quads, deposit_chunk),
        out_shape=[
            cells(packed_rows(across, 2, reach(distance), own), LANES)
            for distance in range(1, DEPTH + 1)
        ]
        + [cells(CH * tall, LANES)],
        in_specs=[SMEM] + [VMEM] * 2,
        out_specs=[VMEM] * (DEPTH + 1),
        compiler_params=LIMIT,
        name="coefficients",
    )(place, arriving, total)

    stack = [coefs[0]] + [
        swapped(distance, matching, coefs[distance - 1])
        for distance, matching in swap_plan(DEPTH)
    ]
    stack[1], solid = lax.optimization_barrier((stack[1], solid))
    solids = nearly_all(solid)
    frame = cells(packed_rows(across, 1, SUBLANES, own) + 2 * tall, LANES)
    layers = CH * len(stack)
    window = cells(layers, across, LANES)
    centre, offset, gain = pl.pallas_call(
        functools.partial(relax_kernel, quads),
        out_shape=[
            cells(packed_rows(across, 1, SUBLANES, own), LANES),
            window,
            window,
        ],
        in_specs=[SMEM] + [VMEM] * len(stack),
        out_specs=[VMEM] * 3,
        scratch_shapes=[pltpu.VMEM(window.shape, window.dtype)] * 2,
        compiler_params=LIMIT,
        name="relax",
    )(level, *stack)
    centre, solids = lax.optimization_barrier((centre, solids))
    solid_sampled = pl.pallas_call(
        functools.partial(solid_kernel, quads, grain_chunk),
        out_shape=cells(1, grains),
        in_specs=[SMEM] + [VMEM] * 3,
        out_specs=VMEM,
        compiler_params=LIMIT,
        cost_estimate=pl.CostEstimate(
            flops=8 * own * CH * across * grains, bytes_accessed=2**20, transcendentals=0
        ),
        name="solid",
    )(place, grain_cell, weight, solids)

    pressures = [centre] + [swapped(*swap, centre) for swap in swap_plan(1)]
    pressures, solid_sampled = lax.optimization_barrier((pressures, solid_sampled))
    mine = pl.pallas_call(
        functools.partial(finish_kernel, quads),
        out_shape=frame,
        in_specs=[SMEM] + [VMEM] * 5,
        out_specs=VMEM,
        scratch_shapes=[pltpu.VMEM((3 * CH, across, LANES), jnp.float32)] * 2,
        compiler_params=LIMIT,
        name="finish",
    )(level, offset, gain, *pressures)

    def sampled_from(held, index, *earlier):
        return pl.pallas_call(
            functools.partial(
                sampled_kernel, quads, grain_chunk, place_offsets(quads)[index], index
            ),
            out_shape=cells(3, grains),
            in_specs=[SMEM] + [VMEM] * (3 + len(earlier)),
            out_specs=VMEM,
            compiler_params=LIMIT,
            cost_estimate=pl.CostEstimate(
                flops=12 * own * CH * across * grains, bytes_accessed=2**20, transcendentals=0
            ),
            name="sampled",
        )(place, grain_cell, weight, held, *earlier)

    held = mine[None]
    partial = sampled_from(held, 0)
    for bit in early:
        known = held.shape[0]
        held = jnp.concatenate([held, over_quad(bit, held)], axis=0)
        held, partial = lax.optimization_barrier((held, partial))
        for index in range(known, held.shape[0]):
            partial = sampled_from(held, index, partial)
    got = over_quad(last, jnp.concatenate([held, solids], axis=1))
    pressure, drag = pl.pallas_call(
        functools.partial(drag_kernel, quads, grain_chunk),
        out_shape=[cells(CH, CA, CB), cells(3, grains)],
        in_specs=[SMEM] * 2 + [VMEM] * 8,
        out_specs=[VMEM] * 2,
        scratch_shapes=[pltpu.VMEM((quads, CH, tall, LANES), jnp.float32)],
        compiler_params=LIMIT,
        name="drag",
    )(
        place,
        grain_count,
        grain_cell,
        weight,
        volume,
        grain_velocity,
        solid_sampled,
        partial,
        held,
        got,
    )
    return pressure, drag


def solution(mesh):
    placed = (
        P(None, ("slab", "quad")),
        P(("slab", "quad")),
        P(("slab", "quad")),
        P(("slab", "quad")),
        P(None, ("slab", "quad")),
    )
    return jax.shard_map(
        body,
        mesh=mesh,
        in_specs=placed,
        out_specs=(P("slab", "quad", None), P(None, ("slab", "quad"))),
        check_vma=False,
    )
```
